128 devices in a mesh: seq: 4 (over x), ctx: 32 (over z, y, core).
Axes of the slice: x: 4, y: 4, z: 4, core: 2. Of those that a mesh axis runs over, the one named last changes fastest.
Arguments:
- tokens: bfloat16 [16384, 1600], P(('seq', 'ctx')), may hold values from -6 to 6
- norm_gain: float32 [1600], replicated, may hold values from 0.5 to 1.5
- qkv_weight: bfloat16 [1600, 2240], P('ctx'), may hold values from -0.15625 to 0.15625
- attn_out_weight: bfloat16 [1600, 1600], P('ctx'), may hold values from -0.15625 to 0.15625
- in_weight: bfloat16 [1600, 6400], P('ctx'), may hold values from -0.15625 to 0.15625
- conv_weight: float32 [4, 3200], replicated, may hold values from -3 to 3
- conv_bias: float32 [3200], replicated, may hold values from -3 to 3
- xproj_weight: bfloat16 [3200, 132], P('ctx'), may hold values from -0.109375 to 0.109375
- dt_weight: bfloat16 [3200, 100], P('ctx'), may hold values from -0.625 to 0.625
- dt_bias: float32 [3200], replicated, may hold values from -7 to -2
- decay_log: float32 [3200, 16], replicated, may hold values from -7 to 0
- skip_gain: float32 [3200], replicated, may hold values from 0.5 to 1.5
- mamba_out_weight: bfloat16 [3200, 1600], P('ctx'), may hold values from -0.109375 to 0.109375
- attn_gain: float32 [1600], replicated, may hold values from 0.5 to 1.5
- mamba_gain: float32 [1600], replicated, may hold values from 0.5 to 1.5
- ffn_gain: float32 [1600], replicated, may hold values from 0.5 to 1.5
- gate_up_weight: bfloat16 [1600, 11008], P('ctx'), may hold values from -0.15625 to 0.15625
- down_weight: bfloat16 [5504, 1600], P('ctx'), may hold values from -0.078125 to 0.078125
- cotangent: bfloat16 [16384, 1600], P(('seq', 'ctx')), may hold values from -6 to 6
Outputs:
- output: bfloat16 [16384, 1600], P(('seq', 'ctx'))
- tokens_grad: float32 [16384, 1600], P(('seq', 'ctx'))
- norm_gain_grad: float32 [1600], replicated
- qkv_weight_grad: float32 [1600, 2240], P('ctx')
- attn_out_weight_grad: float32 [1600, 1600], P('ctx')
- in_weight_grad: float32 [1600, 6400], P('ctx')
- conv_weight_grad: float32 [4, 3200], replicated
- conv_bias_grad: float32 [3200], replicated
- xproj_weight_grad: float32 [3200, 132], P('ctx')
- dt_weight_grad: float32 [3200, 100], P('ctx')
- dt_bias_grad: float32 [3200], replicated
- decay_log_grad: float32 [3200, 16], replicated
- skip_gain_grad: float32 [3200], replicated
- mamba_out_weight_grad: float32 [3200, 1600], P('ctx')
- attn_gain_grad: float32 [1600], replicated
- mamba_gain_grad: float32 [1600], replicated
- ffn_gain_grad: float32 [1600], replicated
- gate_up_weight_grad: float32 [1600, 11008], P('ctx')
- down_weight_grad: float32 [5504, 1600], P('ctx')
The draws below stay inside these ranges and needn't reach their ends.
All inputs are finite; a program needn't handle non-finite values.
Results may differ from the reference program's by a relative error of at most 0.024.
Values may be sent and summed in bfloat16 or wider, within the bound.
No kernel may reach another device: no remote copies, remote signals or barrier semaphores. Data moves between devices by JAX's collectives and lax.ppermute only.
A program may use at most 576 MiB of HBM per device.

```python
import jax
import jax.numpy as jnp
from jax import lax

D = 1600
HEADS = 25
KV_HEADS = 5
HEAD_DIM = 64
DI = 3200
N_STATE = 16
CONV = 4
DT_RANK = 100
FF = 5504
WINDOW = 1024
TOK_DEV = 128
SEQ_LEN = 4096
TOKENS = 16384
N_SEQ = 4


def block_levels(key, extent, shards, least, top_value):
    def one(dim, blocks):
        heights = jax.random.uniform(jax.random.fold_in(jax.random.fold_in(key, 6), dim), (blocks,), jnp.float32, least / len(shards), top_value / len(shards))
        return jnp.repeat(jnp.exp(heights), extent[dim] // blocks).reshape((-1,) + (1,) * (len(extent) - dim - 1))

    loudness = one(*shards[0])
    for cut in shards[1:]:
        loudness = loudness * one(*cut)
    return loudness


def normal_values(own_key, shape, deviation, bound, split=(), held_as=jnp.bfloat16):
    values = jax.random.normal(own_key, shape, jnp.float32) * deviation
    if len(split) > 0:
        values = block_levels(own_key, shape, split, -0.22, 0.18) * values
    return jnp.clip(values, min=-bound, max=bound).astype(held_as)


def setup_inputs(seed: int = 0) -> dict:
    arg_keys = jax.random.split(jax.random.key(seed), 20)
    return {
        "tokens": normal_values(arg_keys[0], (TOKENS, D), 1.0, 6.0, ((0, 128),)),
        "norm_gain": jnp.clip(1.0 + 0.1 * jax.random.normal(arg_keys[1], (D,), jnp.float32), 0.5, 1.5),
        "qkv_weight": normal_values(arg_keys[2], (D, (HEADS + 2 * KV_HEADS) * HEAD_DIM), D ** -0.5, 0.15625, ((0, 32),)),
        "attn_out_weight": normal_values(arg_keys[3], (HEADS * HEAD_DIM, D), (HEADS * HEAD_DIM) ** -0.5, 0.15625, ((0, 32),)),
        "in_weight": normal_values(arg_keys[4], (D, 2 * DI), D ** -0.5, 0.15625, ((0, 32),)),
        "conv_weight": normal_values(arg_keys[5], (CONV, DI), CONV ** -0.5, 3.0, (), jnp.float32),
        "conv_bias": normal_values(arg_keys[6], (DI,), 0.5, 3.0, (), jnp.float32),
        "xproj_weight": normal_values(arg_keys[7], (DI, DT_RANK + 2 * N_STATE), DI ** -0.5, 0.109375, ((0, 32),)),
        "dt_weight": normal_values(arg_keys[8], (DI, DT_RANK), DT_RANK ** -0.5, 0.625, ((0, 32),)),
        "dt_bias": jnp.clip(jax.random.uniform(arg_keys[9], (DI,), jnp.float32, -7.0, -2.0), -7.0, -2.0),
        "decay_log": jnp.clip(jax.random.uniform(arg_keys[10], (DI, N_STATE), jnp.float32, -7.0, 0.0), -7.0, 0.0),
        "skip_gain": jnp.clip(jax.random.uniform(arg_keys[11], (DI,), jnp.float32, 0.5, 1.5), 0.5, 1.5),
        "mamba_out_weight": normal_values(arg_keys[12], (DI, D), DI ** -0.5, 0.109375, ((0, 32),)),
        "attn_gain": jnp.clip(1.0 + 0.1 * jax.random.normal(arg_keys[13], (D,), jnp.float32), 0.5, 1.5),
        "mamba_gain": jnp.clip(1.0 + 0.1 * jax.random.normal(arg_keys[14], (D,), jnp.float32), 0.5, 1.5),
        "ffn_gain": jnp.clip(1.0 + 0.1 * jax.random.normal(arg_keys[15], (D,), jnp.float32), 0.5, 1.5),
        "gate_up_weight": normal_values(arg_keys[16], (D, 2 * FF), D ** -0.5, 0.15625, ((0, 32),)),
        "down_weight": normal_values(arg_keys[17], (FF, D), FF ** -0.5, 0.078125, ((0, 32),)),
        "cotangent": normal_values(arg_keys[18], (TOKENS, D), 1.0, 6.0, ((0, 128),)),
    }


@jax.custom_vjp
def low(v):
    return lax.optimization_barrier(v.astype(jnp.bfloat16)).astype(jnp.float32)

@jax.custom_vjp
def low_back(v):
    return v

def low_keep(v):
    return (low(v), None)

def low_pass(kept, grad):
    return (grad,)

def back_keep(v):
    return (v, None)

def back_low(kept, grad):
    return (low(grad),)
low.defvjp(low_keep, low_pass)
low_back.defvjp(back_keep, back_low)
EPS = 1e-05
NEG_BIG = -1e+30

def norm_scale(values, gain):
    return values * lax.rsqrt(lax.optimization_barrier(jnp.mean(values * values, axis=-1, keepdims=True)) + EPS) * gain

def matmul(operand, other):
    return jnp.dot(operand, other, precision=lax.Precision.HIGHEST)

def attend(queries, key_rows, value_rows):
    length = queries.shape[0]
    block_rows = min(512, length)
    per_group = HEADS // KV_HEADS
    score_scale = HEAD_DIM ** (-0.5)
    width = key_rows.shape[1]
    key_padded = jnp.concatenate([jnp.zeros((WINDOW, width), jnp.float32), key_rows])
    value_padded = jnp.concatenate([jnp.zeros((WINDOW, width), jnp.float32), value_rows])

    def one_block(block_index):
        first_row = block_index * block_rows
        query_block = lax.dynamic_slice_in_dim(queries, first_row, block_rows, 0).reshape(block_rows, KV_HEADS, per_group, HEAD_DIM)
        key_block = lax.dynamic_slice_in_dim(key_padded, first_row, WINDOW + block_rows, 0).reshape(WINDOW + block_rows, KV_HEADS, HEAD_DIM)
        value_block = lax.dynamic_slice_in_dim(value_padded, first_row, WINDOW + block_rows, 0).reshape(WINDOW + block_rows, KV_HEADS, HEAD_DIM)
        query_pos = first_row + jnp.arange(block_rows, dtype=jnp.int32)
        key_pos = first_row - WINDOW + jnp.arange(WINDOW + block_rows, dtype=jnp.int32)
        visible = (key_pos[None, :] >= 0) & (key_pos[None, :] <= query_pos[:, None]) & (query_pos[:, None] - key_pos[None, :] < WINDOW)
        scores = low_back(jnp.einsum('tkgd,skd->kgts', query_block, key_block, precision=lax.Precision.HIGHEST) * score_scale)
        masked = jnp.where(visible[None, None], scores, NEG_BIG)
        row_peak = lax.optimization_barrier(jnp.max(masked, axis=-1, keepdims=True))
        expd = jnp.exp(masked - row_peak)
        probs = expd / lax.optimization_barrier(jnp.sum(expd, axis=-1, keepdims=True))
        mixed = jnp.einsum('kgts,skd->tkgd', low(probs), value_block, precision=lax.Precision.HIGHEST)
        return mixed.reshape(block_rows, HEADS * HEAD_DIM)
    blocks = lax.map(jax.checkpoint(one_block), jnp.arange(length // block_rows, dtype=jnp.int32))
    return blocks.reshape(length, HEADS * HEAD_DIM)

def selective(step_size, inner_act, b_in, c_out, decay_rate):
    length = step_size.shape[0]
    blocks = length // TOK_DEV

    def token_scan(state_now, sequence):
        step_here, act_here, b_here, c_here = sequence
        state_next = jnp.exp(step_here[:, None] * decay_rate) * state_now + (step_here * act_here)[:, None] * b_here[None, :]
        return (state_next, lax.optimization_barrier(jnp.sum(state_next * c_here[None, :], axis=1)))

    def block_scan(state_now, sequence):
        return lax.scan(token_scan, state_now, sequence)
    shaped = tuple((array.reshape(blocks, TOK_DEV, array.shape[1]) for array in (step_size, inner_act, b_in, c_out)))
    _, outputs = lax.scan(jax.checkpoint(block_scan), jnp.zeros((DI, N_STATE), jnp.float32), shaped)
    return outputs.reshape(length, DI)

def layer(inputs, norm_gain, qkv_weight, attn_out_weight, in_weight, conv_weight, conv_bias, xproj_weight, dt_weight, dt_bias, decay_log, skip_gain, mamba_out_weight, attn_gain, mamba_gain, ffn_gain, gate_up_weight, down_weight):
    length = inputs.shape[0]
    head_width = HEADS * HEAD_DIM
    kv_width = KV_HEADS * HEAD_DIM
    normed = low(norm_scale(inputs, norm_gain))
    projected = low(low_back(matmul(normed, qkv_weight)))
    queries = projected[:, :head_width]
    key_rows = projected[:, head_width:head_width + kv_width]
    value_rows = projected[:, head_width + kv_width:]
    attended = low(low_back(attend(queries, key_rows, value_rows)))
    attn_branch = low_back(matmul(attended, attn_out_weight))
    in_proj = low_back(matmul(normed, in_weight))
    conv_in = in_proj[:, :DI]
    gate_z = in_proj[:, DI:]
    padded = jnp.concatenate([jnp.zeros((CONV - 1, DI), jnp.float32), conv_in])
    conv_sum = conv_bias
    for offset in range(CONV):
        conv_sum = conv_sum + conv_weight[offset] * padded[offset:offset + length]
    inner_act = low(jax.nn.silu(conv_sum))
    xproj = low_back(matmul(inner_act, xproj_weight))
    dt_low = low(xproj[:, :DT_RANK])
    b_in = xproj[:, DT_RANK:DT_RANK + N_STATE]
    c_out = xproj[:, DT_RANK + N_STATE:]
    pre = low_back(matmul(dt_low, dt_weight.T)) + dt_bias
    step_size = jax.nn.softplus(pre)
    decay_rate = -jnp.exp(decay_log)
    scan_out = selective(step_size, inner_act, b_in, c_out, decay_rate) + skip_gain * inner_act
    gated = low(scan_out * jax.nn.silu(gate_z))
    mamba_branch = low_back(matmul(gated, mamba_out_weight))
    residual = inputs + 0.5 * (norm_scale(attn_branch, attn_gain) + norm_scale(mamba_branch, mamba_gain))
    ffn_input = low(norm_scale(residual, ffn_gain))
    gate_up = low_back(matmul(ffn_input, gate_up_weight))
    hidden = low(jax.nn.silu(gate_up[:, :FF]) * gate_up[:, FF:])
    return residual + matmul(hidden, down_weight)

def reference(tokens, norm_gain, qkv_weight, attn_out_weight, in_weight, conv_weight, conv_bias, xproj_weight, dt_weight, dt_bias, decay_log, skip_gain, mamba_out_weight, attn_gain, mamba_gain, ffn_gain, gate_up_weight, down_weight, cotangent):
    params = tuple((array.astype(jnp.float32) for array in (norm_gain, qkv_weight, attn_out_weight, in_weight, conv_weight, conv_bias, xproj_weight, dt_weight, dt_bias, decay_log, skip_gain, mamba_out_weight, attn_gain, mamba_gain, ffn_gain, gate_up_weight, down_weight)))
    inputs = tokens.astype(jnp.float32).reshape(N_SEQ, SEQ_LEN, D)
    upstream = cotangent.astype(jnp.float32).reshape(N_SEQ, SEQ_LEN, D)

    def per_sequence(totals, sequence):
        seq_input, seq_cot = sequence
        result, pullback = jax.vjp(layer, seq_input, *params)
        gradients = pullback(seq_cot)
        return (tuple((running + new_grad for running, new_grad in zip(totals, gradients[1:]))), (result, gradients[0]))
    totals, (results, input_grads) = lax.scan(per_sequence, tuple((jnp.zeros_like(array) for array in params)), (inputs, upstream))
    return (results.reshape(TOKENS, D).astype(jnp.bfloat16), input_grads.reshape(TOKENS, D), totals[0], totals[1], totals[2], totals[3], totals[4], totals[5], totals[6], totals[7], totals[8], totals[9], totals[10], totals[11], totals[12], totals[13], totals[14], totals[15], totals[16])
```

```python
import functools

import jax
import jax.numpy as jnp
from jax import lax
from jax.experimental import pallas as pl
from jax.experimental.pallas import tpu as pltpu
from jax.sharding import PartitionSpec as P

D = 1600
HEADS = 25
KV_HEADS = 5
GROUP = HEADS // KV_HEADS
HEAD_DIM = 64
DI = 3200
N_STATE = 16
CONV = 4
DT_RANK = 100
FF = 5504
WINDOW = 1024
EPS = 1e-05
NEG_BIG = -1e30
LOG2E = 1.4426950408889634
LN2 = 0.6931471805599453

NX = 4
NC = 32
T = 128
KEYS = WINDOW + T
ROWS = 50
ROWS_P = 56
ROWS_64 = 64
DP = NC * ROWS_P
CH = DI // NX
CHP = 896
FFX = FF // NX
FFP = 1408
CSUB = CH // NC
FSUB = FFX // NC
QKV = 2240
QKV_P = 2304
AO_P = 1664
XD = 256

F32 = jnp.float32
BF16 = jnp.bfloat16
VMEM_LIMIT = 60 * 1024 * 1024


def dot(a, b, ca, cb, out=F32):
    return lax.dot_general(a, b, (((ca,), (cb,)), ((), ())), preferred_element_type=F32).astype(out)


def norm_scale(values, gain):
    return values * lax.rsqrt(jnp.mean(values * values, axis=-1, keepdims=True) + EPS) * gain


RIGHT = [(i, (i + 1) % NX) for i in range(NX)]
LEFT = [(i, (i - 1) % NX) for i in range(NX)]


def gather_x(v):
    half = v.shape[0] // 2
    before = lax.ppermute(v, "seq", RIGHT)
    after = lax.ppermute(v, "seq", LEFT)
    far_a = lax.ppermute(before[:half], "seq", RIGHT)
    far_b = lax.ppermute(after[half:], "seq", LEFT)
    return [v, after, jnp.concatenate([far_a, far_b]), before]


def scatter_x(parts):
    half = parts[0].shape[0] // 2
    from_left = lax.ppermute(parts[2][:half], "seq", RIGHT)
    from_right = lax.ppermute(parts[2][half:], "seq", LEFT)
    to_right = jnp.concatenate(
        [(parts[1][:half].astype(F32) + from_left.astype(F32)).astype(BF16), parts[1][half:]]
    )
    to_left = jnp.concatenate(
        [parts[3][:half], (parts[3][half:].astype(F32) + from_right.astype(F32)).astype(BF16)]
    )
    a = lax.ppermute(to_right, "seq", RIGHT)
    b = lax.ppermute(to_left, "seq", LEFT)
    return parts[0].astype(F32) + a.astype(F32) + b.astype(F32)


def total_x(v):
    blocks = [v[:, k * T : (k + 1) * T] for k in range(NX)]

    def turned(by):
        return jnp.concatenate([blocks[(k + by) % NX] for k in range(NX)], axis=1)

    a = lax.ppermute(turned(1), "seq", RIGHT)
    b = lax.ppermute(turned(-1), "seq", LEFT)
    c = lax.ppermute(turned(2), "seq", [(i, (i + 2) % NX) for i in range(NX)])
    return v.astype(F32) + a.astype(F32) + b.astype(F32) + c.astype(F32)


def in_order(pieces, place):
    out = []
    for j in range(NX):
        value = pieces[0]
        for k in range(1, NX):
            value = jnp.where(place == (j - k) % NX, pieces[k], value)
        out.append(value)
    return out


def place_index(x, z, y, c):
    return x * NC + z * 8 + y * 2 + c


TURN = [
    (place_index(x, z, y, c), place_index(z, y, 2 * c + x // 2, x % 2))
    for x in range(4)
    for z in range(4)
    for y in range(4)
    for c in range(2)
]
TURN_BACK = [(b, a) for a, b in TURN]


def shift_ctx(v, by):
    return lax.ppermute(v, "ctx", [(i, i + by) for i in range(NC) if 0 <= i + by < NC])


def tie(*values):
    return lax.optimization_barrier(values)


SWAP = [(i, i ^ 1) for i in range(NC)]


def carried(part, rate2, index, reverse):
    sign = -1 if reverse else 1

    def after(first, then):
        state = then[:, :N_STATE] + jnp.exp2(rate2[None] * then[:, N_STATE:]) * first[:, :N_STATE]
        return jnp.concatenate([state, first[:, N_STATE:] + then[:, N_STATE:]], axis=1)

    def keep(flag, v):
        return jnp.where(flag, v, 0.0)

    def send(v, pairs):
        flat = lax.ppermute(v.reshape(NX * (N_STATE + 1), CHP).astype(BF16), "ctx", pairs)
        return flat.astype(F32).reshape(NX, N_STATE + 1, CHP)

    core = index % 2
    y = (index // 2) % 4
    if reverse:
        core, y = 1 - core, 3 - y
    other = send(part, SWAP)
    inside = keep(core == 1, other)
    chip = jnp.where(core == 1, after(other, part), after(part, other))
    rows = []
    for k in range(1, 4):
        rows.append(send(chip, [(i, i // 8 * 8 + (i + sign * 2 * k) % 8) for i in range(NC)]))
    pre = [keep(y >= k, rows[k - 1]) for k in range(1, 4)]
    suc = [keep(y < k, rows[k - 1]) for k in range(1, 4)]
    row_pre = after(after(pre[2], pre[1]), pre[0])
    row = after(after(after(after(row_pre, chip), suc[2]), suc[1]), suc[0])
    planes = []
    for k in range(1, 4):
        by = sign * 8 * k
        planes.append(send(row, [(i, i + by) for i in range(NC) if 0 <= i + by < NC]))
    plane_pre = after(after(planes[2], planes[1]), planes[0])
    return after(after(plane_pre, row_pre), inside)[:, :N_STATE]


def key_window(own, core):
    mine = jnp.concatenate([shift_ctx(own, 2 * k) for k in (4, 3, 2, 1)] + [own])
    other = lax.ppermute(mine, "ctx", SWAP)
    odd = jnp.where(core == 0, other[: 4 * T], other[T:])
    blocks = []
    for k in range(4):
        blocks += [mine[k * T : (k + 1) * T], odd[k * T : (k + 1) * T]]
    return jnp.concatenate(blocks + [mine[4 * T :]])


def key_window_back(grad, core):
    blocks = [grad[k * T : (k + 1) * T] for k in range(9)]
    other = lax.ppermute(jnp.concatenate(blocks[1::2]).astype(BF16), "ctx", SWAP).astype(F32)
    none = jnp.zeros_like(blocks[0])
    mine = jnp.concatenate(blocks[::2]) + jnp.where(
        core == 0, jnp.concatenate([none, other]), jnp.concatenate([other, none])
    )
    total = mine[4 * T :]
    for k in range(1, 5):
        term = mine[(4 - k) * T : (5 - k) * T].astype(BF16)
        total = total + shift_ctx(term, -2 * k).astype(F32)
    return total


TILES = CHP // 128


def lanes(j):
    return slice(j * 128, (j + 1) * 128)


def spread(source, target):
    for t in range(T):
        target[t] = jnp.broadcast_to(source[:, t : t + 1], (N_STATE, 128))


CHUNK = 16
WIDE = CHUNK * N_STATE
SCAN_GROUPS = ((0, 1, 2, 3), (4, 5, 6))
ADJOINT_GROUPS = ((0, 1, 2), (3, 4), (5, 6))


def chunk_diagonal():
    column = lax.broadcasted_iota(jnp.int32, (T, WIDE), 1) // N_STATE
    return column == lax.broadcasted_iota(jnp.int32, (T, WIDE), 0) % CHUNK


def chunk_rows(coef):
    pick = lax.broadcasted_iota(jnp.int32, (N_STATE, WIDE), 1) % N_STATE
    pick = (pick == lax.broadcasted_iota(jnp.int32, (N_STATE, WIDE), 0)).astype(BF16)
    wide = dot(coef.astype(BF16), pick, 0, 0)
    return jnp.where(chunk_diagonal(), wide, 0.0).astype(BF16)


def lane_sums(partial):
    flat = partial.reshape(T * N_STATE, 128).astype(BF16)
    wide = dot(flat, jnp.ones((128, 128), BF16), 1, 0).reshape(T, N_STATE, 128)
    token = lax.broadcasted_iota(jnp.int32, (T, N_STATE, 128), 0)
    lane = lax.broadcasted_iota(jnp.int32, (T, N_STATE, 128), 2)
    return jnp.sum(jnp.where(token == lane, wide, 0.0), axis=0)


def token_rows(chunk):
    return pl.ds(pl.multiple_of(chunk * CHUNK, CHUNK), CHUNK)


def state_rows(token):
    return pl.ds(pl.multiple_of(token * N_STATE, N_STATE), N_STATE)


def forward_scan(step, drive, spread_b, rate2, group, states, emit):
    rates = [rate2[:, lanes(j)] for j in group]

    def one(chunk, states):
        rows = token_rows(chunk)
        steps = [step[rows, lanes(j)] for j in group]
        drives = [drive[rows, lanes(j)] for j in group]
        states = list(states)
        for r in range(CHUNK):
            b_here = spread_b[chunk * CHUNK + r]
            for k, j in enumerate(group):
                a = jnp.exp2(steps[k][r : r + 1] * rates[k])
                states[k] = a * states[k] + drives[k][r : r + 1] * b_here
                emit(chunk * CHUNK + r, j, states[k])
        return tuple(states)

    return lax.fori_loop(0, T // CHUNK, one, tuple(states))


def chunks():
    return [(slice(c * CHUNK, (c + 1) * CHUNK), slice(c * WIDE, (c + 1) * WIDE)) for c in range(T // CHUNK)]


def scan_end_kernel(step, act, b_t, rate2, out, spread_b, drive):
    spread(b_t, spread_b)
    drive[...] = step[...] * act[...].astype(F32)
    for group in SCAN_GROUPS:
        zero = [jnp.zeros((N_STATE, 128), F32) for _ in group]
        states = forward_scan(step, drive, spread_b, rate2, group, zero, lambda t, j, h: None)
        for k, j in enumerate(group):
            out[0, :N_STATE, lanes(j)] = states[k]
    out[0, N_STATE:, :] = jnp.sum(step[...], axis=0, keepdims=True)


def scan_kernel(
    step, act, gate_z, b_t, c_t, start, rate2, skip, states_out, scan_out, gated, spread_b, drive, sum_c
):
    spread(b_t, spread_b)
    drive[...] = step[...] * act[...].astype(F32)
    sum_c[...] = chunk_rows(c_t[...])

    def emit(t, j, h):
        states_out[0, state_rows(t), lanes(j)] = h.astype(BF16)

    for group in SCAN_GROUPS:
        forward_scan(step, drive, spread_b, rate2, group, [start[0, :, lanes(j)] for j in group], emit)
    for rows, wide in chunks():
        y = dot(sum_c[rows, :], states_out[0, wide, :], 1, 0) + skip[...] * act[rows, :].astype(F32)
        scan_out[rows, :] = y
        z = gate_z[rows, :]
        gated[rows, :] = (y * (z * jax.nn.sigmoid(z))).astype(BF16)


def adjoint_end_kernel(step, g_scan, c_t, rate2, out, spread_c):
    spread(c_t, spread_c)
    for group in SCAN_GROUPS:
        rates = [rate2[:, lanes(j)] for j in group]

        def one(lap, adjoints):
            chunk = T // CHUNK - 1 - lap
            rows = token_rows(chunk)
            steps = [step[rows, lanes(j)] for j in group]
            grads = [g_scan[rows, lanes(j)] for j in group]
            adjoints = list(adjoints)
            for r in reversed(range(CHUNK)):
                c_here = spread_c[chunk * CHUNK + r]
                for k in range(len(group)):
                    a = jnp.exp2(steps[k][r : r + 1] * rates[k])
                    adjoints[k] = a * (grads[k][r : r + 1] * c_here + adjoints[k])
            return tuple(adjoints)

        zero = tuple(jnp.zeros((N_STATE, 128), F32) for _ in group)
        adjoints = lax.fori_loop(0, T // CHUNK, one, zero)
        for k, j in enumerate(group):
            out[0, :N_STATE, lanes(j)] = adjoints[k]
    out[0, N_STATE:, :] = jnp.sum(step[...], axis=0, keepdims=True)


def adjoint_kernel(
    step, act, g_scan, b_t, c_t, states, start, later, rate2, skip,
    g_step, g_act, g_rate, g_b, g_c, spread_c, drive, sum_b, adjoint, flow_rate, part_b, part_c,
):
    spread(c_t, spread_c)
    drive[...] = step[...] * act[...].astype(F32)
    sum_b[...] = chunk_rows(b_t[...])
    ones = chunk_diagonal()[:CHUNK].astype(BF16)
    for group in ADJOINT_GROUPS:
        rates = [rate2[:, lanes(j)] for j in group]

        def one(lap, carry):
            chunk = T // CHUNK - 1 - lap
            rows = token_rows(chunk)
            steps = [step[rows, lanes(j)] for j in group]
            grads = [g_scan[rows, lanes(j)] for j in group]
            drives = [drive[rows, lanes(j)] for j in group]
            adjoints, totals = list(carry[0]), list(carry[1])
            last = chunk * CHUNK + CHUNK - 1
            held = [states[0, state_rows(last), lanes(j)].astype(F32) for j in group]
            for r in reversed(range(CHUNK)):
                t = chunk * CHUNK + r
                here = state_rows(t)
                c_here = spread_c[t]
                b_sum = c_sum = None
                for k, j in enumerate(group):
                    g_row = grads[k][r : r + 1]
                    lam = g_row * c_here + adjoints[k]
                    adjoint[here, lanes(j)] = lam.astype(BF16)
                    step_row = steps[k][r : r + 1]
                    m = jnp.exp2(step_row * rates[k]) * lam
                    b_term = lam * drives[k][r : r + 1]
                    c_term = held[k] * g_row
                    b_sum = b_term if b_sum is None else b_sum + b_term
                    c_sum = c_term if c_sum is None else c_sum + c_term
                    before = states[0, state_rows(jnp.maximum(t - 1, 0)), lanes(j)].astype(F32)
                    if r == 0:
                        before = jnp.where(chunk == 0, start[0, :, lanes(j)], before)
                    flow = m * before
                    totals[k] = totals[k] + flow * step_row
                    flow_rate[here, lanes(j)] = (flow * rates[k]).astype(BF16)
                    adjoints[k] = m
                    held[k] = before
                if group[0] == 0:
                    part_b[t] = b_sum
                    part_c[t] = c_sum
                else:
                    part_b[t] += b_sum
                    part_c[t] += c_sum
            return (tuple(adjoints), tuple(totals))

        zero = tuple(jnp.zeros((N_STATE, 128), F32) for _ in group)
        first = tuple(later[0, :, lanes(j)] for j in group)
        _, totals = lax.fori_loop(0, T // CHUNK, one, (first, zero))
        for k, j in enumerate(group):
            g_rate[0, :, lanes(j)] = totals[k]
    for rows, wide in chunks():
        lam_b = dot(sum_b[rows, :], adjoint[wide, :], 1, 0)
        flow_sum = dot(ones, flow_rate[wide, :], 1, 0)
        g_step[rows, :] = flow_sum * LN2 + act[rows, :].astype(F32) * lam_b
        g_act[rows, :] = step[rows, :] * lam_b + skip[...] * g_scan[rows, :]
    g_b[...] = lane_sums(part_b[...])
    g_c[...] = lane_sums(part_c[...])


def seq_call(kernel, ins, outs, scratch, cost):
    def spec(shape, kind):
        if kind == "rows":
            return pl.BlockSpec((shape[0] // NX,) + tuple(shape[1:]), lambda s: (s, 0))
        if kind == "lanes":
            return pl.BlockSpec((shape[0], shape[1] // NX), lambda s: (0, s))
        if kind == "lead":
            return pl.BlockSpec((1,) + tuple(shape[1:]), lambda s: (s, 0, 0))
        return pl.BlockSpec(tuple(shape), lambda s: (0,) * len(shape))

    return pl.pallas_call(
        kernel,
        grid=(NX,),
        in_specs=[spec(a.shape, kind) for a, kind in ins],
        out_specs=[spec(shape, kind) for shape, _, kind in outs],
        out_shape=[jax.ShapeDtypeStruct(shape, dtype) for shape, dtype, _ in outs],
        scratch_shapes=scratch,
        compiler_params=pltpu.CompilerParams(vmem_limit_bytes=VMEM_LIMIT),
        cost_estimate=cost,
    )(*[a for a, _ in ins])


def cost(us):
    return pl.CostEstimate(flops=int(us * 1e9), bytes_accessed=int(us * 1e6), transcendentals=0)


def visible_keys(lowest):
    t = lax.broadcasted_iota(jnp.int32, (T, KEYS), 0)
    s = lax.broadcasted_iota(jnp.int32, (T, KEYS), 1)
    return (s > t) & (s <= t + WINDOW) & (s >= lowest)


def attend_kernel(lowest, q, k, v, out, lse):
    seen = visible_keys(lowest[0])
    for g in range(GROUP):
        rows = slice(g * T, (g + 1) * T)
        scores = jnp.where(seen, dot(q[0, rows, :], k[0], 1, 1), NEG_BIG)
        peak = jnp.max(scores, axis=-1, keepdims=True)
        raised = jnp.exp(scores - peak)
        mass = jnp.sum(raised, axis=-1, keepdims=True)
        probs = (raised / mass).astype(BF16)
        out[0, rows, :] = dot(probs, v[0], 1, 0, BF16)
        lse[0, rows, :] = peak + jnp.log(mass)


def attend_back_kernel(lowest, q, k, v, g_out, lse, g_q, g_k, g_v):
    seen = visible_keys(lowest[0])
    for g in range(GROUP):
        rows = slice(g * T, (g + 1) * T)
        q_here = q[0, rows, :]
        g_here = g_out[0, rows, :]
        scores = jnp.where(seen, dot(q_here, k[0], 1, 1), NEG_BIG)
        probs = jnp.exp(scores - lse[0, rows, :])
        g_probs = dot(g_here, v[0], 1, 1)
        inner = jnp.sum(probs * g_probs, axis=-1, keepdims=True)
        g_scores = (probs * (g_probs - inner)).astype(BF16)
        g_q[0, rows, :] = (dot(g_scores, k[0], 1, 0) * HEAD_DIM ** (-0.5)).astype(BF16)
        k_term = dot(g_scores, q_here, 0, 0)
        v_term = dot(probs.astype(BF16), g_here, 0, 0)
        if g == 0:
            g_k[0] = k_term
            g_v[0] = v_term
        else:
            g_k[0] += k_term
            g_v[0] += v_term


def head_call(kernel, lowest, ins, outs, us):
    def spec(shape):
        return pl.BlockSpec((1,) + tuple(shape[1:]), lambda h: (h, 0, 0))

    return pl.pallas_call(
        kernel,
        grid=(KV_HEADS,),
        in_specs=[pl.BlockSpec(memory_space=pltpu.SMEM)] + [spec(a.shape) for a in ins],
        out_specs=[spec(shape) for shape, _ in outs],
        out_shape=[jax.ShapeDtypeStruct(shape, dtype) for shape, dtype in outs],
        compiler_params=pltpu.CompilerParams(vmem_limit_bytes=VMEM_LIMIT),
        cost_estimate=cost(us),
    )(lowest, *ins)


def split_queries(v):
    return v.reshape(T, KV_HEADS, GROUP, HEAD_DIM).transpose(1, 2, 0, 3).reshape(KV_HEADS, GROUP * T, HEAD_DIM)


def join_queries(v):
    return v.reshape(KV_HEADS, GROUP, T, HEAD_DIM).transpose(2, 0, 1, 3).reshape(T, HEADS * HEAD_DIM)


def split_keys(v):
    return v.reshape(v.shape[0], KV_HEADS, HEAD_DIM).transpose(1, 0, 2)


def join_keys(v):
    return v.transpose(1, 0, 2).reshape(v.shape[1], KV_HEADS * HEAD_DIM)


def pad_to(v, rows, columns):
    return jnp.pad(v, ((0, rows - v.shape[0]), (0, columns - v.shape[1])))


def rows_64(v):
    turned = v.T.reshape(NC, ROWS_P, v.shape[0])
    return jnp.pad(turned, ((0, 0), (0, ROWS_64 - ROWS_P), (0, 0))).reshape(NC * ROWS_64, v.shape[0])


def products_kernel(count, *refs):
    out = refs[-1]
    at = 0
    for k in range(count):
        width = refs[2 * k + 1].shape[1]
        out[:, at : at + width] = dot(refs[2 * k][...], refs[2 * k + 1][...], 1, 0, BF16)
        at += width


def products(pairs, us):
    block = 512
    rows = NC * ROWS_64
    width = sum(b.shape[1] for _, b in pairs)
    specs = []
    for a, b in pairs:
        specs.append(pl.BlockSpec((block, a.shape[1]), lambda i: (i, 0)))
        specs.append(pl.BlockSpec(b.shape, lambda i: (0, 0)))
    return pl.pallas_call(
        functools.partial(products_kernel, len(pairs)),
        grid=(rows // block,),
        in_specs=specs,
        out_specs=pl.BlockSpec((block, width), lambda i: (i, 0)),
        out_shape=jax.ShapeDtypeStruct((rows, width), BF16),
        compiler_params=pltpu.CompilerParams(vmem_limit_bytes=VMEM_LIMIT),
        cost_estimate=cost(us),
    )(*[v for pair in pairs for v in pair])


def rows_sum(v):
    return lax.psum_scatter(v, "ctx", scatter_dimension=0, tiled=True)


def ring_sum(v, dim, place, plus, minus):
    parts = [lax.dynamic_index_in_dim(v, (place + k) % 4, dim, False) for k in range(4)]
    half = v.shape[-1] // 2
    from_left = lax.ppermute(parts[2][..., :half], "ctx", plus)
    from_right = lax.ppermute(parts[2][..., half:], "ctx", minus)
    to_right = jnp.concatenate(
        [(parts[1][..., :half].astype(F32) + from_left.astype(F32)).astype(BF16), parts[1][..., half:]], axis=-1
    )
    to_left = jnp.concatenate(
        [parts[3][..., :half], (parts[3][..., half:].astype(F32) + from_right.astype(F32)).astype(BF16)], axis=-1
    )
    a = lax.ppermute(to_right, "ctx", plus)
    b = lax.ppermute(to_left, "ctx", minus)
    return parts[0].astype(F32) + a.astype(F32) + b.astype(F32)


def ring_pairs(stride, by):
    return [(i, i + (((i // stride) % 4 + by) % 4 - (i // stride) % 4) * stride) for i in range(NC)]


def rows_sum_by_rings(v, index, y_first):
    core, y, z = index % 2, (index // 2) % 4, index // 8
    width = v.shape[1]
    v = v.reshape(NC // 2, 2, ROWS_P, width)
    other = lax.ppermute(lax.dynamic_index_in_dim(v, 1 - core, 1, False), "ctx", SWAP)
    v = lax.dynamic_index_in_dim(v, core, 1, False).astype(F32) + other.astype(F32)
    v = v.astype(BF16).reshape(4, 4, ROWS_P, width)
    along_y = (y, ring_pairs(2, 1), ring_pairs(2, -1))
    along_z = (z, ring_pairs(8, 1), ring_pairs(8, -1))
    if y_first:
        return ring_sum(ring_sum(v, 1, *along_y).astype(BF16), 0, *along_z)
    return ring_sum(ring_sum(v, 0, *along_z).astype(BF16), 0, *along_y)


def body(
    tokens,
    norm_gain,
    qkv_weight,
    attn_out_weight,
    in_weight,
    conv_weight,
    conv_bias,
    xproj_weight,
    dt_weight,
    dt_bias,
    decay_log,
    skip_gain,
    mamba_out_weight,
    attn_gain,
    mamba_gain,
    ffn_gain,
    gate_up_weight,
    down_weight,
    cotangent,
):
    x = lax.axis_index("seq")
    index = lax.axis_index("ctx")

    def columns(v, first, count):
        return lax.dynamic_slice_in_dim(v, first, count, v.ndim - 1)

    def order(count, size, rows):
        place = lax.broadcasted_iota(jnp.int32, (size, DP), 1)
        source = place // ROWS_P * rows + place % ROWS_P
        hit = (source == lax.broadcasted_iota(jnp.int32, (size, DP), 0)) & (place % ROWS_P < rows)
        return lax.optimization_barrier((hit & (source < count)).astype(BF16))

    widen_m = order(D, D, ROWS)
    widen_channels = order(CH, CHP, CSUB)
    widen_hidden = order(FFX, FFP, FSUB)

    def widen(v, matrix=widen_m):
        return dot(v, matrix, 1, 0, BF16)

    def narrow(v, matrix=widen_m):
        return dot(v.astype(BF16), matrix, 1, 1)

    by_channel = pad_to(jnp.concatenate([xproj_weight, dt_weight], axis=1), 2 * ROWS, XD)
    first = jnp.concatenate(
        [
            pad_to(columns(in_weight, x * CH, CH), ROWS_P, CHP),
            pad_to(columns(in_weight, DI + x * CH, CH), ROWS_P, CHP),
            pad_to(by_channel[:ROWS], ROWS_P, XD),
            pad_to(by_channel[ROWS:], ROWS_P, XD),
        ],
        axis=1,
    )
    first = lax.all_gather(first, "ctx", axis=0, tiled=True)
    sub_mamba = lax.dynamic_slice_in_dim(mamba_out_weight, x * CSUB, CSUB, 0)
    sub_down = lax.dynamic_slice_in_dim(down_weight, x * FSUB, FSUB, 0)
    sub_wide = lax.ppermute(
        jnp.concatenate([pad_to(sub_down, 48, D), pad_to(sub_mamba, 32, D)]), ("seq", "ctx"), TURN
    )
    second = jnp.concatenate(
        [
            pad_to(qkv_weight, ROWS_P, QKV_P),
            pad_to(attn_out_weight, ROWS_P, AO_P),
            pad_to(sub_wide[48 : 48 + CSUB], ROWS_P, AO_P),
        ],
        axis=1,
    )
    second = lax.all_gather(second, "ctx", axis=0, tiled=True)
    third = jnp.concatenate(
        [
            pad_to(columns(gate_up_weight, x * FFX, FFX), ROWS_P, FFP),
            pad_to(columns(gate_up_weight, FF + x * FFX, FFX), ROWS_P, FFP),
            pad_to(sub_wide[:FSUB], ROWS_P, AO_P),
        ],
        axis=1,
    )
    third = lax.all_gather(third, "ctx", axis=0, tiled=True)
    w_in = first[:, : 2 * CHP]
    small = first[:, 2 * CHP :].reshape(NC, ROWS_P, 2 * XD)
    small = lax.dynamic_slice_in_dim(small, x * (NC // NX), NC // NX, 0)[:, :ROWS]
    small = jnp.stack([small[:, :, :XD], small[:, :, XD:]], axis=1).reshape(CH, XD)
    w_small = pad_to(small, CHP, XD)
    w_xproj = w_small[:, : DT_RANK + 2 * N_STATE]
    w_dt = w_small[:, DT_RANK + 2 * N_STATE : 2 * DT_RANK + 2 * N_STATE]
    w_qkv = second[:, :QKV]
    w_attn = second[:, QKV_P : QKV_P + D]
    w_mamba = second[:, QKV_P + AO_P :]
    w_gate_up = third[:, : 2 * FFP]
    w_down = third[:, 2 * FFP :]

    def channel(v):
        part = columns(v, x * CH, CH)
        return jnp.pad(part, ((0, 0),) * (v.ndim - 1) + ((0, CHP - CH),))

    taps = channel(conv_weight)
    conv_b = channel(conv_bias)[None]
    dt_b = channel(dt_bias)[None]
    skip = channel(skip_gain)[None]
    decay_rate = -jnp.exp(channel(decay_log.T))
    rate2 = decay_rate * LOG2E

    inputs = tokens.astype(F32)
    normed_f, norm1_pullback = jax.vjp(norm_scale, inputs, norm_gain)
    normed = widen(normed_f.astype(BF16))
    normed_all = jnp.concatenate(gather_x(normed))
    cot_all = jnp.concatenate(gather_x(pad_to(cotangent, T, AO_P)))

    in_proj = dot(normed_all, w_in, 1, 0)
    conv_in = in_proj[:, :CHP].reshape(NX, T, CHP)
    gate_z = in_proj[:, CHP:]
    tails = shift_ctx(conv_in[:, T - (CONV - 1) :].reshape(NX * (CONV - 1), CHP), 1)
    padded = jnp.concatenate([tails.reshape(NX, CONV - 1, CHP), conv_in], axis=1)
    conv_sum = conv_b[None]
    for j in range(CONV):
        conv_sum = conv_sum + taps[j] * padded[:, j : j + T]
    conv_sum = conv_sum.reshape(NX * T, CHP)
    act_f, conv_pullback = jax.vjp(jax.nn.silu, conv_sum)
    act = act_f.astype(BF16)
    xproj_t = total_x(dot(w_xproj, act, 0, 1, BF16))
    dt_low_t = xproj_t[:DT_RANK].astype(BF16)
    b_t = xproj_t[DT_RANK : DT_RANK + N_STATE]
    c_t = xproj_t[DT_RANK + N_STATE :]
    pre = dot(dt_low_t, w_dt, 0, 1) + dt_b
    step = jax.nn.softplus(pre)
    (scan_end,) = seq_call(
        scan_end_kernel,
        [(step, "rows"), (act, "rows"), (b_t, "lanes"), (rate2, "all")],
        [((NX, N_STATE + 1, CHP), F32, "lead")],
        [pltpu.VMEM((T, N_STATE, 128), F32), pltpu.VMEM((T, CHP), F32)],
        cost(8),
    )
    start = carried(scan_end, rate2, index, False)

    projected = dot(normed, w_qkv, 1, 0, BF16)
    kv_own = projected[:, D:]
    core = index % 2
    kv = key_window(kv_own, core)
    queries = split_queries(projected[:, :D] * jnp.asarray(HEAD_DIM ** (-0.5), BF16))
    keys = split_keys(kv[:, : KV_HEADS * HEAD_DIM])
    values = split_keys(kv[:, KV_HEADS * HEAD_DIM :])
    lowest = jnp.maximum(0, WINDOW - index * T).astype(jnp.int32).reshape(1)
    attended_h, lse = head_call(
        attend_kernel,
        lowest,
        [queries, keys, values],
        [((KV_HEADS, GROUP * T, HEAD_DIM), BF16), ((KV_HEADS, GROUP * T, 1), F32)],
        12,
    )
    attended = widen(join_queries(attended_h))
    attn_branch = dot(attended, w_attn, 1, 0)

    states, scan_out, gated = seq_call(
        scan_kernel,
        [
            (step, "rows"),
            (act, "rows"),
            (gate_z, "rows"),
            (b_t, "lanes"),
            (c_t, "lanes"),
            (start, "lead"),
            (rate2, "all"),
            (skip, "all"),
        ],
        [
            ((NX, T * N_STATE, CHP), BF16, "lead"),
            ((NX * T, CHP), F32, "rows"),
            ((NX * T, CHP), BF16, "rows"),
        ],
        [
            pltpu.VMEM((T, N_STATE, 128), F32),
            pltpu.VMEM((T, CHP), F32),
            pltpu.VMEM((T, WIDE), BF16),
        ],
        cost(14),
    )
    gated = widen(gated, widen_channels)
    mamba_terms = dot(gated, w_mamba, 1, 0, BF16)
    mamba_branch = scatter_x([mamba_terms[k * T : (k + 1) * T] for k in range(NX)])[:, :D]

    def mixing(attn_part, mamba_part, gain_attn, gain_mamba):
        return 0.5 * (norm_scale(attn_part, gain_attn) + norm_scale(mamba_part, gain_mamba))

    mixed, mix_pullback = jax.vjp(mixing, attn_branch, mamba_branch, attn_gain, mamba_gain)
    residual = inputs + mixed
    ffn_f, norm2_pullback = jax.vjp(norm_scale, residual, ffn_gain)
    ffn_all = jnp.concatenate(gather_x(widen(ffn_f.astype(BF16))))
    g_hidden = narrow(dot(cot_all, w_down, 1, 1, BF16), widen_hidden)
    ffn_all, g_hidden = tie(ffn_all, g_hidden)
    gate_up = dot(ffn_all, w_gate_up, 1, 0)

    def swiglu(gate, up):
        return jax.nn.silu(gate) * up

    hidden_f, swiglu_pullback = jax.vjp(swiglu, gate_up[:, :FFP], gate_up[:, FFP:])
    hidden = widen(hidden_f.astype(BF16), widen_hidden)
    g_gate, g_up = swiglu_pullback(g_hidden)
    g_gate_up = jnp.concatenate([g_gate.astype(BF16), g_up.astype(BF16)], axis=1)
    g_ffn_terms = dot(g_gate_up, w_gate_up, 1, 1, BF16)
    g_ffn_in = narrow(scatter_x([g_ffn_terms[k * T : (k + 1) * T] for k in range(NX)]))
    down_terms = dot(hidden, w_down, 1, 0, BF16)
    down_sum = scatter_x([down_terms[k * T : (k + 1) * T] for k in range(NX)])
    output = (residual + down_sum[:, :D]).astype(BF16)
    g_norm2, g_ffn_gain = norm2_pullback(g_ffn_in)
    g_residual = cotangent.astype(F32) + g_norm2
    g_attn_f, g_mamba_f, g_attn_gain, g_mamba_gain = mix_pullback(g_residual)
    g_attn = g_attn_f.astype(BF16)
    g_mamba_all = jnp.concatenate(gather_x(pad_to(g_mamba_f.astype(BF16), T, AO_P)))

    ffn_term = products([(rows_64(ffn_all), g_gate_up), (rows_64(hidden), cot_all)], 12)
    ffn_sum = rows_sum(ffn_term)
    g_mamba_all, ffn_term = tie(g_mamba_all, ffn_term)

    (g_gated,) = tie(narrow(dot(g_mamba_all, w_mamba, 1, 1, BF16), widen_channels))
    silu_z, gate_pullback = jax.vjp(jax.nn.silu, gate_z)
    g_scan = g_gated * silu_z
    (g_gate_z,) = gate_pullback(g_gated * scan_out)
    g_skip = jnp.sum(g_scan * act.astype(F32), axis=0)
    (adjoint_end,) = seq_call(
        adjoint_end_kernel,
        [(step, "rows"), (g_scan, "rows"), (c_t, "lanes"), (rate2, "all")],
        [((NX, N_STATE + 1, CHP), F32, "lead")],
        [pltpu.VMEM((T, N_STATE, 128), F32)],
        cost(8),
    )
    later = carried(adjoint_end, rate2, index, True)

    g_attended = narrow(dot(g_attn, w_attn, 1, 1, BF16)).astype(BF16)
    g_queries, g_keys, g_values = head_call(
        attend_back_kernel,
        lowest,
        [queries, keys, values, split_queries(g_attended), lse],
        [
            ((KV_HEADS, GROUP * T, HEAD_DIM), BF16),
            ((KV_HEADS, KEYS, HEAD_DIM), F32),
            ((KV_HEADS, KEYS, HEAD_DIM), F32),
        ],
        25,
    )
    g_kv = jnp.concatenate([join_keys(g_keys), join_keys(g_values)], axis=1)
    g_kv = key_window_back(g_kv, core)
    g_projected = jnp.concatenate([join_queries(g_queries), g_kv.astype(BF16)], axis=1)
    branch_term = products(
        [(rows_64(attended), pad_to(g_attn, T, AO_P)), (rows_64(gated), g_mamba_all)], 8
    )
    branch_term, ffn_sum = tie(branch_term, ffn_sum)
    branch_sum = rows_sum(branch_term)
    qkv_term = dot(normed, pad_to(g_projected, T, QKV_P), 0, 0, BF16)
    qkv_sum = rows_sum_by_rings(qkv_term, index, True)
    g_normed_attn = dot(g_projected, w_qkv, 1, 1)
    later, g_queries = tie(later, g_queries)

    g_step, g_act, g_rate, g_b, g_c = seq_call(
        adjoint_kernel,
        [
            (step, "rows"),
            (act, "rows"),
            (g_scan, "rows"),
            (b_t, "lanes"),
            (c_t, "lanes"),
            (states, "lead"),
            (start, "lead"),
            (later, "lead"),
            (rate2, "all"),
            (skip, "all"),
        ],
        [
            ((NX * T, CHP), F32, "rows"),
            ((NX * T, CHP), F32, "rows"),
            ((NX, N_STATE, CHP), F32, "lead"),
            ((N_STATE, NX * T), F32, "lanes"),
            ((N_STATE, NX * T), F32, "lanes"),
        ],
        [
            pltpu.VMEM((T, N_STATE, 128), F32),
            pltpu.VMEM((T, CHP), F32),
            pltpu.VMEM((T, WIDE), BF16),
            pltpu.VMEM((T * N_STATE, CHP), BF16),
            pltpu.VMEM((T * N_STATE, CHP), BF16),
            pltpu.VMEM((T, N_STATE, 128), F32),
            pltpu.VMEM((T, N_STATE, 128), F32),
        ],
        cost(25),
    )
    g_decay = jnp.sum(g_rate, axis=0) * decay_rate
    g_pre_f = g_step * jax.nn.sigmoid(pre)
    g_dt_bias = jnp.sum(g_pre_f, axis=0)
    g_pre = g_pre_f.astype(BF16)
    dt_term = dot(g_pre, dt_low_t, 0, 1, BF16)
    g_xproj_t = jnp.concatenate([dot(w_dt, g_pre, 0, 1), g_b, g_c]).astype(BF16)
    g_xproj_t = total_x(g_xproj_t).astype(BF16)
    xproj_term = dot(act, g_xproj_t, 0, 1, BF16)
    g_act = g_act + dot(g_xproj_t, w_xproj, 0, 1)
    (g_conv_sum,) = conv_pullback(g_act)
    g_conv_bias = jnp.sum(g_conv_sum, axis=0)
    g_conv_3 = g_conv_sum.reshape(NX, T, CHP)
    g_taps = [jnp.sum(g_conv_3 * padded[:, j : j + T], axis=(0, 1)) for j in range(CONV)]
    g_padded = jnp.zeros((NX, T + CONV - 1, CHP), F32)
    for j in range(CONV):
        g_padded = g_padded + jnp.pad(taps[j] * g_conv_3, ((0, 0), (j, CONV - 1 - j), (0, 0)))
    back = shift_ctx(g_padded[:, : CONV - 1].reshape(NX * (CONV - 1), CHP).astype(BF16), -1)
    back = back.astype(F32).reshape(NX, CONV - 1, CHP)
    g_conv_in = g_padded[:, CONV - 1 :] + jnp.pad(back, ((0, 0), (T - (CONV - 1), 0), (0, 0)))
    g_in_proj = jnp.concatenate(
        [g_conv_in.reshape(NX * T, CHP).astype(BF16), g_gate_z.astype(BF16)], axis=1
    )
    small_term = pad_to(jnp.concatenate([xproj_term[:CH], dt_term[:CH]], axis=1), CH, XD)
    small_term = jnp.pad(small_term.reshape(NC, CSUB, XD), ((0, 0), (0, ROWS_P - CSUB), (0, 0)))
    in_term = jnp.concatenate(
        [dot(normed_all, g_in_proj, 0, 0, BF16), small_term.reshape(DP, XD)], axis=1
    )
    in_sum = rows_sum_by_rings(in_term, index, False).astype(BF16)
    g_normed_terms = dot(g_in_proj, w_in, 1, 1, BF16)
    g_normed = scatter_x([g_normed_terms[k * T : (k + 1) * T] for k in range(NX)]) + g_normed_attn
    g_norm1, g_norm_gain = norm1_pullback(narrow(g_normed))
    tokens_grad = g_residual + g_norm1

    def all_columns(total, width):
        pieces = in_order(gather_x(total), x)
        halves = []
        for first_column in range(0, total.shape[1], total.shape[1] // 2):
            halves += [p[:ROWS, first_column : first_column + width] for p in pieces]
        return jnp.concatenate(halves, axis=1).astype(F32)

    def sequences_sum(total, width):
        a, b, c, d = gather_x(total)
        return (a.astype(F32) + b.astype(F32) + c.astype(F32) + d.astype(F32))[:ROWS, :width]

    def all_rows(total):
        turned = lax.ppermute(total, ("seq", "ctx"), TURN_BACK)
        a = lax.ppermute(turned, "seq", RIGHT)
        b = lax.ppermute(turned, "seq", LEFT)
        c = lax.ppermute(turned, "seq", [(i, (i + 2) % NX) for i in range(NX)])
        return jnp.concatenate(in_order([turned, b, c, a], x)).astype(F32)

    small_rows = all_rows(in_sum[:CSUB, 2 * CHP :])
    g_xproj_w = small_rows[:, : DT_RANK + 2 * N_STATE]
    g_dt_w = small_rows[:, DT_RANK + 2 * N_STATE : 2 * DT_RANK + 2 * N_STATE]

    gains = jnp.stack([g_norm_gain, g_attn_gain, g_mamba_gain, g_ffn_gain])
    gains = jnp.pad(gains, ((0, 0), (0, 2 * CHP - D))).reshape(8, CHP)
    table = jnp.concatenate(
        [
            jnp.stack(g_taps),
            g_conv_bias[None],
            g_dt_bias[None],
            g_skip[None],
            g_decay,
            jnp.zeros((1, CHP), F32),
            gains,
        ]
    )
    own = jnp.sum(lax.all_to_all(table, "ctx", 0, 0, tiled=True), axis=0, keepdims=True)
    a = lax.ppermute(own, "seq", RIGHT)
    b = lax.ppermute(own, "seq", LEFT)
    c = lax.ppermute(own, "seq", [(i, (i + 2) % NX) for i in range(NX)])
    whole = own + a + b + c
    shared = index >= 24
    four = jnp.concatenate([jnp.where(shared, whole, p) for p in in_order([own, b, c, a], x)])
    spread_rows = jnp.broadcast_to(four[None], (NC, NX, CHP))
    every = lax.all_to_all(spread_rows, "ctx", 0, 0, tiled=True)
    by_rows = every[:24, :, :CH].reshape(24, DI)
    gains = every[24:, 0].reshape(4, 2 * CHP)[:, :D]

    return (
        output,
        tokens_grad,
        gains[0],
        sequences_sum(qkv_sum.astype(BF16), QKV),
        sequences_sum(branch_sum[:ROWS_P, :AO_P], D),
        all_columns(in_sum[:, : 2 * CHP], CH),
        by_rows[:4],
        by_rows[4],
        g_xproj_w,
        g_dt_w,
        by_rows[5],
        by_rows[7:23].T,
        by_rows[6],
        all_rows(branch_sum[:CSUB, AO_P : AO_P + D]),
        gains[1],
        gains[2],
        gains[3],
        all_columns(ffn_sum[:ROWS_P, : 2 * FFP], FFX),
        all_rows(ffn_sum[:FSUB, 2 * FFP : 2 * FFP + D]),
    )


def solution(mesh):
    whole = P()
    ctx = P("ctx", None)
    both = P(("seq", "ctx"), None)
    return jax.shard_map(
        body,
        mesh=mesh,
        in_specs=(
            both, whole, ctx, ctx, ctx, whole, whole, ctx, ctx, whole, whole, whole,
            ctx, whole, whole, whole, ctx, ctx, both,
        ),
        out_specs=(
            both, both, whole, ctx, ctx, ctx, whole, whole, ctx, ctx, whole, whole,
            whole, ctx, whole, whole, whole, ctx, ctx,
        ),
        check_vma=False,
    )
```

```python
import functools

import jax
import jax.numpy as jnp
from jax import lax
from jax.experimental import pallas as pl
from jax.experimental.pallas import tpu as pltpu
from jax.sharding import PartitionSpec as P

D = 1600
HEADS = 25
KV_HEADS = 5
GROUP = HEADS // KV_HEADS
HEAD_DIM = 64
DI = 3200
N_STATE = 16
CONV = 4
DT_RANK = 100
FF = 5504
WINDOW = 1024
EPS = 1e-05
NEG_BIG = -1e30
LOG2E = 1.4426950408889634
LN2 = 0.6931471805599453

NX = 4
NC = 32
T = 128
KEYS = WINDOW + T
ROWS = 50
ROWS_P = 56
ROWS_64 = 64
DP = NC * ROWS_P
CH = DI // NX
CHP = 896
FFX = FF // NX
FFP = 1408
CSUB = CH // NC
FSUB = FFX // NC
QKV = 2240
QKV_P = 2304
AO_P = 1664
XD = 256

F32 = jnp.float32
BF16 = jnp.bfloat16
VMEM_LIMIT = 60 * 1024 * 1024


def dot(a, b, ca, cb, out=F32):
    return lax.dot_general(a, b, (((ca,), (cb,)), ((), ())), preferred_element_type=F32).astype(out)


def norm_scale(values, gain):
    return values * lax.rsqrt(jnp.mean(values * values, axis=-1, keepdims=True) + EPS) * gain


RIGHT = [(i, (i + 1) % NX) for i in range(NX)]
LEFT = [(i, (i - 1) % NX) for i in range(NX)]


def gather_x_near(v):
    return v, lax.ppermute(v, "seq", LEFT), lax.ppermute(v, "seq", RIGHT)


def gather_x_far(v, after, before):
    half = v.shape[0] // 2
    far_a = lax.ppermute(before[:half], "seq", RIGHT)
    far_b = lax.ppermute(after[half:], "seq", LEFT)
    return [v, after, jnp.concatenate([far_a, far_b]), before]


def gather_x(v):
    return gather_x_far(*gather_x_near(v))


def spread_x(v):
    far = lax.ppermute(v, "seq", [(i, (i + 2) % NX) for i in range(NX)])
    return [v, lax.ppermute(v, "seq", LEFT), far, lax.ppermute(v, "seq", RIGHT)]


def scatter_x_far(parts):
    half = parts[0].shape[0] // 2
    from_left = lax.ppermute(parts[2][:half], "seq", RIGHT)
    from_right = lax.ppermute(parts[2][half:], "seq", LEFT)
    to_right = jnp.concatenate(
        [(parts[1][:half].astype(F32) + from_left.astype(F32)).astype(BF16), parts[1][half:]]
    )
    to_left = jnp.concatenate(
        [parts[3][:half], (parts[3][half:].astype(F32) + from_right.astype(F32)).astype(BF16)]
    )
    return parts[0], to_right, to_left


def scatter_x_near(own, to_right, to_left):
    a = lax.ppermute(to_right, "seq", RIGHT)
    b = lax.ppermute(to_left, "seq", LEFT)
    return own.astype(F32) + a.astype(F32) + b.astype(F32)


def scatter_x(parts):
    return scatter_x_near(*scatter_x_far(parts))


def total_x(v):
    blocks = [v[:, k * T : (k + 1) * T] for k in range(NX)]

    def turned(by):
        return jnp.concatenate([blocks[(k + by) % NX] for k in range(NX)], axis=1)

    a = lax.ppermute(turned(1), "seq", RIGHT)
    b = lax.ppermute(turned(-1), "seq", LEFT)
    c = lax.ppermute(turned(2), "seq", [(i, (i + 2) % NX) for i in range(NX)])
    return v.astype(F32) + a.astype(F32) + b.astype(F32) + c.astype(F32)


def in_order(pieces, place):
    out = []
    for j in range(NX):
        value = pieces[0]
        for k in range(1, NX):
            value = jnp.where(place == (j - k) % NX, pieces[k], value)
        out.append(value)
    return out


def place_index(x, z, y, c):
    return x * NC + z * 8 + y * 2 + c


TURN = [
    (place_index(x, z, y, c), place_index(z, y, 2 * c + x // 2, x % 2))
    for x in range(4)
    for z in range(4)
    for y in range(4)
    for c in range(2)
]
TURN_BACK = [(b, a) for a, b in TURN]


def shift_ctx(v, by):
    return lax.ppermute(v, "ctx", [(i, i + by) for i in range(NC) if 0 <= i + by < NC])


def tie(*values):
    return lax.optimization_barrier(values)


SWAP = [(i, i ^ 1) for i in range(NC)]


def carried(state, steps, rate2, index, reverse, beside):
    sign = -1 if reverse else 1

    def after(first, then):
        return (then[0] + jnp.exp2(rate2[None] * then[1]) * first[0], first[1] + then[1])

    def keep(flag, part):
        return tuple(jnp.where(flag, v, 0.0) for v in part)

    def send(part, pairs):
        flat = jnp.concatenate([part[0].reshape(NX * N_STATE, CHP), part[1].reshape(NX, CHP)])
        flat = lax.ppermute(flat.astype(BF16), "ctx", pairs).astype(F32)
        return (flat[: NX * N_STATE].reshape(NX, N_STATE, CHP), flat[NX * N_STATE :].reshape(NX, 1, CHP))

    part = (state, steps)
    core = index % 2
    y = (index // 2) % 4
    if reverse:
        core, y = 1 - core, 3 - y
    other = send(part, SWAP)
    inside = keep(core == 1, other)
    chip = tuple(jnp.where(core == 1, a, b) for a, b in zip(after(other, part), after(part, other)))
    *chip, beside = tie(*chip, beside)
    rows = []
    for k in range(1, 4):
        rows.append(send(chip, [(i, i // 8 * 8 + (i + sign * 2 * k) % 8) for i in range(NC)]))
    pre = [keep(y >= k, rows[k - 1]) for k in range(1, 4)]
    suc = [keep(y < k, rows[k - 1]) for k in range(1, 4)]
    row_pre = after(after(pre[2], pre[1]), pre[0])
    row = after(after(after(after(row_pre, chip), suc[2]), suc[1]), suc[0])
    planes = []
    for k in range(1, 4):
        by = sign * 8 * k
        planes.append(send(row, [(i, i + by) for i in range(NC) if 0 <= i + by < NC]))
    plane_pre = after(after(planes[2], planes[1]), planes[0])
    return after(after(plane_pre, row_pre), inside)[0], beside


def key_window_back(even, odd, core):
    other = lax.ppermute(odd, "ctx", SWAP)
    none = jnp.zeros((T, odd.shape[1]), BF16)
    mine = even.astype(F32) + jnp.where(
        core == 0, jnp.concatenate([none, other]), jnp.concatenate([other, none])
    ).astype(F32)
    total = mine[4 * T :]
    for k in range(1, 5):
        term = mine[(4 - k) * T : (5 - k) * T].astype(BF16)
        total = total + shift_ctx(term, -2 * k).astype(F32)
    return total


TILES = CHP // 128


def lanes(j):
    return slice(j * 128, (j + 1) * 128)


def spread(source, target):
    for t in range(T):
        target[t] = jnp.broadcast_to(source[:, t : t + 1], (N_STATE, 128))


CHUNK = 16
WIDE = CHUNK * N_STATE
SCAN_GROUPS = ((0, 1, 2, 3), (4, 5, 6))
ADJOINT_GROUPS = ((0, 1, 2), (3, 4), (5, 6))


def chunk_diagonal():
    column = lax.broadcasted_iota(jnp.int32, (T, WIDE), 1) // N_STATE
    return column == lax.broadcasted_iota(jnp.int32, (T, WIDE), 0) % CHUNK


def chunk_rows(coef):
    pick = lax.broadcasted_iota(jnp.int32, (N_STATE, WIDE), 1) % N_STATE
    pick = (pick == lax.broadcasted_iota(jnp.int32, (N_STATE, WIDE), 0)).astype(BF16)
    wide = dot(coef.astype(BF16), pick, 0, 0)
    return jnp.where(chunk_diagonal(), wide, 0.0).astype(BF16)


def lane_sums(partial):
    flat = partial.reshape(T * N_STATE, 128).astype(BF16)
    wide = dot(flat, jnp.ones((128, 128), BF16), 1, 0).reshape(T, N_STATE, 128)
    token = lax.broadcasted_iota(jnp.int32, (T, N_STATE, 128), 0)
    lane = lax.broadcasted_iota(jnp.int32, (T, N_STATE, 128), 2)
    return jnp.sum(jnp.where(token == lane, wide, 0.0), axis=0)


def token_rows(chunk):
    return pl.ds(pl.multiple_of(chunk * CHUNK, CHUNK), CHUNK)


def state_rows(token):
    return pl.ds(pl.multiple_of(token * N_STATE, N_STATE), N_STATE)


def forward_scan(step, drive, spread_b, rate2, group, states, emit):
    rates = [rate2[:, lanes(j)] for j in group]

    def one(chunk, states):
        rows = token_rows(chunk)
        steps = [step[rows, lanes(j)] for j in group]
        drives = [drive[rows, lanes(j)] for j in group]
        states = list(states)
        for r in range(CHUNK):
            b_here = spread_b[chunk * CHUNK + r]
            for k, j in enumerate(group):
                a = jnp.exp2(steps[k][r : r + 1] * rates[k])
                states[k] = a * states[k] + drives[k][r : r + 1] * b_here
                emit(chunk * CHUNK + r, j, states[k])
        return tuple(states)

    return lax.fori_loop(0, T // CHUNK, one, tuple(states))


def chunks():
    return [(slice(c * CHUNK, (c + 1) * CHUNK), slice(c * WIDE, (c + 1) * WIDE)) for c in range(T // CHUNK)]


def scan_end_kernel(step, act, b_t, rate2, out, total, spread_b, drive):
    spread(b_t, spread_b)
    drive[...] = step[...] * act[...].astype(F32)
    for group in SCAN_GROUPS:
        zero = [jnp.zeros((N_STATE, 128), F32) for _ in group]
        states = forward_scan(step, drive, spread_b, rate2, group, zero, lambda t, j, h: None)
        for k, j in enumerate(group):
            out[0, :, lanes(j)] = states[k]
    total[0] = jnp.sum(step[...], axis=0, keepdims=True)


def scan_kernel(
    step, act, gate_z, b_t, c_t, start, rate2, skip, states_out, scan_out, gated, spread_b, drive, sum_c
):
    spread(b_t, spread_b)
    drive[...] = step[...] * act[...].astype(F32)
    sum_c[...] = chunk_rows(c_t[...])

    def emit(t, j, h):
        states_out[0, state_rows(t), lanes(j)] = h.astype(BF16)

    for group in SCAN_GROUPS:
        forward_scan(step, drive, spread_b, rate2, group, [start[0, :, lanes(j)] for j in group], emit)
    for rows, wide in chunks():
        y = dot(sum_c[rows, :], states_out[0, wide, :], 1, 0) + skip[...] * act[rows, :].astype(F32)
        scan_out[rows, :] = y
        z = gate_z[rows, :]
        gated[rows, :] = (y * (z * jax.nn.sigmoid(z))).astype(BF16)


def adjoint_end_kernel(step, g_scan, c_t, rate2, out, spread_c):
    spread(c_t, spread_c)
    for group in SCAN_GROUPS:
        rates = [rate2[:, lanes(j)] for j in group]

        def one(lap, adjoints):
            chunk = T // CHUNK - 1 - lap
            rows = token_rows(chunk)
            steps = [step[rows, lanes(j)] for j in group]
            grads = [g_scan[rows, lanes(j)] for j in group]
            adjoints = list(adjoints)
            for r in reversed(range(CHUNK)):
                c_here = spread_c[chunk * CHUNK + r]
                for k in range(len(group)):
                    a = jnp.exp2(steps[k][r : r + 1] * rates[k])
                    adjoints[k] = a * (grads[k][r : r + 1] * c_here + adjoints[k])
            return tuple(adjoints)

        zero = tuple(jnp.zeros((N_STATE, 128), F32) for _ in group)
        adjoints = lax.fori_loop(0, T // CHUNK, one, zero)
        for k, j in enumerate(group):
            out[0, :, lanes(j)] = adjoints[k]


def adjoint_kernel(
    step, act, g_scan, b_t, c_t, states, start, later, rate2, skip,
    g_step, g_act, g_rate, g_b, g_c, spread_c, drive, sum_b, adjoint, flow_rate, part_b, part_c,
):
    spread(c_t, spread_c)
    drive[...] = step[...] * act[...].astype(F32)
    sum_b[...] = chunk_rows(b_t[...])
    ones = chunk_diagonal()[:CHUNK].astype(BF16)
    for group in ADJOINT_GROUPS:
        rates = [rate2[:, lanes(j)] for j in group]

        def one(lap, carry):
            chunk = T // CHUNK - 1 - lap
            rows = token_rows(chunk)
            steps = [step[rows, lanes(j)] for j in group]
            grads = [g_scan[rows, lanes(j)] for j in group]
            drives = [drive[rows, lanes(j)] for j in group]
            adjoints, totals = list(carry[0]), list(carry[1])
            last = chunk * CHUNK + CHUNK - 1
            held = [states[0, state_rows(last), lanes(j)].astype(F32) for j in group]
            for r in reversed(range(CHUNK)):
                t = chunk * CHUNK + r
                here = state_rows(t)
                c_here = spread_c[t]
                b_sum = c_sum = None
                for k, j in enumerate(group):
                    g_row = grads[k][r : r + 1]
                    lam = g_row * c_here + adjoints[k]
                    adjoint[here, lanes(j)] = lam.astype(BF16)
                    step_row = steps[k][r : r + 1]
                    m = jnp.exp2(step_row * rates[k]) * lam
                    b_term = lam * drives[k][r : r + 1]
                    c_term = held[k] * g_row
                    b_sum = b_term if b_sum is None else b_sum + b_term
                    c_sum = c_term if c_sum is None else c_sum + c_term
                    before = states[0, state_rows(jnp.maximum(t - 1, 0)), lanes(j)].astype(F32)
                    if r == 0:
                        before = jnp.where(chunk == 0, start[0, :, lanes(j)], before)
                    flow = m * before
                    totals[k] = totals[k] + flow * step_row
                    flow_rate[here, lanes(j)] = (flow * rates[k]).astype(BF16)
                    adjoints[k] = m
                    held[k] = before
                if group[0] == 0:
                    part_b[t] = b_sum
                    part_c[t] = c_sum
                else:
                    part_b[t] += b_sum
                    part_c[t] += c_sum
            return (tuple(adjoints), tuple(totals))

        zero = tuple(jnp.zeros((N_STATE, 128), F32) for _ in group)
        first = tuple(later[0, :, lanes(j)] for j in group)
        _, totals = lax.fori_loop(0, T // CHUNK, one, (first, zero))
        for k, j in enumerate(group):
            g_rate[0, :, lanes(j)] = totals[k]
    for rows, wide in chunks():
        lam_b = dot(sum_b[rows, :], adjoint[wide, :], 1, 0)
        flow_sum = dot(ones, flow_rate[wide, :], 1, 0)
        g_step[rows, :] = flow_sum * LN2 + act[rows, :].astype(F32) * lam_b
        g_act[rows, :] = step[rows, :] * lam_b + skip[...] * g_scan[rows, :]
    g_b[...] = lane_sums(part_b[...])
    g_c[...] = lane_sums(part_c[...])


def seq_call(kernel, ins, outs, scratch, cost):
    def spec(shape, kind):
        if kind == "rows":
            return pl.BlockSpec((shape[0] // NX,) + tuple(shape[1:]), lambda s: (s, 0))
        if kind == "lanes":
            return pl.BlockSpec((shape[0], shape[1] // NX), lambda s: (0, s))
        if kind == "lead":
            return pl.BlockSpec((1,) + tuple(shape[1:]), lambda s: (s, 0, 0))
        return pl.BlockSpec(tuple(shape), lambda s: (0,) * len(shape))

    return pl.pallas_call(
        kernel,
        grid=(NX,),
        in_specs=[spec(a.shape, kind) for a, kind in ins],
        out_specs=[spec(shape, kind) for shape, _, kind in outs],
        out_shape=[jax.ShapeDtypeStruct(shape, dtype) for shape, dtype, _ in outs],
        scratch_shapes=scratch,
        compiler_params=pltpu.CompilerParams(vmem_limit_bytes=VMEM_LIMIT),
        cost_estimate=cost,
    )(*[a for a, _ in ins])


def cost(us):
    return pl.CostEstimate(flops=int(us * 1e9), bytes_accessed=int(us * 1e6), transcendentals=0)


def visible_keys(lowest):
    t = lax.broadcasted_iota(jnp.int32, (T, KEYS), 0)
    s = lax.broadcasted_iota(jnp.int32, (T, KEYS), 1)
    return (s > t) & (s <= t + WINDOW) & (s >= lowest)


def head_lanes(h, base=0):
    return slice(base + h * HEAD_DIM, base + (h + 1) * HEAD_DIM)


def stage(core, projected, mine, other, q_s, k_s, v_s):
    for block in range(9):
        rows = slice(block * T, (block + 1) * T)
        half = block // 2
        source = mine if block % 2 == 0 else other
        start = half * T if block % 2 == 0 else pl.multiple_of((half + core) * T, T)
        for n in range(KV_HEADS):
            k_s[n, rows, :] = source[pl.ds(start, T), head_lanes(n)]
            v_s[n, rows, :] = source[pl.ds(start, T), head_lanes(n, KV_HEADS * HEAD_DIM)]
    for n in range(KV_HEADS):
        for g in range(GROUP):
            q = projected[:, head_lanes(n * GROUP + g)].astype(F32) * HEAD_DIM ** (-0.5)
            q_s[n, g * T : (g + 1) * T, :] = q.astype(BF16)


def attend_kernel(place, projected, mine, other, out, lse, q_s, k_s, v_s, o_s):
    seen = visible_keys(place[0])
    stage(place[1], projected, mine, other, q_s, k_s, v_s)

    @pl.loop(0, KV_HEADS)
    def _(n):
        for g in range(GROUP):
            rows = slice(g * T, (g + 1) * T)
            scores = jnp.where(seen, dot(q_s[n, rows, :], k_s[n], 1, 1), NEG_BIG)
            peak = jnp.max(scores, axis=-1, keepdims=True)
            raised = jnp.exp(scores - peak)
            mass = jnp.sum(raised, axis=-1, keepdims=True)
            probs = (raised / mass).astype(BF16)
            o_s[n, rows, :] = dot(probs, v_s[n], 1, 0, BF16)
            lse[n, rows, :] = peak + jnp.log(mass)

    for n in range(KV_HEADS):
        for g in range(GROUP):
            out[:, head_lanes(n * GROUP + g)] = o_s[n, g * T : (g + 1) * T, :]


def attend_back_kernel(place, projected, mine, other, g_out, lse, g_q, g_even, g_odd, q_s, k_s, v_s, g_s, gq_s, gk_s, gv_s):
    seen = visible_keys(place[0])
    stage(place[1], projected, mine, other, q_s, k_s, v_s)
    for n in range(KV_HEADS):
        for g in range(GROUP):
            g_s[n, g * T : (g + 1) * T, :] = g_out[:, head_lanes(n * GROUP + g)]

    @pl.loop(0, KV_HEADS)
    def _(n):
        for g in range(GROUP):
            rows = slice(g * T, (g + 1) * T)
            q_here = q_s[n, rows, :]
            g_here = g_s[n, rows, :]
            scores = jnp.where(seen, dot(q_here, k_s[n], 1, 1), NEG_BIG)
            probs = jnp.exp(scores - lse[n, rows, :])
            g_probs = dot(g_here, v_s[n], 1, 1)
            inner = jnp.sum(probs * g_probs, axis=-1, keepdims=True)
            g_scores = (probs * (g_probs - inner)).astype(BF16)
            gq_s[n, rows, :] = (dot(g_scores, k_s[n], 1, 0) * HEAD_DIM ** (-0.5)).astype(BF16)
            k_term = dot(g_scores, q_here, 0, 0)
            v_term = dot(probs.astype(BF16), g_here, 0, 0)
            if g == 0:
                gk_s[n] = k_term
                gv_s[n] = v_term
            else:
                gk_s[n] += k_term
                gv_s[n] += v_term

    for n in range(KV_HEADS):
        for block in range(9):
            rows = slice(block * T, (block + 1) * T)
            out = g_even if block % 2 == 0 else g_odd
            into = slice(block // 2 * T, (block // 2 + 1) * T)
            out[into, head_lanes(n)] = gk_s[n, rows, :].astype(BF16)
            out[into, head_lanes(n, KV_HEADS * HEAD_DIM)] = gv_s[n, rows, :].astype(BF16)
        for g in range(GROUP):
            g_q[:, head_lanes(n * GROUP + g)] = gq_s[n, g * T : (g + 1) * T, :]


def head_call(kernel, lowest, ins, outs, scratch, us):
    def spec(shape):
        return pl.BlockSpec(tuple(shape), lambda: (0,) * len(shape))

    return pl.pallas_call(
        kernel,
        in_specs=[pl.BlockSpec(memory_space=pltpu.SMEM)] + [spec(a.shape) for a in ins],
        out_specs=[spec(shape) for shape, _ in outs],
        out_shape=[jax.ShapeDtypeStruct(shape, dtype) for shape, dtype in outs],
        scratch_shapes=[pltpu.VMEM(shape, dtype) for shape, dtype in scratch],
        compiler_params=pltpu.CompilerParams(vmem_limit_bytes=VMEM_LIMIT),
        cost_estimate=cost(us),
    )(lowest, *ins)


Q_SHAPE = (KV_HEADS, GROUP * T, HEAD_DIM)
K_SHAPE = (KV_HEADS, KEYS, HEAD_DIM)


def pad_to(v, rows, columns):
    return jnp.pad(v, ((0, rows - v.shape[0]), (0, columns - v.shape[1])))


def products_kernel(count, rows_out, *refs):
    out = refs[2 * count]
    at = 0
    for k in range(count):
        turned = refs[2 * k][...].T
        other = refs[2 * k + 1]
        width = other.shape[1]
        for first in range(0, width, 512):
            size = min(512, width - first)
            product = dot(turned, other[:, first : first + size], 1, 0)
            if rows_out == ROWS_P:
                out[:, at + first : at + first + size] = product.astype(BF16)
                continue
            for d in range(NC // 2):
                rows = product[d * ROWS_P : (d + 1) * ROWS_P]
                rows = jnp.concatenate([rows, jnp.zeros((rows_out - ROWS_P, size), F32)])
                out[d * rows_out : (d + 1) * rows_out, at + first : at + first + size] = rows.astype(BF16)
        at += width


def products(pairs, us, rows_out=ROWS_64, spare=0):
    width = sum(b.shape[1] for _, b in pairs)
    specs = []
    for a, b in pairs:
        specs.append(pl.BlockSpec((a.shape[0], DP // 2), lambda i: (0, i)))
        specs.append(pl.BlockSpec(b.shape, lambda i: (0, 0)))
    return pl.pallas_call(
        functools.partial(products_kernel, len(pairs), rows_out),
        grid=(2,),
        in_specs=specs,
        out_specs=pl.BlockSpec((NC // 2 * rows_out, width), lambda i: (i, 0)),
        out_shape=jax.ShapeDtypeStruct((NC * rows_out, width + spare), BF16),
        compiler_params=pltpu.CompilerParams(vmem_limit_bytes=VMEM_LIMIT),
        cost_estimate=cost(us),
    )(*[v for pair in pairs for v in pair])


def product_into(held, a, b, us):
    width = b.shape[1]
    block = 384
    skip = (held.shape[1] - width) // block

    def kernel(a_ref, b_ref, _, out):
        products_kernel(1, ROWS_64, a_ref, b_ref, out)

    return pl.pallas_call(
        kernel,
        grid=(2, width // block),
        in_specs=[
            pl.BlockSpec((a.shape[0], DP // 2), lambda i, j: (0, i)),
            pl.BlockSpec((b.shape[0], block), lambda i, j: (0, j)),
            pl.BlockSpec(memory_space=pl.ANY),
        ],
        out_specs=pl.BlockSpec((NC // 2 * ROWS_64, block), lambda i, j: (i, j + skip)),
        out_shape=jax.ShapeDtypeStruct(held.shape, BF16),
        input_output_aliases={2: 0},
        compiler_params=pltpu.CompilerParams(vmem_limit_bytes=VMEM_LIMIT),
        cost_estimate=cost(us),
    )(a, b, held)


def rows_sum(v):
    return lax.psum_scatter(v, "ctx", scatter_dimension=0, tiled=True)


def ring_far(v, dim, place, plus, minus):
    parts = [lax.dynamic_index_in_dim(v, (place + k) % 4, dim, False) for k in range(4)]
    half = -(-v.shape[-1] // 256) * 128
    from_left = lax.ppermute(parts[2][..., :half], "ctx", plus)
    from_right = lax.ppermute(parts[2][..., half:], "ctx", minus)
    to_right = jnp.concatenate(
        [(parts[1][..., :half].astype(F32) + from_left.astype(F32)).astype(BF16), parts[1][..., half:]], axis=-1
    )
    to_left = jnp.concatenate(
        [parts[3][..., :half], (parts[3][..., half:].astype(F32) + from_right.astype(F32)).astype(BF16)], axis=-1
    )
    return parts[0], to_right, to_left


def ring_near(own, to_right, to_left, plus, minus):
    a = lax.ppermute(to_right, "ctx", plus)
    b = lax.ppermute(to_left, "ctx", minus)
    return own.astype(F32) + a.astype(F32) + b.astype(F32)


def ring_pairs(stride, by):
    return [(i, i + (((i // stride) % 4 + by) % 4 - (i // stride) % 4) * stride) for i in range(NC)]


def core_halves(terms, core):
    def half(which):
        return jnp.concatenate(
            [
                lax.dynamic_index_in_dim(v.reshape(NC // 2, 2, ROWS_P, v.shape[1]), which, 1, False)
                for v in terms
            ],
            axis=-1,
        )

    return half(1 - core), half(core)


def core_sum(theirs, mine):
    other = lax.ppermute(theirs, "ctx", SWAP)
    v = mine.astype(F32) + other.astype(F32)
    return v.reshape(4, 4, ROWS_P, v.shape[-1])


def body(
    tokens,
    norm_gain,
    qkv_weight,
    attn_out_weight,
    in_weight,
    conv_weight,
    conv_bias,
    xproj_weight,
    dt_weight,
    dt_bias,
    decay_log,
    skip_gain,
    mamba_out_weight,
    attn_gain,
    mamba_gain,
    ffn_gain,
    gate_up_weight,
    down_weight,
    cotangent,
):
    x = lax.axis_index("seq")
    index = lax.axis_index("ctx")

    def columns(v, first, count):
        return lax.dynamic_slice_in_dim(v, first, count, v.ndim - 1)

    def order(count, size, rows):
        place = lax.broadcasted_iota(jnp.int32, (size, DP), 1)
        source = place // ROWS_P * rows + place % ROWS_P
        hit = (source == lax.broadcasted_iota(jnp.int32, (size, DP), 0)) & (place % ROWS_P < rows)
        return lax.optimization_barrier((hit & (source < count)).astype(BF16))

    widen_m = order(D, D, ROWS)
    widen_channels = order(CH, CHP, CSUB)
    widen_hidden = order(FFX, FFP, FSUB)

    def widen(v, matrix=None):
        return dot(v, widen_m if matrix is None else matrix, 1, 0, BF16)

    narrow_m = lax.optimization_barrier(widen_m.T)

    def narrow(v, matrix=None):
        if matrix is None:
            return dot(v.astype(BF16), narrow_m, 1, 0)
        return dot(v.astype(BF16), matrix, 1, 1)

    by_channel = pad_to(jnp.concatenate([xproj_weight, dt_weight], axis=1), 2 * ROWS, XD)
    first = jnp.concatenate(
        [
            pad_to(columns(in_weight, x * CH, CH), ROWS_P, CHP),
            pad_to(columns(in_weight, DI + x * CH, CH), ROWS_P, CHP),
            pad_to(by_channel[:ROWS], ROWS_P, XD),
            pad_to(by_channel[ROWS:], ROWS_P, XD),
            pad_to(qkv_weight, ROWS_P, QKV_P),
        ],
        axis=1,
    )
    first = lax.all_gather(first, "ctx", axis=0, tiled=True)
    sub_mamba = lax.dynamic_slice_in_dim(mamba_out_weight, x * CSUB, CSUB, 0)
    sub_down = lax.dynamic_slice_in_dim(down_weight, x * FSUB, FSUB, 0)
    sub_wide = lax.ppermute(
        jnp.concatenate([pad_to(sub_down, 48, D), pad_to(sub_mamba, 32, D)]), ("seq", "ctx"), TURN
    )
    second = jnp.concatenate(
        [
            pad_to(attn_out_weight, ROWS_P, AO_P),
            pad_to(sub_wide[48 : 48 + CSUB], ROWS_P, AO_P),
        ],
        axis=1,
    )
    third = jnp.concatenate(
        [
            pad_to(columns(gate_up_weight, x * FFX, FFX), ROWS_P, FFP),
            pad_to(columns(gate_up_weight, FF + x * FFX, FFX), ROWS_P, FFP),
            pad_to(sub_wide[:FSUB], ROWS_P, AO_P),
        ],
        axis=1,
    )
    inputs = tokens.astype(F32)
    normed_f, norm1_pullback = jax.vjp(norm_scale, inputs, norm_gain)
    normed = widen(normed_f.astype(BF16))
    normed, second = tie(normed, second)
    second = lax.all_gather(second, "ctx", axis=0, tiled=True)
    normed_all = jnp.concatenate(gather_x(normed))
    cot_all = jnp.concatenate(gather_x(pad_to(cotangent, T, AO_P)))
    first, normed_all, cot_all, third, widen_m, narrow_m, widen_channels, widen_hidden = tie(
        first, normed_all, cot_all, third, widen_m, narrow_m, widen_channels, widen_hidden
    )
    third = lax.all_gather(third, "ctx", axis=0, tiled=True)
    w_in = first[:, : 2 * CHP]
    small = first[:, 2 * CHP : 2 * CHP + 2 * XD].reshape(NC, ROWS_P, 2 * XD)
    small = lax.dynamic_slice_in_dim(small, x * (NC // NX), NC // NX, 0)[:, :ROWS]
    small = jnp.stack([small[:, :, :XD], small[:, :, XD:]], axis=1).reshape(CH, XD)
    w_small = pad_to(small, CHP, XD)
    w_xproj = w_small[:, : DT_RANK + 2 * N_STATE]
    w_dt = w_small[:, DT_RANK + 2 * N_STATE : 2 * DT_RANK + 2 * N_STATE]
    w_qkv = first[:, 2 * CHP + 2 * XD :]
    w_attn = second[:, :AO_P]
    w_mamba = second[:, AO_P:]
    w_gate_up = third[:, : 2 * FFP]
    w_down = third[:, 2 * FFP :]

    def channel(v):
        part = columns(v, x * CH, CH)
        return jnp.pad(part, ((0, 0),) * (v.ndim - 1) + ((0, CHP - CH),))

    taps = channel(conv_weight)
    conv_b = channel(conv_bias)[None]
    dt_b = channel(dt_bias)[None]
    skip = channel(skip_gain)[None]
    decay_rate = -jnp.exp(channel(decay_log.T))
    rate2 = decay_rate * LOG2E


    in_proj = dot(normed_all, w_in, 1, 0)
    conv_in = in_proj[:, :CHP].reshape(NX, T, CHP)
    gate_z = in_proj[:, CHP:]
    tails = shift_ctx(conv_in[:, T - (CONV - 1) :].reshape(NX * (CONV - 1), CHP), 1)
    padded = jnp.concatenate([tails.reshape(NX, CONV - 1, CHP), conv_in], axis=1)
    conv_sum = conv_b[None]
    for j in range(CONV):
        conv_sum = conv_sum + taps[j] * padded[:, j : j + T]
    conv_sum = conv_sum.reshape(NX * T, CHP)
    act_f, conv_pullback = jax.vjp(jax.nn.silu, conv_sum)
    act = act_f.astype(BF16)
    xproj_t = dot(w_xproj, act, 0, 1, BF16)
    in_proj, normed_q = tie(in_proj, normed)
    projected = dot(normed_q, w_qkv, 1, 0, BF16)
    xproj_t, projected = tie(xproj_t, projected)
    xproj_t = total_x(xproj_t)
    kv_own = projected[:, D:QKV]
    core = index % 2
    kv_mine = jnp.concatenate([shift_ctx(kv_own, 2 * k) for k in (4, 3, 2, 1)] + [kv_own])
    dt_low_t = xproj_t[:DT_RANK].astype(BF16)
    b_t = xproj_t[DT_RANK : DT_RANK + N_STATE]
    c_t = xproj_t[DT_RANK + N_STATE :]
    pre = dot(dt_low_t, w_dt, 0, 1) + dt_b
    step = jax.nn.softplus(pre)
    scan_end, steps = seq_call(
        scan_end_kernel,
        [(step, "rows"), (act, "rows"), (b_t, "lanes"), (rate2, "all")],
        [((NX, N_STATE, CHP), F32, "lead"), ((NX, 1, CHP), F32, "lead")],
        [pltpu.VMEM((T, N_STATE, 128), F32), pltpu.VMEM((T, CHP), F32)],
        cost(8),
    )

    scan_end, kv_mine = tie(scan_end, kv_mine)
    kv_other = lax.ppermute(kv_mine, "ctx", SWAP)
    start, kv_other = carried(scan_end, steps, rate2, index, False, kv_other)
    place_here = jnp.stack([jnp.maximum(0, WINDOW - index * T), core]).astype(jnp.int32)
    attended, lse = head_call(
        attend_kernel,
        place_here,
        [projected, kv_mine, kv_other],
        [((T, D), BF16), ((KV_HEADS, GROUP * T, 1), F32)],
        [(Q_SHAPE, BF16), (K_SHAPE, BF16), (K_SHAPE, BF16), (Q_SHAPE, BF16)],
        15,
    )
    start, attended, lse = tie(start, attended, lse)
    attended = widen(attended)
    attn_branch = dot(attended, w_attn, 1, 0)[:, :D]

    states, scan_out, gated = seq_call(
        scan_kernel,
        [
            (step, "rows"),
            (act, "rows"),
            (gate_z, "rows"),
            (b_t, "lanes"),
            (c_t, "lanes"),
            (start, "lead"),
            (rate2, "all"),
            (skip, "all"),
        ],
        [
            ((NX, T * N_STATE, CHP), BF16, "lead"),
            ((NX * T, CHP), F32, "rows"),
            ((NX * T, CHP), BF16, "rows"),
        ],
        [
            pltpu.VMEM((T, N_STATE, 128), F32),
            pltpu.VMEM((T, CHP), F32),
            pltpu.VMEM((T, WIDE), BF16),
        ],
        cost(14),
    )
    gated = widen(gated, widen_channels)
    mamba_terms = dot(gated, w_mamba, 1, 0, BF16)

    mamba_branch = scatter_x([mamba_terms[k * T : (k + 1) * T] for k in range(NX)])[:, :D]

    def mixing(attn_part, mamba_part, gain_attn, gain_mamba):
        return 0.5 * (norm_scale(attn_part, gain_attn) + norm_scale(mamba_part, gain_mamba))

    mamba_branch, cot_all = tie(mamba_branch, cot_all)
    mixed, mix_pullback = jax.vjp(mixing, attn_branch, mamba_branch, attn_gain, mamba_gain)
    residual = inputs + mixed
    ffn_f, norm2_pullback = jax.vjp(norm_scale, residual, ffn_gain)
    ffn_near = gather_x_near(widen(ffn_f.astype(BF16)))
    (g_hidden,) = tie(dot(cot_all, w_down, 1, 1, BF16))
    g_hidden = narrow(g_hidden, widen_hidden)
    g_hidden, *ffn_near = tie(g_hidden, *ffn_near)
    ffn_all = jnp.concatenate(gather_x_far(*ffn_near))
    gate_up = dot(ffn_all, w_gate_up, 1, 0)

    def swiglu(gate, up):
        return jax.nn.silu(gate) * up

    hidden_f, swiglu_pullback = jax.vjp(swiglu, gate_up[:, :FFP], gate_up[:, FFP:])
    hidden_f = hidden_f.astype(BF16)
    g_gate, g_up = swiglu_pullback(g_hidden)
    g_gate_up = jnp.concatenate([g_gate.astype(BF16), g_up.astype(BF16)], axis=1)
    g_ffn_terms = dot(g_gate_up, w_gate_up, 1, 1, BF16)
    g_ffn_terms, hidden_f, g_gate_up, ffn_all = tie(g_ffn_terms, hidden_f, g_gate_up, ffn_all)
    hidden = widen(hidden_f, widen_hidden)
    ffn_term = products([(ffn_all, g_gate_up), (hidden, cot_all)], 14)
    g_ffn_sum = scatter_x([g_ffn_terms[k * T : (k + 1) * T] for k in range(NX)])
    g_ffn_sum, ffn_term, hidden = tie(g_ffn_sum, ffn_term, hidden)
    ffn_sum = rows_sum(ffn_term)
    (g_ffn_in,) = tie(narrow(g_ffn_sum))
    g_norm2, g_ffn_gain = norm2_pullback(g_ffn_in)
    g_residual = cotangent.astype(F32) + g_norm2
    g_attn_f, g_mamba_f, g_attn_gain, g_mamba_gain = mix_pullback(g_residual)
    g_attn = pad_to(g_attn_f.astype(BF16), T, AO_P)
    g_mamba_near = gather_x_near(pad_to(g_mamba_f.astype(BF16), T, AO_P))

    g_attended = narrow(dot(g_attn, w_attn, 1, 1, BF16)).astype(BF16)
    down_terms = dot(hidden, w_down, 1, 0, BF16)
    g_attended, *g_mamba_near = tie(g_attended, *g_mamba_near)
    g_mamba_all = jnp.concatenate(gather_x_far(*g_mamba_near))
    g_mamba_all, down_terms = tie(g_mamba_all, down_terms)
    (g_gated,) = tie(dot(g_mamba_all, w_mamba, 1, 1, BF16))
    (g_gated,) = tie(narrow(g_gated, widen_channels))
    silu_z, gate_pullback = jax.vjp(jax.nn.silu, gate_z)
    g_scan = g_gated * silu_z
    (g_gate_z,) = gate_pullback(g_gated * scan_out)
    g_skip = jnp.sum(g_scan * act.astype(F32), axis=0)
    (adjoint_end,) = seq_call(
        adjoint_end_kernel,
        [(step, "rows"), (g_scan, "rows"), (c_t, "lanes"), (rate2, "all")],
        [((NX, N_STATE, CHP), F32, "lead")],
        [pltpu.VMEM((T, N_STATE, 128), F32)],
        cost(8),
    )
    later, g_attended = carried(adjoint_end, steps, rate2, index, True, g_attended)

    g_queries, g_even, g_odd = head_call(
        attend_back_kernel,
        place_here,
        [projected, kv_mine, kv_other, g_attended, lse],
        [
            ((T, D), BF16),
            ((5 * T, 2 * KV_HEADS * HEAD_DIM), BF16),
            ((4 * T, 2 * KV_HEADS * HEAD_DIM), BF16),
        ],
        [
            (Q_SHAPE, BF16),
            (K_SHAPE, BF16),
            (K_SHAPE, BF16),
            (Q_SHAPE, BF16),
            (Q_SHAPE, BF16),
            (K_SHAPE, F32),
            (K_SHAPE, F32),
        ],
        22,
    )
    g_projected = jnp.concatenate([g_queries, key_window_back(g_even, g_odd, core).astype(BF16)], axis=1)
    g_projected = pad_to(g_projected, T, QKV_P)
    branch_term = products(
        [(attended, g_attn), (gated, g_mamba_all), (normed_all, g_gate_z.astype(BF16))],
        12,
        spare=QKV_P,
    )
    branch_term = product_into(branch_term, normed, g_projected, 4)
    later, branch_term, ffn_sum = tie(later, branch_term, ffn_sum)
    branch_sum = rows_sum(branch_term)

    gate_up_near = gather_x_near(ffn_sum[:ROWS_P, : 2 * FFP])

    g_step, g_act, g_rate, g_b, g_c = seq_call(
        adjoint_kernel,
        [
            (step, "rows"),
            (act, "rows"),
            (g_scan, "rows"),
            (b_t, "lanes"),
            (c_t, "lanes"),
            (states, "lead"),
            (start, "lead"),
            (later, "lead"),
            (rate2, "all"),
            (skip, "all"),
        ],
        [
            ((NX * T, CHP), F32, "rows"),
            ((NX * T, CHP), F32, "rows"),
            ((NX, N_STATE, CHP), F32, "lead"),
            ((N_STATE, NX * T), F32, "lanes"),
            ((N_STATE, NX * T), F32, "lanes"),
        ],
        [
            pltpu.VMEM((T, N_STATE, 128), F32),
            pltpu.VMEM((T, CHP), F32),
            pltpu.VMEM((T, WIDE), BF16),
            pltpu.VMEM((T * N_STATE, CHP), BF16),
            pltpu.VMEM((T * N_STATE, CHP), BF16),
            pltpu.VMEM((T, N_STATE, 128), F32),
            pltpu.VMEM((T, N_STATE, 128), F32),
        ],
        cost(25),
    )
    g_step, *gate_up_near = tie(g_step, *gate_up_near)
    g_decay = jnp.sum(g_rate, axis=0) * decay_rate
    g_pre_f = g_step * jax.nn.sigmoid(pre)
    g_dt_bias = jnp.sum(g_pre_f, axis=0)
    g_pre = g_pre_f.astype(BF16)
    dt_term = dot(g_pre, dt_low_t, 0, 1, BF16)
    g_xproj_t = jnp.concatenate([dot(w_dt, g_pre, 0, 1), g_b, g_c]).astype(BF16)
    g_xproj_t = total_x(g_xproj_t).astype(BF16)
    g_xproj_t, *gate_up = tie(g_xproj_t, *gather_x_far(*gate_up_near))
    xproj_term = dot(act, g_xproj_t, 0, 1, BF16)
    g_act = g_act + dot(g_xproj_t, w_xproj, 0, 1)
    (g_conv_sum,) = conv_pullback(g_act)
    g_conv_bias = jnp.sum(g_conv_sum, axis=0)
    g_conv_3 = g_conv_sum.reshape(NX, T, CHP)
    g_taps = [jnp.sum(g_conv_3 * padded[:, j : j + T], axis=(0, 1)) for j in range(CONV)]
    g_padded = jnp.zeros((NX, T + CONV - 1, CHP), F32)
    for j in range(CONV):
        g_padded = g_padded + jnp.pad(taps[j] * g_conv_3, ((0, 0), (j, CONV - 1 - j), (0, 0)))
    back = shift_ctx(g_padded[:, : CONV - 1].reshape(NX * (CONV - 1), CHP).astype(BF16), -1)
    back = back.astype(F32).reshape(NX, CONV - 1, CHP)
    g_conv_in = g_padded[:, CONV - 1 :] + jnp.pad(back, ((0, 0), (T - (CONV - 1), 0), (0, 0)))
    g_in_proj = jnp.concatenate(
        [g_conv_in.reshape(NX * T, CHP).astype(BF16), g_gate_z.astype(BF16)], axis=1
    )
    small_term = pad_to(jnp.concatenate([xproj_term[:CH], dt_term[:CH]], axis=1), CH, XD)
    small_term = jnp.pad(small_term.reshape(NC, CSUB, XD), ((0, 0), (0, ROWS_P - CSUB), (0, 0)))
    in_c_term = products([(normed_all, g_in_proj[:, :CHP])], 4, ROWS_P)
    theirs, mine = core_halves([in_c_term, small_term.reshape(DP, XD)], core)
    theirs, mine, g_in_proj, g_projected = tie(theirs, mine, g_in_proj, g_projected)
    in_half = core_sum(theirs, mine)
    g_normed_attn = dot(g_projected, w_qkv, 1, 1)
    g_normed_terms = dot(g_in_proj, w_in, 1, 1, BF16)
    g_norm_gain = jnp.sum(g_normed_terms.astype(F32) * normed_all.astype(F32), axis=0)
    g_norm_gain = g_norm_gain + jnp.sum(g_normed_attn * normed.astype(F32), axis=0)
    g_norm_gain = g_norm_gain.reshape(NC, ROWS_P)[:, :ROWS].reshape(D) / norm_gain
    gains = jnp.stack([g_norm_gain, g_attn_gain, g_mamba_gain, g_ffn_gain])
    gains = jnp.pad(gains, ((0, 0), (0, 2 * CHP - D))).reshape(8, CHP)
    table = jnp.concatenate(
        [
            jnp.stack(g_taps),
            g_conv_bias[None],
            g_dt_bias[None],
            g_skip[None],
            g_decay,
            jnp.zeros((1, CHP), F32),
            gains,
        ]
    )
    table = jnp.pad(table, ((0, 0), (0, 4 * XD - CHP))).reshape(NC // 2, 8, XD)
    table = jnp.pad(table, ((0, 0), (32, ROWS_P - 40), (CHP, 0))).reshape(4, 4, ROWS_P, CHP + XD)
    in_half = (in_half + table).astype(BF16)
    both = jnp.concatenate([g_normed_terms, down_terms], axis=1)
    in_half, both = tie(in_half, both)
    both = scatter_x_far([both[k * T : (k + 1) * T] for k in range(NX)])
    along_z = (ring_pairs(8, 1), ring_pairs(8, -1))
    along_y = (ring_pairs(2, 1), ring_pairs(2, -1))
    in_half = ring_far(in_half, 0, index // 8, *along_z)
    in_half, both = tie(in_half, both)
    in_half = ring_near(*in_half, *along_z).astype(BF16)
    both = scatter_x_near(*both)
    in_half, branch_sum = tie(in_half, branch_sum)
    branch = jnp.concatenate([branch_sum[:ROWS_P, :AO_P], branch_sum[:ROWS_P, 2 * AO_P :]], axis=1)
    branch = gather_x_near(branch)
    in_sum = ring_near(*ring_far(in_half, 0, (index // 2) % 4, *along_y), *along_y)
    table = jnp.broadcast_to(in_sum[None, 32:40, CHP:], (NC, 8, XD))
    in_sum = in_sum.astype(BF16)
    owned = jnp.concatenate(
        [
            ffn_sum[:48, 2 * FFP : 2 * FFP + AO_P],
            branch_sum[:32, AO_P : 2 * AO_P],
            pad_to(in_sum[:32, CHP:], 32, AO_P),
        ]
    )
    owned = lax.ppermute(owned, ("seq", "ctx"), TURN_BACK)
    in_parts = in_order(spread_x(in_sum[:, :CHP]), x)
    table = lax.all_to_all(table, "ctx", 0, 0, tiled=True)
    table = jnp.sum(table.reshape(NC // 2, 2, 2, 4 * XD), axis=1).reshape(NC, 4 * XD)
    last = gather_x(jnp.concatenate([owned, pad_to(table.astype(BF16), NC, AO_P)]))
    last = in_order(last, x)
    by_rows = jnp.concatenate([v[112:136, :CH] for v in last], axis=1).astype(F32)
    gains = sum(v[136:144, :CHP].astype(F32) for v in last).reshape(4, 2 * CHP)[:, :D]

    (g_normed,) = tie(narrow(both[:, :DP] + g_normed_attn))
    g_norm1, _ = norm1_pullback(g_normed)
    tokens_grad = g_residual + g_norm1
    output = (residual + both[:, DP : DP + D]).astype(BF16)

    def side_by_side(parts, width):
        halves = []
        size = parts[0].shape[1] // 2
        for first_column in range(0, 2 * size, size):
            halves += [p[:ROWS, first_column : first_column + width] for p in parts]
        return jnp.concatenate(halves, axis=1).astype(F32)

    branch = gather_x_far(*branch)
    attn_w = sum(v[:ROWS, :D].astype(F32) for v in branch)
    qkv_w = sum(v[:ROWS, AO_P + CHP : AO_P + CHP + QKV].astype(F32) for v in branch)
    down_w = jnp.concatenate([v[:FSUB, :D] for v in last]).astype(F32)
    mamba_w = jnp.concatenate([v[48 : 48 + CSUB, :D] for v in last]).astype(F32)
    small_rows = jnp.concatenate([v[80 : 80 + CSUB, :XD] for v in last]).astype(F32)
    in_z = in_order([v[:, AO_P : AO_P + CHP] for v in branch], x)
    in_w = jnp.concatenate(
        [v[:ROWS, :CH] for v in in_parts + in_z], axis=1
    ).astype(F32)
    g_xproj_w = small_rows[:, : DT_RANK + 2 * N_STATE]
    g_dt_w = small_rows[:, DT_RANK + 2 * N_STATE : 2 * DT_RANK + 2 * N_STATE]

    return (
        output,
        tokens_grad,
        gains[0],
        qkv_w,
        attn_w,
        in_w,
        by_rows[:4],
        by_rows[4],
        g_xproj_w,
        g_dt_w,
        by_rows[5],
        by_rows[7:23].T,
        by_rows[6],
        mamba_w,
        gains[1],
        gains[2],
        gains[3],
        side_by_side(in_order(gate_up, x), FFX),
        down_w,
    )


def solution(mesh):
    whole = P()
    ctx = P("ctx", None)
    both = P(("seq", "ctx"), None)
    return jax.shard_map(
        body,
        mesh=mesh,
        in_specs=(
            both, whole, ctx, ctx, ctx, whole, whole, ctx, ctx, whole, whole, whole,
            ctx, whole, whole, whole, ctx, ctx, both,
        ),
        out_specs=(
            both, both, whole, ctx, ctx, ctx, whole, whole, ctx, ctx, whole, whole,
            whole, ctx, whole, whole, whole, ctx, ctx,
        ),
        check_vma=False,
    )
```

```python
import functools

import jax
import jax.numpy as jnp
from jax import lax
from jax.experimental import pallas as pl
from jax.experimental.pallas import tpu as pltpu
from jax.sharding import PartitionSpec as P

D = 1600
HEADS = 25
KV_HEADS = 5
GROUP = HEADS // KV_HEADS
HEAD_DIM = 64
DI = 3200
N_STATE = 16
CONV = 4
DT_RANK = 100
FF = 5504
WINDOW = 1024
EPS = 1e-05
NEG_BIG = -1e30
LOG2E = 1.4426950408889634
LN2 = 0.6931471805599453

NX = 4
NC = 32
T = 128
KEYS = WINDOW + T
ROWS = 50
ROWS_P = 56
ROWS_64 = 64
DP = NC * ROWS_P
CH = DI // NX
CHP = 896
FFX = FF // NX
FFP = 1408
CSUB = CH // NC
FSUB = FFX // NC
QKV = 2240
QKV_P = 2304
AO_P = 1664
XD = 256

CTX = ("zy", "core")
SEQ_CTX = ("seq",) + CTX

F32 = jnp.float32
BF16 = jnp.bfloat16
VMEM_LIMIT = 60 * 1024 * 1024


def dot(a, b, ca, cb, out=F32):
    return lax.dot_general(a, b, (((ca,), (cb,)), ((), ())), preferred_element_type=F32).astype(out)


def norm_scale(values, gain):
    return values * lax.rsqrt(jnp.mean(values * values, axis=-1, keepdims=True) + EPS) * gain


RIGHT = [(i, (i + 1) % NX) for i in range(NX)]
LEFT = [(i, (i - 1) % NX) for i in range(NX)]


def gather_x_near(v):
    return v, lax.ppermute(v, "seq", LEFT), lax.ppermute(v, "seq", RIGHT)


def gather_x_far(v, after, before):
    half = v.shape[0] // 2
    far_a = lax.ppermute(before[:half], "seq", RIGHT)
    far_b = lax.ppermute(after[half:], "seq", LEFT)
    return [v, after, jnp.concatenate([far_a, far_b]), before]


def gather_x(v):
    return gather_x_far(*gather_x_near(v))


def spread_x(v):
    far = lax.ppermute(v, "seq", [(i, (i + 2) % NX) for i in range(NX)])
    return [v, lax.ppermute(v, "seq", LEFT), far, lax.ppermute(v, "seq", RIGHT)]


def total_x_pairs(v):
    half = -(-v.shape[1] // 256) * 128
    pairs = ([(0, 1), (1, 0), (2, 3), (3, 2)], [(0, 3), (3, 0), (1, 2), (2, 1)])
    out = []
    for part, order in ((v[:, :half], pairs), (v[:, half:], pairs[::-1])):
        for each in order:
            other = lax.ppermute(part, "seq", each)
            part = (part.astype(F32) + other.astype(F32)).astype(BF16)
        out.append(part)
    return jnp.concatenate(out, axis=1)


def scatter_x_far(parts):
    half = parts[0].shape[0] // 2
    from_left = lax.ppermute(parts[2][:half], "seq", RIGHT)
    from_right = lax.ppermute(parts[2][half:], "seq", LEFT)
    to_right = jnp.concatenate(
        [(parts[1][:half].astype(F32) + from_left.astype(F32)).astype(BF16), parts[1][half:]]
    )
    to_left = jnp.concatenate(
        [parts[3][:half], (parts[3][half:].astype(F32) + from_right.astype(F32)).astype(BF16)]
    )
    return parts[0], to_right, to_left


def scatter_x_near(own, to_right, to_left):
    a = lax.ppermute(to_right, "seq", RIGHT)
    b = lax.ppermute(to_left, "seq", LEFT)
    return own.astype(F32) + a.astype(F32) + b.astype(F32)


def scatter_x(parts):
    return scatter_x_near(*scatter_x_far(parts))


def total_x(v):
    blocks = [v[:, k * T : (k + 1) * T] for k in range(NX)]

    def turned(by):
        return jnp.concatenate([blocks[(k + by) % NX] for k in range(NX)], axis=1)

    a = lax.ppermute(turned(1), "seq", RIGHT)
    b = lax.ppermute(turned(-1), "seq", LEFT)
    c = lax.ppermute(turned(2), "seq", [(i, (i + 2) % NX) for i in range(NX)])
    return v.astype(F32) + a.astype(F32) + b.astype(F32) + c.astype(F32)


def in_order(pieces, place):
    out = []
    for j in range(NX):
        value = pieces[0]
        for k in range(1, NX):
            value = jnp.where(place == (j - k) % NX, pieces[k], value)
        out.append(value)
    return out


def place_index(x, z, y, c):
    return x * NC + z * 8 + y * 2 + c


TURN = [
    (place_index(x, z, y, c), place_index(z, y, 2 * c + x // 2, x % 2))
    for x in range(4)
    for z in range(4)
    for y in range(4)
    for c in range(2)
]
TURN_BACK = [(b, a) for a, b in TURN]


def shift_ctx(v, by):
    return lax.ppermute(v, CTX, [(i, i + by) for i in range(NC) if 0 <= i + by < NC])


def tie(*values):
    return lax.optimization_barrier(values)


SWAP = [(i, i ^ 1) for i in range(NC)]


def carried(state, steps, rate2, index, reverse, beside):
    sign = -1 if reverse else 1

    def after(first, then):
        return (then[0] + jnp.exp2(rate2[None] * then[1]) * first[0], first[1] + then[1])

    def keep(flag, part):
        return tuple(jnp.where(flag, v, 0.0) for v in part)

    def send(part, pairs):
        flat = jnp.concatenate([part[0].reshape(NX * N_STATE, CHP), part[1].reshape(NX, CHP)])
        flat = lax.ppermute(flat.astype(BF16), CTX, pairs).astype(F32)
        return (flat[: NX * N_STATE].reshape(NX, N_STATE, CHP), flat[NX * N_STATE :].reshape(NX, 1, CHP))

    part = (state, steps)
    core = index % 2
    y = (index // 2) % 4
    if reverse:
        core, y = 1 - core, 3 - y
    other = send(part, SWAP)
    inside = keep(core == 1, other)
    chip = tuple(jnp.where(core == 1, a, b) for a, b in zip(after(other, part), after(part, other)))
    *chip, beside = tie(*chip, beside)
    rows = []
    for k in range(1, 4):
        rows.append(send(chip, [(i, i // 8 * 8 + (i + sign * 2 * k) % 8) for i in range(NC)]))
    pre = [keep(y >= k, rows[k - 1]) for k in range(1, 4)]
    suc = [keep(y < k, rows[k - 1]) for k in range(1, 4)]
    row_pre = after(after(pre[2], pre[1]), pre[0])
    row = after(after(after(after(row_pre, chip), suc[2]), suc[1]), suc[0])
    planes = []
    for k in range(1, 4):
        by = sign * 8 * k
        planes.append(send(row, [(i, i + by) for i in range(NC) if 0 <= i + by < NC]))
    plane_pre = after(after(planes[2], planes[1]), planes[0])
    return after(after(plane_pre, row_pre), inside)[0], beside


def key_window_chip(even, odd, core):
    other = lax.ppermute(odd, CTX, SWAP)
    none = jnp.zeros((T, odd.shape[1]), BF16)
    mine = even.astype(F32) + jnp.where(
        core == 0, jnp.concatenate([none, other]), jnp.concatenate([other, none])
    ).astype(F32)
    return mine


def key_window_back(mine):
    total = mine[4 * T :]
    for k in range(1, 5):
        term = mine[(4 - k) * T : (5 - k) * T].astype(BF16)
        total = total + shift_ctx(term, -2 * k).astype(F32)
    return total


TILES = CHP // 128


def lanes(j):
    return slice(j * 128, (j + 1) * 128)


def spread(source, target):
    for t in range(T):
        target[t] = jnp.broadcast_to(source[:, t : t + 1], (N_STATE, 128))


CHUNK = 16
WIDE = CHUNK * N_STATE
SCAN_GROUPS = ((0, 1, 2, 3), (4, 5, 6))
ADJOINT_GROUPS = ((0, 1, 2), (3, 4), (5, 6))


def chunk_diagonal():
    column = lax.broadcasted_iota(jnp.int32, (T, WIDE), 1) // N_STATE
    return column == lax.broadcasted_iota(jnp.int32, (T, WIDE), 0) % CHUNK


def chunk_rows(coef):
    pick = lax.broadcasted_iota(jnp.int32, (N_STATE, WIDE), 1) % N_STATE
    pick = (pick == lax.broadcasted_iota(jnp.int32, (N_STATE, WIDE), 0)).astype(BF16)
    wide = dot(coef.astype(BF16), pick, 0, 0)
    return jnp.where(chunk_diagonal(), wide, 0.0).astype(BF16)


def lane_sums(partial):
    flat = partial.reshape(T * N_STATE, 128).astype(BF16)
    wide = dot(flat, jnp.ones((128, 128), BF16), 1, 0).reshape(T, N_STATE, 128)
    token = lax.broadcasted_iota(jnp.int32, (T, N_STATE, 128), 0)
    lane = lax.broadcasted_iota(jnp.int32, (T, N_STATE, 128), 2)
    return jnp.sum(jnp.where(token == lane, wide, 0.0), axis=0)


def token_rows(chunk):
    return pl.ds(pl.multiple_of(chunk * CHUNK, CHUNK), CHUNK)


def state_rows(token):
    return pl.ds(pl.multiple_of(token * N_STATE, N_STATE), N_STATE)


def forward_scan(step, drive, spread_b, rate2, group, states, emit):
    rates = [rate2[:, lanes(j)] for j in group]

    def one(chunk, states):
        rows = token_rows(chunk)
        steps = [step[rows, lanes(j)] for j in group]
        drives = [drive[rows, lanes(j)] for j in group]
        states = list(states)
        for r in range(CHUNK):
            b_here = spread_b[chunk * CHUNK + r]
            for k, j in enumerate(group):
                a = jnp.exp2(steps[k][r : r + 1] * rates[k])
                states[k] = a * states[k] + drives[k][r : r + 1] * b_here
                emit(chunk * CHUNK + r, j, states[k])
        return tuple(states)

    return lax.fori_loop(0, T // CHUNK, one, tuple(states))


def chunks():
    return [(slice(c * CHUNK, (c + 1) * CHUNK), slice(c * WIDE, (c + 1) * WIDE)) for c in range(T // CHUNK)]


def scan_end_kernel(step, act, b_t, rate2, out, total, spread_b, drive):
    spread(b_t, spread_b)
    drive[...] = step[...] * act[...].astype(F32)
    for group in SCAN_GROUPS:
        zero = [jnp.zeros((N_STATE, 128), F32) for _ in group]
        states = forward_scan(step, drive, spread_b, rate2, group, zero, lambda t, j, h: None)
        for k, j in enumerate(group):
            out[0, :, lanes(j)] = states[k]
    total[0] = jnp.sum(step[...], axis=0, keepdims=True)


def scan_kernel(
    step, act, gate_z, b_t, c_t, start, rate2, skip, states_out, scan_out, gated, spread_b, drive, sum_c
):
    spread(b_t, spread_b)
    drive[...] = step[...] * act[...].astype(F32)
    sum_c[...] = chunk_rows(c_t[...])

    def emit(t, j, h):
        states_out[0, state_rows(t), lanes(j)] = h.astype(BF16)

    for group in SCAN_GROUPS:
        forward_scan(step, drive, spread_b, rate2, group, [start[0, :, lanes(j)] for j in group], emit)
    for rows, wide in chunks():
        y = dot(sum_c[rows, :], states_out[0, wide, :], 1, 0) + skip[...] * act[rows, :].astype(F32)
        scan_out[rows, :] = y
        z = gate_z[rows, :]
        gated[rows, :] = (y * (z * jax.nn.sigmoid(z))).astype(BF16)


def adjoint_end_kernel(step, g_scan, c_t, rate2, out, spread_c):
    spread(c_t, spread_c)
    for group in SCAN_GROUPS:
        rates = [rate2[:, lanes(j)] for j in group]

        def one(lap, adjoints):
            chunk = T // CHUNK - 1 - lap
            rows = token_rows(chunk)
            steps = [step[rows, lanes(j)] for j in group]
            grads = [g_scan[rows, lanes(j)] for j in group]
            adjoints = list(adjoints)
            for r in reversed(range(CHUNK)):
                c_here = spread_c[chunk * CHUNK + r]
                for k in range(len(group)):
                    a = jnp.exp2(steps[k][r : r + 1] * rates[k])
                    adjoints[k] = a * (grads[k][r : r + 1] * c_here + adjoints[k])
            return tuple(adjoints)

        zero = tuple(jnp.zeros((N_STATE, 128), F32) for _ in group)
        adjoints = lax.fori_loop(0, T // CHUNK, one, zero)
        for k, j in enumerate(group):
            out[0, :, lanes(j)] = adjoints[k]


def adjoint_kernel(
    step, act, g_scan, b_t, c_t, states, start, later, rate2, skip,
    g_step, g_act, g_rate, g_b, g_c, spread_c, drive, sum_b, adjoint, flow_rate, part_b, part_c,
):
    spread(c_t, spread_c)
    drive[...] = step[...] * act[...].astype(F32)
    sum_b[...] = chunk_rows(b_t[...])
    ones = chunk_diagonal()[:CHUNK].astype(BF16)
    for group in ADJOINT_GROUPS:
        rates = [rate2[:, lanes(j)] for j in group]

        def one(lap, carry):
            chunk = T // CHUNK - 1 - lap
            rows = token_rows(chunk)
            steps = [step[rows, lanes(j)] for j in group]
            grads = [g_scan[rows, lanes(j)] for j in group]
            drives = [drive[rows, lanes(j)] for j in group]
            adjoints, totals = list(carry[0]), list(carry[1])
            last = chunk * CHUNK + CHUNK - 1
            held = [states[0, state_rows(last), lanes(j)].astype(F32) for j in group]
            for r in reversed(range(CHUNK)):
                t = chunk * CHUNK + r
                here = state_rows(t)
                c_here = spread_c[t]
                b_sum = c_sum = None
                for k, j in enumerate(group):
                    g_row = grads[k][r : r + 1]
                    lam = g_row * c_here + adjoints[k]
                    adjoint[here, lanes(j)] = lam.astype(BF16)
                    step_row = steps[k][r : r + 1]
                    m = jnp.exp2(step_row * rates[k]) * lam
                    b_term = lam * drives[k][r : r + 1]
                    c_term = held[k] * g_row
                    b_sum = b_term if b_sum is None else b_sum + b_term
                    c_sum = c_term if c_sum is None else c_sum + c_term
                    before = states[0, state_rows(jnp.maximum(t - 1, 0)), lanes(j)].astype(F32)
                    if r == 0:
                        before = jnp.where(chunk == 0, start[0, :, lanes(j)], before)
                    flow = m * before
                    totals[k] = totals[k] + flow * step_row
                    flow_rate[here, lanes(j)] = (flow * rates[k]).astype(BF16)
                    adjoints[k] = m
                    held[k] = before
                if group[0] == 0:
                    part_b[t] = b_sum
                    part_c[t] = c_sum
                else:
                    part_b[t] += b_sum
                    part_c[t] += c_sum
            return (tuple(adjoints), tuple(totals))

        zero = tuple(jnp.zeros((N_STATE, 128), F32) for _ in group)
        first = tuple(later[0, :, lanes(j)] for j in group)
        _, totals = lax.fori_loop(0, T // CHUNK, one, (first, zero))
        for k, j in enumerate(group):
            g_rate[0, :, lanes(j)] = totals[k]
    for rows, wide in chunks():
        lam_b = dot(sum_b[rows, :], adjoint[wide, :], 1, 0)
        flow_sum = dot(ones, flow_rate[wide, :], 1, 0)
        g_step[rows, :] = flow_sum * LN2 + act[rows, :].astype(F32) * lam_b
        g_act[rows, :] = step[rows, :] * lam_b + skip[...] * g_scan[rows, :]
    g_b[...] = lane_sums(part_b[...])
    g_c[...] = lane_sums(part_c[...])


def seq_call(kernel, ins, outs, scratch, cost):
    def spec(shape, kind):
        if kind == "rows":
            return pl.BlockSpec((shape[0] // NX,) + tuple(shape[1:]), lambda s: (s, 0))
        if kind == "lanes":
            return pl.BlockSpec((shape[0], shape[1] // NX), lambda s: (0, s))
        if kind == "lead":
            return pl.BlockSpec((1,) + tuple(shape[1:]), lambda s: (s, 0, 0))
        return pl.BlockSpec(tuple(shape), lambda s: (0,) * len(shape))

    return pl.pallas_call(
        kernel,
        grid=(NX,),
        in_specs=[spec(a.shape, kind) for a, kind in ins],
        out_specs=[spec(shape, kind) for shape, _, kind in outs],
        out_shape=[jax.ShapeDtypeStruct(shape, dtype) for shape, dtype, _ in outs],
        scratch_shapes=scratch,
        compiler_params=pltpu.CompilerParams(vmem_limit_bytes=VMEM_LIMIT),
        cost_estimate=cost,
    )(*[a for a, _ in ins])


def cost(us):
    return pl.CostEstimate(flops=int(us * 1e9), bytes_accessed=int(us * 1e6), transcendentals=0)


def visible_keys(lowest):
    t = lax.broadcasted_iota(jnp.int32, (T, KEYS), 0)
    s = lax.broadcasted_iota(jnp.int32, (T, KEYS), 1)
    return (s > t) & (s <= t + WINDOW) & (s >= lowest)


def head_lanes(h, base=0):
    return slice(base + h * HEAD_DIM, base + (h + 1) * HEAD_DIM)


def stage(core, projected, mine, other, q_s, k_s, v_s):
    for block in range(9):
        rows = slice(block * T, (block + 1) * T)
        half = block // 2
        source = mine if block % 2 == 0 else other
        start = half * T if block % 2 == 0 else pl.multiple_of((half + core) * T, T)
        for n in range(KV_HEADS):
            k_s[n, rows, :] = source[pl.ds(start, T), head_lanes(n)]
            v_s[n, rows, :] = source[pl.ds(start, T), head_lanes(n, KV_HEADS * HEAD_DIM)]
    for n in range(KV_HEADS):
        for g in range(GROUP):
            q = projected[:, head_lanes(n * GROUP + g)].astype(F32) * HEAD_DIM ** (-0.5)
            q_s[n, g * T : (g + 1) * T, :] = q.astype(BF16)


def attend_kernel(place, projected, mine, other, out, lse, q_s, k_s, v_s, o_s):
    seen = visible_keys(place[0])
    stage(place[1], projected, mine, other, q_s, k_s, v_s)

    @pl.loop(0, KV_HEADS)
    def _(n):
        for g in range(GROUP):
            rows = slice(g * T, (g + 1) * T)
            scores = jnp.where(seen, dot(q_s[n, rows, :], k_s[n], 1, 1), NEG_BIG)
            peak = jnp.max(scores, axis=-1, keepdims=True)
            raised = jnp.exp(scores - peak)
            mass = jnp.sum(raised, axis=-1, keepdims=True)
            probs = (raised / mass).astype(BF16)
            o_s[n, rows, :] = dot(probs, v_s[n], 1, 0, BF16)
            lse[n, rows, :] = peak + jnp.log(mass)

    for n in range(KV_HEADS):
        for g in range(GROUP):
            out[:, head_lanes(n * GROUP + g)] = o_s[n, g * T : (g + 1) * T, :]


def attend_back_kernel(place, projected, mine, other, g_out, lse, g_q, g_even, g_odd, q_s, k_s, v_s, g_s, gq_s, gk_s, gv_s):
    seen = visible_keys(place[0])
    stage(place[1], projected, mine, other, q_s, k_s, v_s)
    for n in range(KV_HEADS):
        for g in range(GROUP):
            g_s[n, g * T : (g + 1) * T, :] = g_out[:, head_lanes(n * GROUP + g)]

    @pl.loop(0, KV_HEADS)
    def _(n):
        for g in range(GROUP):
            rows = slice(g * T, (g + 1) * T)
            q_here = q_s[n, rows, :]
            g_here = g_s[n, rows, :]
            scores = jnp.where(seen, dot(q_here, k_s[n], 1, 1), NEG_BIG)
            probs = jnp.exp(scores - lse[n, rows, :])
            g_probs = dot(g_here, v_s[n], 1, 1)
            inner = jnp.sum(probs * g_probs, axis=-1, keepdims=True)
            g_scores = (probs * (g_probs - inner)).astype(BF16)
            gq_s[n, rows, :] = (dot(g_scores, k_s[n], 1, 0) * HEAD_DIM ** (-0.5)).astype(BF16)
            k_term = dot(g_scores, q_here, 0, 0)
            v_term = dot(probs.astype(BF16), g_here, 0, 0)
            if g == 0:
                gk_s[n] = k_term
                gv_s[n] = v_term
            else:
                gk_s[n] += k_term
                gv_s[n] += v_term

    for n in range(KV_HEADS):
        for block in range(9):
            rows = slice(block * T, (block + 1) * T)
            out = g_even if block % 2 == 0 else g_odd
            into = slice(block // 2 * T, (block // 2 + 1) * T)
            out[into, head_lanes(n)] = gk_s[n, rows, :].astype(BF16)
            out[into, head_lanes(n, KV_HEADS * HEAD_DIM)] = gv_s[n, rows, :].astype(BF16)
        for g in range(GROUP):
            g_q[:, head_lanes(n * GROUP + g)] = gq_s[n, g * T : (g + 1) * T, :]


def head_call(kernel, lowest, ins, outs, scratch, us):
    def spec(shape):
        return pl.BlockSpec(tuple(shape), lambda: (0,) * len(shape))

    return pl.pallas_call(
        kernel,
        in_specs=[pl.BlockSpec(memory_space=pltpu.SMEM)] + [spec(a.shape) for a in ins],
        out_specs=[spec(shape) for shape, _ in outs],
        out_shape=[jax.ShapeDtypeStruct(shape, dtype) for shape, dtype in outs],
        scratch_shapes=[pltpu.VMEM(shape, dtype) for shape, dtype in scratch],
        compiler_params=pltpu.CompilerParams(vmem_limit_bytes=VMEM_LIMIT),
        cost_estimate=cost(us),
    )(lowest, *ins)


Q_SHAPE = (KV_HEADS, GROUP * T, HEAD_DIM)
K_SHAPE = (KV_HEADS, KEYS, HEAD_DIM)


def pad_to(v, rows, columns):
    return jnp.pad(v, ((0, rows - v.shape[0]), (0, columns - v.shape[1])))


def products_kernel(count, rows_out, *refs):
    out = refs[2 * count]
    at = 0
    for k in range(count):
        turned = refs[2 * k][...].T
        other = refs[2 * k + 1]
        width = other.shape[1]
        for first in range(0, width, 512):
            size = min(512, width - first)
            product = dot(turned, other[:, first : first + size], 1, 0)
            if rows_out == ROWS_P:
                out[:, at + first : at + first + size] = product.astype(BF16)
                continue
            for d in range(NC // 2):
                rows = product[d * ROWS_P : (d + 1) * ROWS_P]
                rows = jnp.concatenate([rows, jnp.zeros((rows_out - ROWS_P, size), F32)])
                out[d * rows_out : (d + 1) * rows_out, at + first : at + first + size] = rows.astype(BF16)
        at += width


def products(pairs, us, rows_out=ROWS_64):
    width = sum(b.shape[1] for _, b in pairs)
    specs = []
    for a, b in pairs:
        specs.append(pl.BlockSpec((a.shape[0], DP // 2), lambda i: (0, i)))
        specs.append(pl.BlockSpec(b.shape, lambda i: (0, 0)))
    return pl.pallas_call(
        functools.partial(products_kernel, len(pairs), rows_out),
        grid=(2,),
        in_specs=specs,
        out_specs=pl.BlockSpec((NC // 2 * rows_out, width), lambda i: (i, 0)),
        out_shape=jax.ShapeDtypeStruct((NC * rows_out, width), BF16),
        compiler_params=pltpu.CompilerParams(vmem_limit_bytes=VMEM_LIMIT),
        cost_estimate=cost(us),
    )(*[v for pair in pairs for v in pair])


def half_products_kernel(places, parity, *refs):
    *ins, out, turned, rows = refs
    count = len(places)
    at = 0
    for k, (held, offset) in enumerate(places):
        a, b = ins[2 * k], ins[2 * k + 1]
        depth, width = b.shape
        turned[:, :depth] = a[...].astype(F32).T
        for pair in range(NC // 4):
            first = pl.multiple_of((2 * pair + parity[0]) * ROWS_P, 8)
            block = jnp.concatenate(
                [turned[pl.ds(first, ROWS_P), :depth], jnp.zeros((ROWS_64 - ROWS_P, depth), F32)]
            )
            rows[pair * ROWS_64 : (pair + 1) * ROWS_64, :depth] = block.astype(BF16)
        for first in range(0, width, 512):
            size = min(512, width - first)
            product = dot(rows[:, :depth], b[:, first : first + size], 1, 0)
            if held is not None:
                other = ins[2 * count + held]
                product = product + other[:, offset + first : offset + first + size].astype(F32)
            out[:, at + first : at + first + size] = product.astype(BF16)
        at += width


def half_products(pairs, parity, us, held=(), places=None):
    if places is None:
        places = ((None, 0),) * len(pairs)
    width = sum(b.shape[1] for _, b in pairs)
    block = NC // 4 * ROWS_64
    specs = [pl.BlockSpec(memory_space=pltpu.SMEM)]
    for a, b in pairs:
        specs.append(pl.BlockSpec((a.shape[0], DP // 2), lambda i: (0, i)))
        specs.append(pl.BlockSpec(b.shape, lambda i: (0, 0)))
    for v in held:
        specs.append(pl.BlockSpec((block, v.shape[1]), lambda i: (i, 0)))
    return pl.pallas_call(
        functools.partial(half_products_kernel, places),
        grid=(2,),
        in_specs=specs,
        out_specs=pl.BlockSpec((block, width), lambda i: (i, 0)),
        out_shape=jax.ShapeDtypeStruct((2 * block, width), BF16),
        scratch_shapes=[pltpu.VMEM((DP // 2, NX * T), F32), pltpu.VMEM((block, NX * T), BF16)],
        compiler_params=pltpu.CompilerParams(vmem_limit_bytes=VMEM_LIMIT),
        cost_estimate=cost(us),
    )(parity.astype(jnp.int32).reshape(1), *[v for pair in pairs for v in pair], *held)


def rows_sum(v):
    return lax.psum_scatter(v, CTX, scatter_dimension=0, tiled=True)


def ring_far(v, dim, place, plus, minus):
    parts = [lax.dynamic_index_in_dim(v, (place + k) % 4, dim, False) for k in range(4)]
    half = -(-v.shape[-1] // 256) * 128
    from_left = lax.ppermute(parts[2][..., :half], CTX, plus)
    from_right = lax.ppermute(parts[2][..., half:], CTX, minus)
    to_right = jnp.concatenate(
        [(parts[1][..., :half].astype(F32) + from_left.astype(F32)).astype(BF16), parts[1][..., half:]], axis=-1
    )
    to_left = jnp.concatenate(
        [parts[3][..., :half], (parts[3][..., half:].astype(F32) + from_right.astype(F32)).astype(BF16)], axis=-1
    )
    return parts[0], to_right, to_left


def ring_near(own, to_right, to_left, plus, minus):
    a = lax.ppermute(to_right, CTX, plus)
    b = lax.ppermute(to_left, CTX, minus)
    return own.astype(F32) + a.astype(F32) + b.astype(F32)


def ring_pairs(stride, by):
    return [(i, i + (((i // stride) % 4 + by) % 4 - (i // stride) % 4) * stride) for i in range(NC)]


def core_halves(terms, core):
    def half(which):
        return jnp.concatenate(
            [
                lax.dynamic_index_in_dim(v.reshape(NC // 2, 2, ROWS_P, v.shape[1]), which, 1, False)
                for v in terms
            ],
            axis=-1,
        )

    return half(1 - core), half(core)


def core_sum(theirs, mine):
    other = lax.ppermute(theirs, CTX, SWAP)
    v = mine.astype(F32) + other.astype(F32)
    return v.reshape(4, 4, ROWS_P, v.shape[-1])


def body(
    tokens,
    norm_gain,
    qkv_weight,
    attn_out_weight,
    in_weight,
    conv_weight,
    conv_bias,
    xproj_weight,
    dt_weight,
    dt_bias,
    decay_log,
    skip_gain,
    mamba_out_weight,
    attn_gain,
    mamba_gain,
    ffn_gain,
    gate_up_weight,
    down_weight,
    cotangent,
):
    x = lax.axis_index("seq")
    index = lax.axis_index(CTX)

    def columns(v, first, count):
        return lax.dynamic_slice_in_dim(v, first, count, v.ndim - 1)

    def order(count, size, rows):
        place = lax.broadcasted_iota(jnp.int32, (size, DP), 1)
        source = place // ROWS_P * rows + place % ROWS_P
        hit = (source == lax.broadcasted_iota(jnp.int32, (size, DP), 0)) & (place % ROWS_P < rows)
        return lax.optimization_barrier((hit & (source < count)).astype(BF16))

    widen_m = order(D, D, ROWS)
    widen_channels = order(CH, CHP, CSUB)
    widen_hidden = order(FFX, FFP, FSUB)

    def widen(v, matrix=None):
        return dot(v, widen_m if matrix is None else matrix, 1, 0, BF16)

    narrow_m = lax.optimization_barrier(jnp.pad(widen_m.T, ((0, 0), (0, AO_P - D))))

    def narrow(v, matrix=None):
        if matrix is None:
            return dot(v.astype(BF16), narrow_m, 1, 0)[:, :D]
        return dot(v.astype(BF16), matrix, 1, 1)

    by_channel = pad_to(jnp.concatenate([xproj_weight, dt_weight], axis=1), 2 * ROWS, XD)
    first = jnp.concatenate(
        [
            pad_to(columns(in_weight, x * CH, CH), ROWS_P, CHP),
            pad_to(columns(in_weight, DI + x * CH, CH), ROWS_P, CHP),
            pad_to(by_channel[:ROWS], ROWS_P, XD),
            pad_to(by_channel[ROWS:], ROWS_P, XD),
            pad_to(qkv_weight, ROWS_P, QKV_P),
        ],
        axis=1,
    )
    first = lax.all_gather(first, CTX, axis=0, tiled=True)
    sub_mamba = lax.dynamic_slice_in_dim(mamba_out_weight, x * CSUB, CSUB, 0)
    sub_down = lax.dynamic_slice_in_dim(down_weight, x * FSUB, FSUB, 0)
    sub_wide = lax.ppermute(
        jnp.concatenate([pad_to(sub_down, 48, D), pad_to(sub_mamba, 32, D)]), SEQ_CTX, TURN
    )
    second = jnp.concatenate(
        [
            pad_to(attn_out_weight, ROWS_P, AO_P),
            pad_to(sub_wide[48 : 48 + CSUB], ROWS_P, AO_P),
        ],
        axis=1,
    )
    third = jnp.concatenate(
        [
            pad_to(columns(gate_up_weight, x * FFX, FFX), ROWS_P, FFP),
            pad_to(columns(gate_up_weight, FF + x * FFX, FFX), ROWS_P, FFP),
            pad_to(sub_wide[:FSUB], ROWS_P, AO_P),
        ],
        axis=1,
    )
    inputs = tokens.astype(F32)
    normed_f, norm1_pullback = jax.vjp(norm_scale, inputs, norm_gain)
    normed = widen(normed_f.astype(BF16))
    normed, second = tie(normed, second)
    second = lax.all_gather(second, CTX, axis=0, tiled=True)
    normed_all = jnp.concatenate(gather_x(normed))
    def channel(v):
        part = columns(v, x * CH, CH)
        return jnp.pad(part, ((0, 0),) * (v.ndim - 1) + ((0, CHP - CH),))

    taps = channel(conv_weight)
    conv_b = channel(conv_bias)[None]
    dt_b = channel(dt_bias)[None]
    skip = channel(skip_gain)[None]
    decay_rate = -jnp.exp(channel(decay_log.T))
    rate2 = decay_rate * LOG2E

    cot_all = jnp.concatenate(gather_x(pad_to(cotangent, T, AO_P)))
    first, normed_all, cot_all, third, widen_m, narrow_m, widen_channels, widen_hidden, taps, conv_b, dt_b, skip, rate2 = tie(
        first, normed_all, cot_all, third, widen_m, narrow_m, widen_channels, widen_hidden, taps, conv_b, dt_b, skip, rate2
    )
    third = lax.all_gather(third, CTX, axis=0, tiled=True)
    w_in = first[:, : 2 * CHP]
    w_qkv = first[:, 2 * CHP + 2 * XD :]
    w_attn = second[:, :AO_P]
    w_mamba = second[:, AO_P:]
    w_gate_up = third[:, : 2 * FFP]
    w_down = third[:, 2 * FFP :]

    in_proj = dot(normed_all, w_in, 1, 0)
    in_proj, normed_q, first = tie(in_proj, normed, first)
    small = first[:, 2 * CHP : 2 * CHP + 2 * XD]
    small = small.reshape(NC, ROWS_P, 2 * XD)
    small = lax.dynamic_slice_in_dim(small, x * (NC // NX), NC // NX, 0)[:, :ROWS]
    small = jnp.stack([small[:, :, :XD], small[:, :, XD:]], axis=1).reshape(CH, XD)
    w_small = pad_to(small, CHP, XD)
    w_xproj = w_small[:, : DT_RANK + 2 * N_STATE]
    w_dt = w_small[:, DT_RANK + 2 * N_STATE : 2 * DT_RANK + 2 * N_STATE]
    conv_in = in_proj[:, :CHP].reshape(NX, T, CHP)
    gate_z = in_proj[:, CHP:]
    tails = shift_ctx(conv_in[:, T - (CONV - 1) :].reshape(NX * (CONV - 1), CHP), 1)
    padded = jnp.concatenate([tails.reshape(NX, CONV - 1, CHP), conv_in], axis=1)
    conv_sum = conv_b[None]
    for j in range(CONV):
        conv_sum = conv_sum + taps[j] * padded[:, j : j + T]
    conv_sum = conv_sum.reshape(NX * T, CHP)
    act_f, conv_pullback = jax.vjp(jax.nn.silu, conv_sum)
    act = act_f.astype(BF16)
    xproj_t = dot(w_xproj, act, 0, 1, BF16)
    projected = dot(normed_q, w_qkv, 1, 0, BF16)
    xproj_t, projected = tie(xproj_t, projected)
    xproj_t = total_x(xproj_t)
    kv_own = projected[:, D:QKV]
    core = index % 2
    kv_mine = jnp.concatenate([shift_ctx(kv_own, 2 * k) for k in (4, 3, 2, 1)] + [kv_own])
    dt_low_t = xproj_t[:DT_RANK].astype(BF16)
    b_t = xproj_t[DT_RANK : DT_RANK + N_STATE]
    c_t = xproj_t[DT_RANK + N_STATE :]
    pre = dot(dt_low_t, w_dt, 0, 1) + dt_b
    step = jax.nn.softplus(pre)
    scan_end, steps = seq_call(
        scan_end_kernel,
        [(step, "rows"), (act, "rows"), (b_t, "lanes"), (rate2, "all")],
        [((NX, N_STATE, CHP), F32, "lead"), ((NX, 1, CHP), F32, "lead")],
        [pltpu.VMEM((T, N_STATE, 128), F32), pltpu.VMEM((T, CHP), F32)],
        cost(8),
    )

    scan_end, kv_mine = tie(scan_end, kv_mine)
    kv_other = lax.ppermute(kv_mine, CTX, SWAP)
    start, kv_other = carried(scan_end, steps, rate2, index, False, kv_other)
    place_here = jnp.stack([jnp.maximum(0, WINDOW - index * T), core]).astype(jnp.int32)
    attended, lse = head_call(
        attend_kernel,
        place_here,
        [projected, kv_mine, kv_other],
        [((T, D), BF16), ((KV_HEADS, GROUP * T, 1), F32)],
        [(Q_SHAPE, BF16), (K_SHAPE, BF16), (K_SHAPE, BF16), (Q_SHAPE, BF16)],
        15,
    )
    start, attended, lse = tie(start, attended, lse)
    attended = widen(attended)
    attn_branch = dot(attended, w_attn, 1, 0)[:, :D]

    states, scan_out, gated = seq_call(
        scan_kernel,
        [
            (step, "rows"),
            (act, "rows"),
            (gate_z, "rows"),
            (b_t, "lanes"),
            (c_t, "lanes"),
            (start, "lead"),
            (rate2, "all"),
            (skip, "all"),
        ],
        [
            ((NX, T * N_STATE, CHP), BF16, "lead"),
            ((NX * T, CHP), F32, "rows"),
            ((NX * T, CHP), BF16, "rows"),
        ],
        [
            pltpu.VMEM((T, N_STATE, 128), F32),
            pltpu.VMEM((T, CHP), F32),
            pltpu.VMEM((T, WIDE), BF16),
        ],
        cost(14),
    )
    gated = widen(gated, widen_channels)
    mamba_terms = dot(gated, w_mamba, 1, 0, BF16)

    mamba_branch = scatter_x([mamba_terms[k * T : (k + 1) * T] for k in range(NX)])[:, :D]

    def mixing(attn_part, mamba_part, gain_attn, gain_mamba):
        return 0.5 * (norm_scale(attn_part, gain_attn) + norm_scale(mamba_part, gain_mamba))

    mamba_branch, cot_all = tie(mamba_branch, cot_all)
    mixed, mix_pullback = jax.vjp(mixing, attn_branch, mamba_branch, attn_gain, mamba_gain)
    residual = inputs + mixed
    ffn_f, norm2_pullback = jax.vjp(norm_scale, residual, ffn_gain)
    ffn_near = gather_x_near(widen(ffn_f.astype(BF16)))
    g_hidden = dot(cot_all, w_down, 1, 1, BF16)
    g_hidden, *ffn_near = tie(g_hidden, *ffn_near)
    g_hidden = narrow(g_hidden, widen_hidden)
    ffn_all, g_hidden = tie(jnp.concatenate(gather_x_far(*ffn_near)), g_hidden)
    gate_up = dot(ffn_all, w_gate_up, 1, 0)

    def swiglu(gate, up):
        return jax.nn.silu(gate) * up

    hidden_f, swiglu_pullback = jax.vjp(swiglu, gate_up[:, :FFP], gate_up[:, FFP:])
    hidden_f = hidden_f.astype(BF16)
    g_gate, g_up = swiglu_pullback(g_hidden)
    g_gate_up = jnp.concatenate([g_gate.astype(BF16), g_up.astype(BF16)], axis=1)
    g_ffn_terms = dot(g_gate_up, w_gate_up, 1, 1, BF16)
    g_ffn_terms, hidden_f, g_gate_up, ffn_all = tie(g_ffn_terms, hidden_f, g_gate_up, ffn_all)
    hidden = widen(hidden_f, widen_hidden)
    ffn_term = products([(ffn_all, g_gate_up), (hidden, cot_all)], 14)
    g_ffn_sum = scatter_x([g_ffn_terms[k * T : (k + 1) * T] for k in range(NX)])
    g_ffn_sum, ffn_term, hidden = tie(g_ffn_sum, ffn_term, hidden)
    ffn_sum = rows_sum(ffn_term)
    (g_ffn_in,) = tie(narrow(g_ffn_sum))
    g_norm2, g_ffn_gain = norm2_pullback(g_ffn_in)
    g_residual = cotangent.astype(F32) + g_norm2
    g_attn_f, g_mamba_f, g_attn_gain, g_mamba_gain = mix_pullback(g_residual)
    g_attn = pad_to(g_attn_f.astype(BF16), T, AO_P)
    g_mamba_near = gather_x_near(pad_to(g_mamba_f.astype(BF16), T, AO_P))

    (g_attended,) = tie(dot(g_attn, w_attn, 1, 1, BF16))
    g_attended = narrow(g_attended).astype(BF16)
    g_attended, *g_mamba_near = tie(g_attended, *g_mamba_near)
    g_mamba_all = jnp.concatenate(gather_x_far(*g_mamba_near))
    (g_gated,) = tie(dot(g_mamba_all, w_mamba, 1, 1, BF16))
    (g_gated,) = tie(narrow(g_gated, widen_channels))
    silu_z, gate_pullback = jax.vjp(jax.nn.silu, gate_z)
    g_scan = g_gated * silu_z
    (g_gate_z,) = gate_pullback(g_gated * scan_out)
    g_skip = jnp.sum(g_scan * act.astype(F32), axis=0)
    (adjoint_end,) = seq_call(
        adjoint_end_kernel,
        [(step, "rows"), (g_scan, "rows"), (c_t, "lanes"), (rate2, "all")],
        [((NX, N_STATE, CHP), F32, "lead")],
        [pltpu.VMEM((T, N_STATE, 128), F32)],
        cost(8),
    )
    later, g_attended = carried(adjoint_end, steps, rate2, index, True, g_attended)

    g_queries, g_even, g_odd = head_call(
        attend_back_kernel,
        place_here,
        [projected, kv_mine, kv_other, g_attended, lse],
        [
            ((T, D), BF16),
            ((5 * T, 2 * KV_HEADS * HEAD_DIM), BF16),
            ((4 * T, 2 * KV_HEADS * HEAD_DIM), BF16),
        ],
        [
            (Q_SHAPE, BF16),
            (K_SHAPE, BF16),
            (K_SHAPE, BF16),
            (Q_SHAPE, BF16),
            (Q_SHAPE, BF16),
            (K_SHAPE, F32),
            (K_SHAPE, F32),
        ],
        22,
    )
    kv_chip = key_window_chip(g_even, g_odd, core)
    branch_pairs = [
        (attended, g_attn),
        (gated, g_mamba_all),
        (normed_all, g_gate_z.astype(BF16)),
    ]
    theirs_1 = half_products(branch_pairs, 1 - core, 8)
    later, theirs_1, kv_chip = tie(later, theirs_1, kv_chip)
    other_1 = lax.ppermute(theirs_1, CTX, SWAP)
    g_kv_own = key_window_back(kv_chip)
    g_step, g_act, g_rate, g_b, g_c = seq_call(
        adjoint_kernel,
        [
            (step, "rows"),
            (act, "rows"),
            (g_scan, "rows"),
            (b_t, "lanes"),
            (c_t, "lanes"),
            (states, "lead"),
            (start, "lead"),
            (later, "lead"),
            (rate2, "all"),
            (skip, "all"),
        ],
        [
            ((NX * T, CHP), F32, "rows"),
            ((NX * T, CHP), F32, "rows"),
            ((NX, N_STATE, CHP), F32, "lead"),
            ((N_STATE, NX * T), F32, "lanes"),
            ((N_STATE, NX * T), F32, "lanes"),
        ],
        [
            pltpu.VMEM((T, N_STATE, 128), F32),
            pltpu.VMEM((T, CHP), F32),
            pltpu.VMEM((T, WIDE), BF16),
            pltpu.VMEM((T * N_STATE, CHP), BF16),
            pltpu.VMEM((T * N_STATE, CHP), BF16),
            pltpu.VMEM((T, N_STATE, 128), F32),
            pltpu.VMEM((T, N_STATE, 128), F32),
        ],
        cost(25),
    )
    g_step, other_1, g_kv_own, ffn_sum = tie(g_step, other_1, g_kv_own, ffn_sum)
    gate_up_near = gather_x_near(ffn_sum[:ROWS_P, : 2 * FFP])
    g_projected = pad_to(jnp.concatenate([g_queries, g_kv_own.astype(BF16)], axis=1), T, QKV_P)
    branch_pairs.append((normed, g_projected))
    other_2 = lax.ppermute(half_products(branch_pairs[3:], 1 - core, 3), CTX, SWAP)
    branch_pairs = [branch_pairs[0], branch_pairs[3], branch_pairs[1], branch_pairs[2]]
    branch_term = half_products(
        branch_pairs, core, 12, [other_1, other_2], ((0, 0), (1, 0), (0, AO_P), (0, 2 * AO_P))
    )
    g_decay = jnp.sum(g_rate, axis=0) * decay_rate
    g_pre_f = g_step * jax.nn.sigmoid(pre)
    g_dt_bias = jnp.sum(g_pre_f, axis=0)
    g_pre = g_pre_f.astype(BF16)
    dt_term = dot(g_pre, dt_low_t, 0, 1, BF16)
    g_xproj_t = jnp.concatenate([dot(w_dt, g_pre, 0, 1), g_b, g_c]).astype(BF16)
    g_xproj_t = total_x(g_xproj_t).astype(BF16)
    g_xproj_t, branch_term, *gate_up_near = tie(g_xproj_t, branch_term, *gate_up_near)
    branch_sum = lax.psum_scatter(branch_term, "zy", scatter_dimension=0, tiled=True)
    xproj_term = dot(act, g_xproj_t, 0, 1, BF16)
    g_act = g_act + dot(g_xproj_t, w_xproj, 0, 1)
    (g_conv_sum,) = conv_pullback(g_act)
    g_conv_bias = jnp.sum(g_conv_sum, axis=0)
    g_conv_3 = g_conv_sum.reshape(NX, T, CHP)
    g_taps = [jnp.sum(g_conv_3 * padded[:, j : j + T], axis=(0, 1)) for j in range(CONV)]
    g_padded = jnp.zeros((NX, T + CONV - 1, CHP), F32)
    for j in range(CONV):
        g_padded = g_padded + jnp.pad(taps[j] * g_conv_3, ((0, 0), (j, CONV - 1 - j), (0, 0)))
    back = shift_ctx(g_padded[:, : CONV - 1].reshape(NX * (CONV - 1), CHP).astype(BF16), -1)
    back = back.astype(F32).reshape(NX, CONV - 1, CHP)
    g_conv_in = g_padded[:, CONV - 1 :] + jnp.pad(back, ((0, 0), (T - (CONV - 1), 0), (0, 0)))
    g_in_proj = jnp.concatenate(
        [g_conv_in.reshape(NX * T, CHP).astype(BF16), g_gate_z.astype(BF16)], axis=1
    )
    small_term = pad_to(jnp.concatenate([xproj_term[:CH], dt_term[:CH]], axis=1), CH, XD)
    small_term = jnp.pad(small_term.reshape(NC, CSUB, XD), ((0, 0), (0, ROWS_P - CSUB), (0, 0)))
    in_c_term = products([(normed_all, g_in_proj[:, :CHP])], 4, ROWS_P)
    theirs, mine = core_halves([in_c_term, small_term.reshape(DP, XD)], core)
    theirs, mine, hidden = tie(theirs, mine, hidden)
    down_terms = dot(hidden, w_down, 1, 0, BF16)
    in_half = core_sum(theirs, mine)
    gains = jnp.stack([jnp.zeros_like(g_attn_gain), g_attn_gain, g_mamba_gain, g_ffn_gain])
    gains = jnp.pad(gains, ((0, 0), (0, 2 * CHP - D))).reshape(8, CHP)
    table = jnp.concatenate(
        [
            jnp.stack(g_taps),
            g_conv_bias[None],
            g_dt_bias[None],
            g_skip[None],
            g_decay,
            jnp.zeros((1, CHP), F32),
            gains,
        ]
    )
    table = jnp.pad(table, ((0, 0), (0, 4 * XD - CHP))).reshape(NC // 2, 8, XD)
    table = jnp.pad(table, ((0, 0), (32, ROWS_P - 40), (CHP, 0))).reshape(4, 4, ROWS_P, CHP + XD)
    in_half = (in_half + table).astype(BF16)
    in_half, g_in_proj, g_projected, down_terms = tie(in_half, g_in_proj, g_projected, down_terms)
    g_normed_terms = dot(g_in_proj, w_in, 1, 1, BF16)
    both = jnp.concatenate([g_normed_terms, down_terms], axis=1)
    both = scatter_x_far([both[k * T : (k + 1) * T] for k in range(NX)])
    along_z = (ring_pairs(8, 1), ring_pairs(8, -1))
    along_y = (ring_pairs(2, 1), ring_pairs(2, -1))
    in_half = ring_far(in_half, 0, index // 8, *along_z)
    in_half, both = tie(in_half, both)
    both = scatter_x_near(*both)
    g_normed_attn = dot(g_projected, w_qkv, 1, 1)
    in_half, g_normed_attn, gate_up_near = tie(in_half, g_normed_attn, gate_up_near)
    gate_up = gather_x_far(*gate_up_near)
    in_half = ring_near(*in_half, *along_z).astype(BF16)
    in_half, both = tie(in_half, both)
    in_half = ring_far(in_half, 0, (index // 2) % 4, *along_y)
    (g_normed,) = tie(narrow(both[:, :DP] + g_normed_attn))
    g_norm1, g_norm_gain = norm1_pullback(g_normed)
    in_half, g_norm1, g_norm_gain = tie(in_half, g_norm1, g_norm_gain)
    tokens_grad = g_residual + g_norm1
    output = (residual + both[:, DP : DP + D]).astype(BF16)
    in_sum = ring_near(*in_half, *along_y)
    in_sum, branch_sum = tie(in_sum, branch_sum)
    branch = total_x_pairs(branch_sum[:ROWS_P, : AO_P + QKV_P])
    g_norm_gain = jnp.pad(g_norm_gain, (0, 8 * XD - D)).reshape(8, XD)
    table = jnp.concatenate([in_sum[32:40, CHP:], g_norm_gain])
    table = jnp.broadcast_to(table[None], (NC, 16, XD))
    in_sum = in_sum.astype(BF16)
    owned = jnp.concatenate(
        [
            ffn_sum[:48, 2 * FFP : 2 * FFP + AO_P],
            branch_sum[:32, AO_P + QKV_P : 2 * AO_P + QKV_P],
            pad_to(in_sum[:32, CHP:], 32, AO_P),
        ]
    )
    owned = lax.ppermute(owned, SEQ_CTX, TURN_BACK)
    in_both = jnp.concatenate([in_sum[:, :CHP], branch_sum[:ROWS_P, 2 * AO_P + QKV_P :]], axis=1)
    in_parts = in_order(spread_x(in_both), x)
    table = lax.all_to_all(table, CTX, 0, 0, tiled=True)
    g_norm_gain = jnp.sum(table[:, 8:], axis=0).reshape(2, 4 * XD)
    table = jnp.sum(table[:, :8].reshape(NC // 2, 2, 2, 4 * XD), axis=1).reshape(NC, 4 * XD)
    table = jnp.concatenate([table, jnp.pad(g_norm_gain, ((0, 14), (0, 0)))])
    last = in_order(gather_x(owned), x)
    tables = in_order(spread_x(table.astype(BF16)), x)
    by_rows = jnp.concatenate([v[:24, :CH] for v in tables], axis=1).astype(F32)
    gains = sum(v[24:32, :CHP].astype(F32) for v in tables).reshape(4, 2 * CHP)[:, :D]
    g_norm_gain = sum(v[32:34].astype(F32) for v in tables).reshape(8 * XD)[:D]

    def side_by_side(parts, width):
        halves = []
        size = parts[0].shape[1] // 2
        for first_column in range(0, 2 * size, size):
            halves += [p[:ROWS, first_column : first_column + width] for p in parts]
        return jnp.concatenate(halves, axis=1).astype(F32)

    branch = branch.astype(F32)
    attn_w = branch[:ROWS, :D]
    qkv_w = branch[:ROWS, AO_P : AO_P + QKV]
    down_w = jnp.concatenate([v[:FSUB, :D] for v in last]).astype(F32)
    mamba_w = jnp.concatenate([v[48 : 48 + CSUB, :D] for v in last]).astype(F32)
    small_rows = jnp.concatenate([v[80 : 80 + CSUB, :XD] for v in last]).astype(F32)
    in_w = jnp.concatenate(
        [v[:ROWS, :CH] for v in in_parts] + [v[:ROWS, CHP : CHP + CH] for v in in_parts], axis=1
    ).astype(F32)
    g_xproj_w = small_rows[:, : DT_RANK + 2 * N_STATE]
    g_dt_w = small_rows[:, DT_RANK + 2 * N_STATE : 2 * DT_RANK + 2 * N_STATE]

    return (
        output,
        tokens_grad,
        g_norm_gain,
        qkv_w,
        attn_w,
        in_w,
        by_rows[:4],
        by_rows[4],
        g_xproj_w,
        g_dt_w,
        by_rows[5],
        by_rows[7:23].T,
        by_rows[6],
        mamba_w,
        gains[1],
        gains[2],
        gains[3],
        side_by_side(in_order(gate_up, x), FFX),
        down_w,
    )


def solution(mesh):
    mesh = jax.sharding.Mesh(mesh.devices.reshape(NX, NC // 2, 2), SEQ_CTX)
    whole = P()
    ctx = P(CTX, None)
    both = P(SEQ_CTX, None)
    return jax.shard_map(
        body,
        mesh=mesh,
        in_specs=(
            both, whole, ctx, ctx, ctx, whole, whole, ctx, ctx, whole, whole, whole,
            ctx, whole, whole, whole, ctx, ctx, both,
        ),
        out_specs=(
            both, both, whole, ctx, ctx, ctx, whole, whole, ctx, ctx, whole, whole,
            whole, ctx, whole, whole, whole, ctx, ctx,
        ),
        check_vma=False,
    )
```

```python
import functools

import jax
import jax.numpy as jnp
from jax import lax
from jax.experimental import pallas as pl
from jax.experimental.pallas import tpu as pltpu
from jax.sharding import PartitionSpec as P

D = 1600
HEADS = 25
KV_HEADS = 5
GROUP = HEADS // KV_HEADS
HEAD_DIM = 64
DI = 3200
N_STATE = 16
CONV = 4
DT_RANK = 100
FF = 5504
WINDOW = 1024
EPS = 1e-05
NEG_BIG = -1e30
LOG2E = 1.4426950408889634
LN2 = 0.6931471805599453

NX = 4
NC = 32
T = 128
KEYS = WINDOW + T
ROWS = 50
ROWS_P = 56
ROWS_64 = 64
DP = NC * ROWS_P
CH = DI // NX
CHP = 896
FFX = FF // NX
FFP = 1408
CSUB = CH // NC
FSUB = FFX // NC
QKV = 2240
QKV_P = 2304
AO_P = 1664
XD = 256

CTX = ("zy", "core")
SEQ_CTX = ("seq",) + CTX

F32 = jnp.float32
BF16 = jnp.bfloat16
VMEM_LIMIT = 60 * 1024 * 1024


def dot(a, b, ca, cb, out=F32):
    return lax.dot_general(a, b, (((ca,), (cb,)), ((), ())), preferred_element_type=F32).astype(out)


def norm_scale(values, gain):
    return values * lax.rsqrt(jnp.mean(values * values, axis=-1, keepdims=True) + EPS) * gain


RIGHT = [(i, (i + 1) % NX) for i in range(NX)]
LEFT = [(i, (i - 1) % NX) for i in range(NX)]


def gather_x_near(v):
    return v, lax.ppermute(v, "seq", LEFT), lax.ppermute(v, "seq", RIGHT)


def gather_x_far(v, after, before):
    half = v.shape[0] // 2
    far_a = lax.ppermute(before[:half], "seq", RIGHT)
    far_b = lax.ppermute(after[half:], "seq", LEFT)
    return [v, after, jnp.concatenate([far_a, far_b]), before]


def gather_x(v):
    return gather_x_far(*gather_x_near(v))


def spread_x(v):
    far = lax.ppermute(v, "seq", [(i, (i + 2) % NX) for i in range(NX)])
    return [v, lax.ppermute(v, "seq", LEFT), far, lax.ppermute(v, "seq", RIGHT)]


def total_x_pairs(v):
    half = -(-v.shape[1] // 256) * 128
    pairs = ([(0, 1), (1, 0), (2, 3), (3, 2)], [(0, 3), (3, 0), (1, 2), (2, 1)])
    out = []
    for part, order in ((v[:, :half], pairs), (v[:, half:], pairs[::-1])):
        for each in order:
            other = lax.ppermute(part, "seq", each)
            part = (part.astype(F32) + other.astype(F32)).astype(BF16)
        out.append(part)
    return jnp.concatenate(out, axis=1)


def scatter_x_far(parts):
    half = parts[0].shape[0] // 2
    from_left = lax.ppermute(parts[2][:half], "seq", RIGHT)
    from_right = lax.ppermute(parts[2][half:], "seq", LEFT)
    to_right = jnp.concatenate(
        [(parts[1][:half].astype(F32) + from_left.astype(F32)).astype(BF16), parts[1][half:]]
    )
    to_left = jnp.concatenate(
        [parts[3][:half], (parts[3][half:].astype(F32) + from_right.astype(F32)).astype(BF16)]
    )
    return parts[0], to_right, to_left


def scatter_x_near(own, to_right, to_left):
    a = lax.ppermute(to_right, "seq", RIGHT)
    b = lax.ppermute(to_left, "seq", LEFT)
    return own.astype(F32) + a.astype(F32) + b.astype(F32)


def scatter_x(parts):
    return scatter_x_near(*scatter_x_far(parts))


def total_x(v):
    blocks = [v[:, k * T : (k + 1) * T] for k in range(NX)]

    def turned(by):
        return jnp.concatenate([blocks[(k + by) % NX] for k in range(NX)], axis=1)

    a = lax.ppermute(turned(1), "seq", RIGHT)
    b = lax.ppermute(turned(-1), "seq", LEFT)
    c = lax.ppermute(turned(2), "seq", [(i, (i + 2) % NX) for i in range(NX)])
    return v.astype(F32) + a.astype(F32) + b.astype(F32) + c.astype(F32)


def in_order(pieces, place):
    out = []
    for j in range(NX):
        value = pieces[0]
        for k in range(1, NX):
            value = jnp.where(place == (j - k) % NX, pieces[k], value)
        out.append(value)
    return out


def place_index(x, z, y, c):
    return x * NC + z * 8 + y * 2 + c


TURN = [
    (place_index(x, z, y, c), place_index(z, y, 2 * c + x // 2, x % 2))
    for x in range(4)
    for z in range(4)
    for y in range(4)
    for c in range(2)
]
TURN_BACK = [(b, a) for a, b in TURN]


def shift_ctx(v, by):
    return lax.ppermute(v, CTX, [(i, i + by) for i in range(NC) if 0 <= i + by < NC])


def tie(*values):
    return lax.optimization_barrier(values)


SWAP = [(i, i ^ 1) for i in range(NC)]


def carried(state, steps, rate2, index, reverse, beside):
    sign = -1 if reverse else 1

    def after(first, then):
        return (then[0] + jnp.exp2(rate2[None] * then[1]) * first[0], first[1] + then[1])

    def keep(flag, part):
        return tuple(jnp.where(flag, v, 0.0) for v in part)

    def send(part, pairs):
        flat = jnp.concatenate([part[0].reshape(NX * N_STATE, CHP), part[1].reshape(NX, CHP)])
        flat = lax.ppermute(flat.astype(BF16), CTX, pairs).astype(F32)
        return (flat[: NX * N_STATE].reshape(NX, N_STATE, CHP), flat[NX * N_STATE :].reshape(NX, 1, CHP))

    part = (state, steps)
    core = index % 2
    y = (index // 2) % 4
    if reverse:
        core, y = 1 - core, 3 - y
    other = send(part, SWAP)
    inside = keep(core == 1, other)
    chip = tuple(jnp.where(core == 1, a, b) for a, b in zip(after(other, part), after(part, other)))
    *chip, beside = tie(*chip, beside)
    rows = []
    for k in range(1, 4):
        rows.append(send(chip, [(i, i // 8 * 8 + (i + sign * 2 * k) % 8) for i in range(NC)]))
    pre = [keep(y >= k, rows[k - 1]) for k in range(1, 4)]
    suc = [keep(y < k, rows[k - 1]) for k in range(1, 4)]
    row_pre = after(after(pre[2], pre[1]), pre[0])
    row = after(after(after(after(row_pre, chip), suc[2]), suc[1]), suc[0])
    planes = []
    for k in range(1, 4):
        by = sign * 8 * k
        planes.append(send(row, [(i, i + by) for i in range(NC) if 0 <= i + by < NC]))
    plane_pre = after(after(planes[2], planes[1]), planes[0])
    return after(after(plane_pre, row_pre), inside)[0], beside


def key_window_chip(even, odd, core):
    other = lax.ppermute(odd, CTX, SWAP)
    none = jnp.zeros((T, odd.shape[1]), BF16)
    mine = even.astype(F32) + jnp.where(
        core == 0, jnp.concatenate([none, other]), jnp.concatenate([other, none])
    ).astype(F32)
    return mine


def key_window_back(mine):
    total = mine[4 * T :]
    for k in range(1, 5):
        term = mine[(4 - k) * T : (5 - k) * T].astype(BF16)
        total = total + shift_ctx(term, -2 * k).astype(F32)
    return total


TILES = CHP // 128


def lanes(j):
    return slice(j * 128, (j + 1) * 128)


def spread(source, target):
    for t in range(T):
        target[t] = jnp.broadcast_to(source[:, t : t + 1], (N_STATE, 128))


CHUNK = 16
WIDE = CHUNK * N_STATE
SCAN_GROUPS = ((0, 1, 2, 3), (4, 5, 6))
ADJOINT_GROUPS = ((0, 1, 2), (3, 4), (5, 6))


def chunk_diagonal():
    column = lax.broadcasted_iota(jnp.int32, (T, WIDE), 1) // N_STATE
    return column == lax.broadcasted_iota(jnp.int32, (T, WIDE), 0) % CHUNK


def chunk_rows(coef):
    pick = lax.broadcasted_iota(jnp.int32, (N_STATE, WIDE), 1) % N_STATE
    pick = (pick == lax.broadcasted_iota(jnp.int32, (N_STATE, WIDE), 0)).astype(BF16)
    wide = dot(coef.astype(BF16), pick, 0, 0)
    return jnp.where(chunk_diagonal(), wide, 0.0).astype(BF16)


def lane_sums(partial):
    flat = partial.reshape(T * N_STATE, 128).astype(BF16)
    wide = dot(flat, jnp.ones((128, 128), BF16), 1, 0).reshape(T, N_STATE, 128)
    token = lax.broadcasted_iota(jnp.int32, (T, N_STATE, 128), 0)
    lane = lax.broadcasted_iota(jnp.int32, (T, N_STATE, 128), 2)
    return jnp.sum(jnp.where(token == lane, wide, 0.0), axis=0)


def token_rows(chunk):
    return pl.ds(pl.multiple_of(chunk * CHUNK, CHUNK), CHUNK)


def state_rows(token):
    return pl.ds(pl.multiple_of(token * N_STATE, N_STATE), N_STATE)


def forward_scan(step, drive, spread_b, rate2, group, states, emit):
    rates = [rate2[:, lanes(j)] for j in group]

    def one(chunk, states):
        rows = token_rows(chunk)
        steps = [step[rows, lanes(j)] for j in group]
        drives = [drive[rows, lanes(j)] for j in group]
        states = list(states)
        for r in range(CHUNK):
            b_here = spread_b[chunk * CHUNK + r]
            for k, j in enumerate(group):
                a = jnp.exp2(steps[k][r : r + 1] * rates[k])
                states[k] = a * states[k] + drives[k][r : r + 1] * b_here
                emit(chunk * CHUNK + r, j, states[k])
        return tuple(states)

    return lax.fori_loop(0, T // CHUNK, one, tuple(states))


def chunks():
    return [(slice(c * CHUNK, (c + 1) * CHUNK), slice(c * WIDE, (c + 1) * WIDE)) for c in range(T // CHUNK)]


def scan_end_kernel(step, act, b_t, rate2, out, total, spread_b, drive):
    spread(b_t, spread_b)
    drive[...] = step[...] * act[...].astype(F32)
    for group in SCAN_GROUPS:
        zero = [jnp.zeros((N_STATE, 128), F32) for _ in group]
        states = forward_scan(step, drive, spread_b, rate2, group, zero, lambda t, j, h: None)
        for k, j in enumerate(group):
            out[0, :, lanes(j)] = states[k]
    total[0] = jnp.sum(step[...], axis=0, keepdims=True)


def scan_kernel(
    step, act, gate_z, b_t, c_t, start, rate2, skip, states_out, scan_out, gated, spread_b, drive, sum_c
):
    spread(b_t, spread_b)
    drive[...] = step[...] * act[...].astype(F32)
    sum_c[...] = chunk_rows(c_t[...])

    def emit(t, j, h):
        states_out[0, state_rows(t), lanes(j)] = h.astype(BF16)

    for group in SCAN_GROUPS:
        forward_scan(step, drive, spread_b, rate2, group, [start[0, :, lanes(j)] for j in group], emit)
    for rows, wide in chunks():
        y = dot(sum_c[rows, :], states_out[0, wide, :], 1, 0) + skip[...] * act[rows, :].astype(F32)
        scan_out[rows, :] = y
        z = gate_z[rows, :]
        gated[rows, :] = (y * (z * jax.nn.sigmoid(z))).astype(BF16)


def adjoint_end_kernel(step, g_scan, c_t, rate2, out, spread_c):
    spread(c_t, spread_c)
    for group in SCAN_GROUPS:
        rates = [rate2[:, lanes(j)] for j in group]

        def one(lap, adjoints):
            chunk = T // CHUNK - 1 - lap
            rows = token_rows(chunk)
            steps = [step[rows, lanes(j)] for j in group]
            grads = [g_scan[rows, lanes(j)] for j in group]
            adjoints = list(adjoints)
            for r in reversed(range(CHUNK)):
                c_here = spread_c[chunk * CHUNK + r]
                for k in range(len(group)):
                    a = jnp.exp2(steps[k][r : r + 1] * rates[k])
                    adjoints[k] = a * (grads[k][r : r + 1] * c_here + adjoints[k])
            return tuple(adjoints)

        zero = tuple(jnp.zeros((N_STATE, 128), F32) for _ in group)
        adjoints = lax.fori_loop(0, T // CHUNK, one, zero)
        for k, j in enumerate(group):
            out[0, :, lanes(j)] = adjoints[k]


def adjoint_kernel(
    step, act, g_scan, b_t, c_t, states, start, later, rate2, skip,
    g_step, g_act, g_rate, g_b, g_c, spread_c, drive, sum_b, adjoint, flow_rate, part_b, part_c,
):
    spread(c_t, spread_c)
    drive[...] = step[...] * act[...].astype(F32)
    sum_b[...] = chunk_rows(b_t[...])
    ones = chunk_diagonal()[:CHUNK].astype(BF16)
    for group in ADJOINT_GROUPS:
        rates = [rate2[:, lanes(j)] for j in group]

        def one(lap, carry):
            chunk = T // CHUNK - 1 - lap
            rows = token_rows(chunk)
            steps = [step[rows, lanes(j)] for j in group]
            grads = [g_scan[rows, lanes(j)] for j in group]
            drives = [drive[rows, lanes(j)] for j in group]
            adjoints, totals = list(carry[0]), list(carry[1])
            last = chunk * CHUNK + CHUNK - 1
            held = [states[0, state_rows(last), lanes(j)].astype(F32) for j in group]
            for r in reversed(range(CHUNK)):
                t = chunk * CHUNK + r
                here = state_rows(t)
                c_here = spread_c[t]
                b_sum = c_sum = None
                for k, j in enumerate(group):
                    g_row = grads[k][r : r + 1]
                    lam = g_row * c_here + adjoints[k]
                    adjoint[here, lanes(j)] = lam.astype(BF16)
                    step_row = steps[k][r : r + 1]
                    m = jnp.exp2(step_row * rates[k]) * lam
                    b_term = lam * drives[k][r : r + 1]
                    c_term = held[k] * g_row
                    b_sum = b_term if b_sum is None else b_sum + b_term
                    c_sum = c_term if c_sum is None else c_sum + c_term
                    before = states[0, state_rows(jnp.maximum(t - 1, 0)), lanes(j)].astype(F32)
                    if r == 0:
                        before = jnp.where(chunk == 0, start[0, :, lanes(j)], before)
                    flow = m * before
                    totals[k] = totals[k] + flow * step_row
                    flow_rate[here, lanes(j)] = (flow * rates[k]).astype(BF16)
                    adjoints[k] = m
                    held[k] = before
                if group[0] == 0:
                    part_b[t] = b_sum
                    part_c[t] = c_sum
                else:
                    part_b[t] += b_sum
                    part_c[t] += c_sum
            return (tuple(adjoints), tuple(totals))

        zero = tuple(jnp.zeros((N_STATE, 128), F32) for _ in group)
        first = tuple(later[0, :, lanes(j)] for j in group)
        _, totals = lax.fori_loop(0, T // CHUNK, one, (first, zero))
        for k, j in enumerate(group):
            g_rate[0, :, lanes(j)] = totals[k]
    for rows, wide in chunks():
        lam_b = dot(sum_b[rows, :], adjoint[wide, :], 1, 0)
        flow_sum = dot(ones, flow_rate[wide, :], 1, 0)
        g_step[rows, :] = flow_sum * LN2 + act[rows, :].astype(F32) * lam_b
        g_act[rows, :] = step[rows, :] * lam_b + skip[...] * g_scan[rows, :]
    g_b[...] = lane_sums(part_b[...])
    g_c[...] = lane_sums(part_c[...])


def seq_call(kernel, ins, outs, scratch, cost):
    def spec(shape, kind):
        if kind == "rows":
            return pl.BlockSpec((shape[0] // NX,) + tuple(shape[1:]), lambda s: (s, 0))
        if kind == "lanes":
            return pl.BlockSpec((shape[0], shape[1] // NX), lambda s: (0, s))
        if kind == "lead":
            return pl.BlockSpec((1,) + tuple(shape[1:]), lambda s: (s, 0, 0))
        return pl.BlockSpec(tuple(shape), lambda s: (0,) * len(shape))

    return pl.pallas_call(
        kernel,
        grid=(NX,),
        in_specs=[spec(a.shape, kind) for a, kind in ins],
        out_specs=[spec(shape, kind) for shape, _, kind in outs],
        out_shape=[jax.ShapeDtypeStruct(shape, dtype) for shape, dtype, _ in outs],
        scratch_shapes=scratch,
        compiler_params=pltpu.CompilerParams(vmem_limit_bytes=VMEM_LIMIT),
        cost_estimate=cost,
    )(*[a for a, _ in ins])


def cost(us):
    return pl.CostEstimate(flops=int(us * 1e9), bytes_accessed=int(us * 1e6), transcendentals=0)


def visible_keys(lowest):
    t = lax.broadcasted_iota(jnp.int32, (T, KEYS), 0)
    s = lax.broadcasted_iota(jnp.int32, (T, KEYS), 1)
    return (s > t) & (s <= t + WINDOW) & (s >= lowest)


def head_lanes(h, base=0):
    return slice(base + h * HEAD_DIM, base + (h + 1) * HEAD_DIM)


def stage(core, projected, mine, other, q_s, k_s, v_s):
    for block in range(9):
        rows = slice(block * T, (block + 1) * T)
        half = block // 2
        source = mine if block % 2 == 0 else other
        start = half * T if block % 2 == 0 else pl.multiple_of((half + core) * T, T)
        for n in range(KV_HEADS):
            k_s[n, rows, :] = source[pl.ds(start, T), head_lanes(n)]
            v_s[n, rows, :] = source[pl.ds(start, T), head_lanes(n, KV_HEADS * HEAD_DIM)]
    for n in range(KV_HEADS):
        for g in range(GROUP):
            q = projected[:, head_lanes(n * GROUP + g)].astype(F32) * HEAD_DIM ** (-0.5)
            q_s[n, g * T : (g + 1) * T, :] = q.astype(BF16)


def attend_kernel(place, projected, mine, other, out, lse, q_s, k_s, v_s, o_s):
    seen = visible_keys(place[0])
    stage(place[1], projected, mine, other, q_s, k_s, v_s)

    @pl.loop(0, KV_HEADS)
    def _(n):
        for g in range(GROUP):
            rows = slice(g * T, (g + 1) * T)
            scores = jnp.where(seen, dot(q_s[n, rows, :], k_s[n], 1, 1), NEG_BIG)
            peak = jnp.max(scores, axis=-1, keepdims=True)
            raised = jnp.exp(scores - peak)
            mass = jnp.sum(raised, axis=-1, keepdims=True)
            probs = (raised / mass).astype(BF16)
            o_s[n, rows, :] = dot(probs, v_s[n], 1, 0, BF16)
            lse[n, rows, :] = peak + jnp.log(mass)

    for n in range(KV_HEADS):
        for g in range(GROUP):
            out[:, head_lanes(n * GROUP + g)] = o_s[n, g * T : (g + 1) * T, :]


def attend_back_kernel(place, projected, mine, other, g_out, lse, g_q, g_even, g_odd, q_s, k_s, v_s, g_s, gq_s, gk_s, gv_s):
    seen = visible_keys(place[0])
    stage(place[1], projected, mine, other, q_s, k_s, v_s)
    for n in range(KV_HEADS):
        for g in range(GROUP):
            g_s[n, g * T : (g + 1) * T, :] = g_out[:, head_lanes(n * GROUP + g)]

    @pl.loop(0, KV_HEADS)
    def _(n):
        for g in range(GROUP):
            rows = slice(g * T, (g + 1) * T)
            q_here = q_s[n, rows, :]
            g_here = g_s[n, rows, :]
            scores = jnp.where(seen, dot(q_here, k_s[n], 1, 1), NEG_BIG)
            probs = jnp.exp(scores - lse[n, rows, :])
            g_probs = dot(g_here, v_s[n], 1, 1)
            inner = jnp.sum(probs * g_probs, axis=-1, keepdims=True)
            g_scores = (probs * (g_probs - inner)).astype(BF16)
            gq_s[n, rows, :] = (dot(g_scores, k_s[n], 1, 0) * HEAD_DIM ** (-0.5)).astype(BF16)
            k_term = dot(g_scores, q_here, 0, 0)
            v_term = dot(probs.astype(BF16), g_here, 0, 0)
            if g == 0:
                gk_s[n] = k_term
                gv_s[n] = v_term
            else:
                gk_s[n] += k_term
                gv_s[n] += v_term

    for n in range(KV_HEADS):
        for block in range(9):
            rows = slice(block * T, (block + 1) * T)
            out = g_even if block % 2 == 0 else g_odd
            into = slice(block // 2 * T, (block // 2 + 1) * T)
            out[into, head_lanes(n)] = gk_s[n, rows, :].astype(BF16)
            out[into, head_lanes(n, KV_HEADS * HEAD_DIM)] = gv_s[n, rows, :].astype(BF16)
        for g in range(GROUP):
            g_q[:, head_lanes(n * GROUP + g)] = gq_s[n, g * T : (g + 1) * T, :]


def head_call(kernel, lowest, ins, outs, scratch, us):
    def spec(shape):
        return pl.BlockSpec(tuple(shape), lambda: (0,) * len(shape))

    return pl.pallas_call(
        kernel,
        in_specs=[pl.BlockSpec(memory_space=pltpu.SMEM)] + [spec(a.shape) for a in ins],
        out_specs=[spec(shape) for shape, _ in outs],
        out_shape=[jax.ShapeDtypeStruct(shape, dtype) for shape, dtype in outs],
        scratch_shapes=[pltpu.VMEM(shape, dtype) for shape, dtype in scratch],
        compiler_params=pltpu.CompilerParams(vmem_limit_bytes=VMEM_LIMIT),
        cost_estimate=cost(us),
    )(lowest, *ins)


Q_SHAPE = (KV_HEADS, GROUP * T, HEAD_DIM)
K_SHAPE = (KV_HEADS, KEYS, HEAD_DIM)


def pad_to(v, rows, columns):
    return jnp.pad(v, ((0, rows - v.shape[0]), (0, columns - v.shape[1])))


def products_kernel(count, rows_out, *refs):
    out = refs[2 * count]
    at = 0
    for k in range(count):
        turned = refs[2 * k][...].T
        other = refs[2 * k + 1]
        width = other.shape[1]
        for first in range(0, width, 512):
            size = min(512, width - first)
            product = dot(turned, other[:, first : first + size], 1, 0)
            if rows_out == ROWS_P:
                out[:, at + first : at + first + size] = product.astype(BF16)
                continue
            for d in range(NC // 2):
                rows = product[d * ROWS_P : (d + 1) * ROWS_P]
                rows = jnp.concatenate([rows, jnp.zeros((rows_out - ROWS_P, size), F32)])
                out[d * rows_out : (d + 1) * rows_out, at + first : at + first + size] = rows.astype(BF16)
        at += width


def products(pairs, us, rows_out=ROWS_64):
    width = sum(b.shape[1] for _, b in pairs)
    specs = []
    for a, b in pairs:
        specs.append(pl.BlockSpec((a.shape[0], DP // 2), lambda i: (0, i)))
        specs.append(pl.BlockSpec(b.shape, lambda i: (0, 0)))
    return pl.pallas_call(
        functools.partial(products_kernel, len(pairs), rows_out),
        grid=(2,),
        in_specs=specs,
        out_specs=pl.BlockSpec((NC // 2 * rows_out, width), lambda i: (i, 0)),
        out_shape=jax.ShapeDtypeStruct((NC * rows_out, width), BF16),
        compiler_params=pltpu.CompilerParams(vmem_limit_bytes=VMEM_LIMIT),
        cost_estimate=cost(us),
    )(*[v for pair in pairs for v in pair])


def half_products_kernel(places, parity, *refs):
    *ins, out, turned, rows = refs
    count = len(places)
    at = 0
    for k, (held, offset) in enumerate(places):
        a, b = ins[2 * k], ins[2 * k + 1]
        depth, width = b.shape
        turned[:, :depth] = a[...].astype(F32).T
        for pair in range(NC // 4):
            first = pl.multiple_of((2 * pair + parity[0]) * ROWS_P, 8)
            block = jnp.concatenate(
                [turned[pl.ds(first, ROWS_P), :depth], jnp.zeros((ROWS_64 - ROWS_P, depth), F32)]
            )
            rows[pair * ROWS_64 : (pair + 1) * ROWS_64, :depth] = block.astype(BF16)
        for first in range(0, width, 512):
            size = min(512, width - first)
            product = dot(rows[:, :depth], b[:, first : first + size], 1, 0)
            if held is not None:
                other = ins[2 * count + held]
                product = product + other[:, offset + first : offset + first + size].astype(F32)
            out[:, at + first : at + first + size] = product.astype(BF16)
        at += width


def half_products(pairs, parity, us, held=(), places=None):
    if places is None:
        places = ((None, 0),) * len(pairs)
    width = sum(b.shape[1] for _, b in pairs)
    block = NC // 4 * ROWS_64
    specs = [pl.BlockSpec(memory_space=pltpu.SMEM)]
    for a, b in pairs:
        specs.append(pl.BlockSpec((a.shape[0], DP // 2), lambda i: (0, i)))
        specs.append(pl.BlockSpec(b.shape, lambda i: (0, 0)))
    for v in held:
        specs.append(pl.BlockSpec((block, v.shape[1]), lambda i: (i, 0)))
    return pl.pallas_call(
        functools.partial(half_products_kernel, places),
        grid=(2,),
        in_specs=specs,
        out_specs=pl.BlockSpec((block, width), lambda i: (i, 0)),
        out_shape=jax.ShapeDtypeStruct((2 * block, width), BF16),
        scratch_shapes=[pltpu.VMEM((DP // 2, NX * T), F32), pltpu.VMEM((block, NX * T), BF16)],
        compiler_params=pltpu.CompilerParams(vmem_limit_bytes=VMEM_LIMIT),
        cost_estimate=cost(us),
    )(parity.astype(jnp.int32).reshape(1), *[v for pair in pairs for v in pair], *held)


def rows_sum(v):
    return lax.psum_scatter(v, CTX, scatter_dimension=0, tiled=True)


def ring_far(v, dim, place, plus, minus):
    parts = [lax.dynamic_index_in_dim(v, (place + k) % 4, dim, False) for k in range(4)]
    half = -(-v.shape[-1] // 256) * 128
    from_left = lax.ppermute(parts[2][..., :half], CTX, plus)
    from_right = lax.ppermute(parts[2][..., half:], CTX, minus)
    to_right = jnp.concatenate(
        [(parts[1][..., :half].astype(F32) + from_left.astype(F32)).astype(BF16), parts[1][..., half:]], axis=-1
    )
    to_left = jnp.concatenate(
        [parts[3][..., :half], (parts[3][..., half:].astype(F32) + from_right.astype(F32)).astype(BF16)], axis=-1
    )
    return parts[0], to_right, to_left


def ring_near(own, to_right, to_left, plus, minus):
    a = lax.ppermute(to_right, CTX, plus)
    b = lax.ppermute(to_left, CTX, minus)
    return own.astype(F32) + a.astype(F32) + b.astype(F32)


def ring_pairs(stride, by):
    return [(i, i + (((i // stride) % 4 + by) % 4 - (i // stride) % 4) * stride) for i in range(NC)]


def core_halves(terms, core):
    def half(which):
        return jnp.concatenate(
            [
                lax.dynamic_index_in_dim(v.reshape(NC // 2, 2, ROWS_P, v.shape[1]), which, 1, False)
                for v in terms
            ],
            axis=-1,
        )

    return half(1 - core), half(core)


def core_sum(theirs, mine):
    other = lax.ppermute(theirs, CTX, SWAP)
    v = mine.astype(F32) + other.astype(F32)
    return v.reshape(4, 4, ROWS_P, v.shape[-1])


def body(
    tokens,
    norm_gain,
    qkv_weight,
    attn_out_weight,
    in_weight,
    conv_weight,
    conv_bias,
    xproj_weight,
    dt_weight,
    dt_bias,
    decay_log,
    skip_gain,
    mamba_out_weight,
    attn_gain,
    mamba_gain,
    ffn_gain,
    gate_up_weight,
    down_weight,
    cotangent,
):
    x = lax.axis_index("seq")
    index = lax.axis_index(CTX)

    def columns(v, first, count):
        return lax.dynamic_slice_in_dim(v, first, count, v.ndim - 1)

    def order(count, size, rows):
        place = lax.broadcasted_iota(jnp.int32, (size, DP), 1)
        source = place // ROWS_P * rows + place % ROWS_P
        hit = (source == lax.broadcasted_iota(jnp.int32, (size, DP), 0)) & (place % ROWS_P < rows)
        return lax.optimization_barrier((hit & (source < count)).astype(BF16))

    widen_m = order(D, D, ROWS)
    widen_channels = order(CH, CHP, CSUB)
    widen_hidden = order(FFX, FFP, FSUB)

    def widen(v, matrix=None):
        return dot(v, widen_m if matrix is None else matrix, 1, 0, BF16)

    narrow_m = lax.optimization_barrier(jnp.pad(widen_m.T, ((0, 0), (0, AO_P - D))))

    def narrow(v, matrix=None):
        if matrix is None:
            return dot(v.astype(BF16), narrow_m, 1, 0)[:, :D]
        return dot(v.astype(BF16), matrix, 1, 1)

    by_channel = pad_to(jnp.concatenate([xproj_weight, dt_weight], axis=1), 2 * ROWS, XD)
    first = jnp.concatenate(
        [
            pad_to(columns(in_weight, x * CH, CH), ROWS_P, CHP),
            pad_to(columns(in_weight, DI + x * CH, CH), ROWS_P, CHP),
            pad_to(by_channel[:ROWS], ROWS_P, XD),
            pad_to(by_channel[ROWS:], ROWS_P, XD),
            pad_to(qkv_weight, ROWS_P, QKV_P),
        ],
        axis=1,
    )
    first = lax.all_gather(first, CTX, axis=0, tiled=True)
    sub_mamba = lax.dynamic_slice_in_dim(mamba_out_weight, x * CSUB, CSUB, 0)
    sub_down = lax.dynamic_slice_in_dim(down_weight, x * FSUB, FSUB, 0)
    sub_wide = lax.ppermute(
        jnp.concatenate([pad_to(sub_down, 48, D), pad_to(sub_mamba, 32, D)]), SEQ_CTX, TURN
    )
    second = jnp.concatenate(
        [
            pad_to(attn_out_weight, ROWS_P, AO_P),
            pad_to(sub_wide[48 : 48 + CSUB], ROWS_P, AO_P),
        ],
        axis=1,
    )
    third = jnp.concatenate(
        [
            pad_to(columns(gate_up_weight, x * FFX, FFX), ROWS_P, FFP),
            pad_to(columns(gate_up_weight, FF + x * FFX, FFX), ROWS_P, FFP),
            pad_to(sub_wide[:FSUB], ROWS_P, AO_P),
        ],
        axis=1,
    )
    inputs = tokens.astype(F32)
    normed_f, norm1_pullback = jax.vjp(norm_scale, inputs, norm_gain)
    normed = widen(normed_f.astype(BF16))
    normed, second = tie(normed, second)
    second = lax.all_gather(second, CTX, axis=0, tiled=True)
    normed_all = jnp.concatenate(gather_x(normed))
    def channel(v):
        part = columns(v, x * CH, CH)
        return jnp.pad(part, ((0, 0),) * (v.ndim - 1) + ((0, CHP - CH),))

    taps = channel(conv_weight)
    conv_b = channel(conv_bias)[None]
    dt_b = channel(dt_bias)[None]
    skip = channel(skip_gain)[None]
    decay_rate = -jnp.exp(channel(decay_log.T))
    rate2 = decay_rate * LOG2E

    cot_all = jnp.concatenate(gather_x(pad_to(cotangent, T, AO_P)))
    first, normed_all, cot_all, third, widen_m, narrow_m, widen_channels, widen_hidden, taps, conv_b, dt_b, skip, rate2 = tie(
        first, normed_all, cot_all, third, widen_m, narrow_m, widen_channels, widen_hidden, taps, conv_b, dt_b, skip, rate2
    )
    third = lax.all_gather(third, CTX, axis=0, tiled=True)
    w_in = first[:, : 2 * CHP]
    w_qkv = first[:, 2 * CHP + 2 * XD :]
    w_attn = second[:, :AO_P]
    w_mamba = second[:, AO_P:]
    w_gate_up = third[:, : 2 * FFP]
    w_down = third[:, 2 * FFP :]

    in_proj = dot(normed_all, w_in, 1, 0)
    in_proj, normed_q, first = tie(in_proj, normed, first)
    small = first[:, 2 * CHP : 2 * CHP + 2 * XD]
    small = small.reshape(NC, ROWS_P, 2 * XD)
    small = lax.dynamic_slice_in_dim(small, x * (NC // NX), NC // NX, 0)[:, :ROWS]
    small = jnp.stack([small[:, :, :XD], small[:, :, XD:]], axis=1).reshape(CH, XD)
    w_small = pad_to(small, CHP, XD)
    w_xproj = w_small[:, : DT_RANK + 2 * N_STATE]
    w_dt = w_small[:, DT_RANK + 2 * N_STATE : 2 * DT_RANK + 2 * N_STATE]
    conv_in = in_proj[:, :CHP].reshape(NX, T, CHP)
    gate_z = in_proj[:, CHP:]
    tails = shift_ctx(conv_in[:, T - (CONV - 1) :].reshape(NX * (CONV - 1), CHP), 1)
    padded = jnp.concatenate([tails.reshape(NX, CONV - 1, CHP), conv_in], axis=1)
    conv_sum = conv_b[None]
    for j in range(CONV):
        conv_sum = conv_sum + taps[j] * padded[:, j : j + T]
    conv_sum = conv_sum.reshape(NX * T, CHP)
    act_f, conv_pullback = jax.vjp(jax.nn.silu, conv_sum)
    act = act_f.astype(BF16)
    xproj_t = dot(w_xproj, act, 0, 1, BF16)
    projected = dot(normed_q, w_qkv, 1, 0, BF16)
    xproj_t, projected = tie(xproj_t, projected)
    xproj_t = total_x(xproj_t)
    kv_own = projected[:, D:QKV]
    core = index % 2
    kv_mine = jnp.concatenate([shift_ctx(kv_own, 2 * k) for k in (4, 3, 2, 1)] + [kv_own])
    dt_low_t = xproj_t[:DT_RANK].astype(BF16)
    b_t = xproj_t[DT_RANK : DT_RANK + N_STATE]
    c_t = xproj_t[DT_RANK + N_STATE :]
    pre = dot(dt_low_t, w_dt, 0, 1) + dt_b
    step = jax.nn.softplus(pre)
    scan_end, steps = seq_call(
        scan_end_kernel,
        [(step, "rows"), (act, "rows"), (b_t, "lanes"), (rate2, "all")],
        [((NX, N_STATE, CHP), F32, "lead"), ((NX, 1, CHP), F32, "lead")],
        [pltpu.VMEM((T, N_STATE, 128), F32), pltpu.VMEM((T, CHP), F32)],
        cost(8),
    )

    scan_end, kv_mine = tie(scan_end, kv_mine)
    kv_other = lax.ppermute(kv_mine, CTX, SWAP)
    start, kv_other = carried(scan_end, steps, rate2, index, False, kv_other)
    place_here = jnp.stack([jnp.maximum(0, WINDOW - index * T), core]).astype(jnp.int32)
    attended, lse = head_call(
        attend_kernel,
        place_here,
        [projected, kv_mine, kv_other],
        [((T, D), BF16), ((KV_HEADS, GROUP * T, 1), F32)],
        [(Q_SHAPE, BF16), (K_SHAPE, BF16), (K_SHAPE, BF16), (Q_SHAPE, BF16)],
        15,
    )
    start, attended, lse = tie(start, attended, lse)
    attended = widen(attended)
    attn_branch = dot(attended, w_attn, 1, 0)[:, :D]

    states, scan_out, gated = seq_call(
        scan_kernel,
        [
            (step, "rows"),
            (act, "rows"),
            (gate_z, "rows"),
            (b_t, "lanes"),
            (c_t, "lanes"),
            (start, "lead"),
            (rate2, "all"),
            (skip, "all"),
        ],
        [
            ((NX, T * N_STATE, CHP), BF16, "lead"),
            ((NX * T, CHP), F32, "rows"),
            ((NX * T, CHP), BF16, "rows"),
        ],
        [
            pltpu.VMEM((T, N_STATE, 128), F32),
            pltpu.VMEM((T, CHP), F32),
            pltpu.VMEM((T, WIDE), BF16),
        ],
        cost(14),
    )
    gated = widen(gated, widen_channels)
    mamba_terms = dot(gated, w_mamba, 1, 0, BF16)

    mamba_branch = scatter_x([mamba_terms[k * T : (k + 1) * T] for k in range(NX)])[:, :D]

    def mixing(attn_part, mamba_part, gain_attn, gain_mamba):
        return 0.5 * (norm_scale(attn_part, gain_attn) + norm_scale(mamba_part, gain_mamba))

    mamba_branch, cot_all = tie(mamba_branch, cot_all)
    mixed, mix_pullback = jax.vjp(mixing, attn_branch, mamba_branch, attn_gain, mamba_gain)
    residual = inputs + mixed
    ffn_f, norm2_pullback = jax.vjp(norm_scale, residual, ffn_gain)
    ffn_near = gather_x_near(widen(ffn_f.astype(BF16)))
    g_hidden = dot(cot_all, w_down, 1, 1, BF16)
    g_hidden, *ffn_near = tie(g_hidden, *ffn_near)
    g_hidden = narrow(g_hidden, widen_hidden)
    ffn_all, g_hidden = tie(jnp.concatenate(gather_x_far(*ffn_near)), g_hidden)
    gate_up = dot(ffn_all, w_gate_up, 1, 0)

    def swiglu(gate, up):
        return jax.nn.silu(gate) * up

    hidden_f, swiglu_pullback = jax.vjp(swiglu, gate_up[:, :FFP], gate_up[:, FFP:])
    hidden_f = hidden_f.astype(BF16)
    g_gate, g_up = swiglu_pullback(g_hidden)
    g_gate_up = jnp.concatenate([g_gate.astype(BF16), g_up.astype(BF16)], axis=1)
    g_ffn_terms = dot(g_gate_up, w_gate_up, 1, 1, BF16)
    g_ffn_terms, hidden_f, g_gate_up, ffn_all = tie(g_ffn_terms, hidden_f, g_gate_up, ffn_all)
    hidden = widen(hidden_f, widen_hidden)
    ffn_term = products([(ffn_all, g_gate_up), (hidden, cot_all)], 14)
    g_ffn_sum = scatter_x([g_ffn_terms[k * T : (k + 1) * T] for k in range(NX)])
    g_ffn_sum, ffn_term, hidden = tie(g_ffn_sum, ffn_term, hidden)
    ffn_sum = rows_sum(ffn_term)
    (g_ffn_in,) = tie(narrow(g_ffn_sum))
    g_norm2, g_ffn_gain = norm2_pullback(g_ffn_in)
    g_residual = cotangent.astype(F32) + g_norm2
    g_attn_f, g_mamba_f, g_attn_gain, g_mamba_gain = mix_pullback(g_residual)
    g_attn = pad_to(g_attn_f.astype(BF16), T, AO_P)
    g_mamba_near = gather_x_near(pad_to(g_mamba_f.astype(BF16), T, AO_P))

    (g_attended,) = tie(dot(g_attn, w_attn, 1, 1, BF16))
    g_attended = narrow(g_attended).astype(BF16)
    g_attended, *g_mamba_near = tie(g_attended, *g_mamba_near)
    g_mamba_all = jnp.concatenate(gather_x_far(*g_mamba_near))
    (g_gated,) = tie(dot(g_mamba_all, w_mamba, 1, 1, BF16))
    (g_gated,) = tie(narrow(g_gated, widen_channels))
    silu_z, gate_pullback = jax.vjp(jax.nn.silu, gate_z)
    g_scan = g_gated * silu_z
    (g_gate_z,) = gate_pullback(g_gated * scan_out)
    g_skip = jnp.sum(g_scan * act.astype(F32), axis=0)
    (adjoint_end,) = seq_call(
        adjoint_end_kernel,
        [(step, "rows"), (g_scan, "rows"), (c_t, "lanes"), (rate2, "all")],
        [((NX, N_STATE, CHP), F32, "lead")],
        [pltpu.VMEM((T, N_STATE, 128), F32)],
        cost(8),
    )
    later, g_attended = carried(adjoint_end, steps, rate2, index, True, g_attended)

    g_queries, g_even, g_odd = head_call(
        attend_back_kernel,
        place_here,
        [projected, kv_mine, kv_other, g_attended, lse],
        [
            ((T, D), BF16),
            ((5 * T, 2 * KV_HEADS * HEAD_DIM), BF16),
            ((4 * T, 2 * KV_HEADS * HEAD_DIM), BF16),
        ],
        [
            (Q_SHAPE, BF16),
            (K_SHAPE, BF16),
            (K_SHAPE, BF16),
            (Q_SHAPE, BF16),
            (Q_SHAPE, BF16),
            (K_SHAPE, F32),
            (K_SHAPE, F32),
        ],
        22,
    )
    kv_chip = key_window_chip(g_even, g_odd, core)
    branch_pairs = [
        (attended, g_attn),
        (gated, g_mamba_all),
        (normed_all, g_gate_z.astype(BF16)),
    ]
    theirs_1 = half_products(branch_pairs, 1 - core, 8)
    later, theirs_1, kv_chip = tie(later, theirs_1, kv_chip)
    other_1 = lax.ppermute(theirs_1, CTX, SWAP)
    g_kv_own = key_window_back(kv_chip)
    g_step, g_act, g_rate, g_b, g_c = seq_call(
        adjoint_kernel,
        [
            (step, "rows"),
            (act, "rows"),
            (g_scan, "rows"),
            (b_t, "lanes"),
            (c_t, "lanes"),
            (states, "lead"),
            (start, "lead"),
            (later, "lead"),
            (rate2, "all"),
            (skip, "all"),
        ],
        [
            ((NX * T, CHP), F32, "rows"),
            ((NX * T, CHP), F32, "rows"),
            ((NX, N_STATE, CHP), F32, "lead"),
            ((N_STATE, NX * T), F32, "lanes"),
            ((N_STATE, NX * T), F32, "lanes"),
        ],
        [
            pltpu.VMEM((T, N_STATE, 128), F32),
            pltpu.VMEM((T, CHP), F32),
            pltpu.VMEM((T, WIDE), BF16),
            pltpu.VMEM((T * N_STATE, CHP), BF16),
            pltpu.VMEM((T * N_STATE, CHP), BF16),
            pltpu.VMEM((T, N_STATE, 128), F32),
            pltpu.VMEM((T, N_STATE, 128), F32),
        ],
        cost(25),
    )
    g_step, other_1, g_kv_own, ffn_sum = tie(g_step, other_1, g_kv_own, ffn_sum)
    gate_up_near = gather_x_near(ffn_sum[:ROWS_P, : 2 * FFP])
    g_projected = pad_to(jnp.concatenate([g_queries, g_kv_own.astype(BF16)], axis=1), T, QKV_P)
    branch_pairs.append((normed, g_projected))
    other_2 = lax.ppermute(half_products(branch_pairs[3:], 1 - core, 3), CTX, SWAP)
    branch_pairs = [branch_pairs[0], branch_pairs[3], branch_pairs[1], branch_pairs[2]]
    branch_term = half_products(
        branch_pairs, core, 12, [other_1, other_2], ((0, 0), (1, 0), (0, AO_P), (0, 2 * AO_P))
    )
    g_decay = jnp.sum(g_rate, axis=0) * decay_rate
    g_pre_f = g_step * jax.nn.sigmoid(pre)
    g_dt_bias = jnp.sum(g_pre_f, axis=0)
    g_pre = g_pre_f.astype(BF16)
    dt_term = dot(g_pre, dt_low_t, 0, 1, BF16)
    g_xproj_t = jnp.concatenate([dot(w_dt, g_pre, 0, 1), g_b, g_c]).astype(BF16)
    g_xproj_t = total_x(g_xproj_t).astype(BF16)
    g_xproj_t, branch_term, *gate_up_near = tie(g_xproj_t, branch_term, *gate_up_near)
    branch_sum = lax.psum_scatter(branch_term, "zy", scatter_dimension=0, tiled=True)
    xproj_term = dot(act, g_xproj_t, 0, 1, BF16)
    g_act = g_act + dot(g_xproj_t, w_xproj, 0, 1)
    (g_conv_sum,) = conv_pullback(g_act)
    g_conv_bias = jnp.sum(g_conv_sum, axis=0)
    g_conv_3 = g_conv_sum.reshape(NX, T, CHP)
    g_taps = [jnp.sum(g_conv_3 * padded[:, j : j + T], axis=(0, 1)) for j in range(CONV)]
    g_padded = jnp.zeros((NX, T + CONV - 1, CHP), F32)
    for j in range(CONV):
        g_padded = g_padded + jnp.pad(taps[j] * g_conv_3, ((0, 0), (j, CONV - 1 - j), (0, 0)))
    back = shift_ctx(g_padded[:, : CONV - 1].reshape(NX * (CONV - 1), CHP).astype(BF16), -1)
    back = back.astype(F32).reshape(NX, CONV - 1, CHP)
    g_conv_in = g_padded[:, CONV - 1 :] + jnp.pad(back, ((0, 0), (T - (CONV - 1), 0), (0, 0)))
    g_in_proj = jnp.concatenate(
        [g_conv_in.reshape(NX * T, CHP).astype(BF16), g_gate_z.astype(BF16)], axis=1
    )
    small_term = pad_to(jnp.concatenate([xproj_term[:CH], dt_term[:CH]], axis=1), CH, XD)
    small_term = jnp.pad(small_term.reshape(NC, CSUB, XD), ((0, 0), (0, ROWS_P - CSUB), (0, 0)))
    in_c_term = products([(normed_all, g_in_proj[:, :CHP])], 4, ROWS_P)
    theirs, mine = core_halves([in_c_term, small_term.reshape(DP, XD)], core)
    theirs, mine, hidden = tie(theirs, mine, hidden)
    down_terms = dot(hidden, w_down, 1, 0, BF16)
    in_half = core_sum(theirs, mine)
    gains = jnp.stack([jnp.zeros_like(g_attn_gain), g_attn_gain, g_mamba_gain, g_ffn_gain])
    gains = jnp.pad(gains, ((0, 0), (0, 2 * CHP - D))).reshape(8, CHP)
    table = jnp.concatenate(
        [
            jnp.stack(g_taps),
            g_conv_bias[None],
            g_dt_bias[None],
            g_skip[None],
            g_decay,
            jnp.zeros((1, CHP), F32),
            gains,
        ]
    )
    table = jnp.pad(table, ((0, 0), (0, 4 * XD - CHP))).reshape(NC // 2, 8, XD)
    table = jnp.pad(table, ((0, 0), (32, ROWS_P - 40), (CHP, 0))).reshape(4, 4, ROWS_P, CHP + XD)
    in_half = (in_half + table).astype(BF16)
    in_half, g_in_proj, g_projected, down_terms = tie(in_half, g_in_proj, g_projected, down_terms)
    g_normed_terms = dot(g_in_proj, w_in, 1, 1, BF16)
    both = jnp.concatenate([g_normed_terms, down_terms], axis=1)
    both = scatter_x_far([both[k * T : (k + 1) * T] for k in range(NX)])
    along_z = (ring_pairs(8, 1), ring_pairs(8, -1))
    along_y = (ring_pairs(2, 1), ring_pairs(2, -1))
    in_half = ring_far(in_half, 1, (index // 2) % 4, *along_y)
    both = scatter_x_near(*both)
    g_normed_attn = dot(g_projected, w_qkv, 1, 1)
    in_half, g_normed_attn, gate_up_near = tie(in_half, g_normed_attn, gate_up_near)
    gate_up = gather_x_far(*gate_up_near)
    in_half = ring_near(*in_half, *along_y).astype(BF16)
    in_half = ring_far(in_half, 0, index // 8, *along_z)
    (g_normed,) = tie(narrow(both[:, :DP] + g_normed_attn))
    g_norm1, g_norm_gain = norm1_pullback(g_normed)
    tokens_grad = g_residual + g_norm1
    output = (residual + both[:, DP : DP + D]).astype(BF16)
    in_sum = ring_near(*in_half, *along_z)
    in_sum, branch_sum = tie(in_sum, branch_sum)
    branch = total_x_pairs(branch_sum[:ROWS_P, : AO_P + QKV_P])
    g_norm_gain = jnp.pad(g_norm_gain, (0, 8 * XD - D)).reshape(8, XD)
    table = jnp.concatenate([in_sum[32:40, CHP:], g_norm_gain])
    table = jnp.broadcast_to(table[None], (NC, 16, XD))
    in_sum = in_sum.astype(BF16)
    owned = jnp.concatenate(
        [
            ffn_sum[:48, 2 * FFP : 2 * FFP + AO_P],
            branch_sum[:CSUB, AO_P + QKV_P : 2 * AO_P + QKV_P],
            pad_to(in_sum[:CSUB, CHP:].reshape(CSUB * XD // D, D), 32 - CSUB, AO_P),
        ]
    )
    owned = lax.ppermute(owned, SEQ_CTX, TURN_BACK)
    in_both = jnp.concatenate([in_sum[:, :CHP], branch_sum[:ROWS_P, 2 * AO_P + QKV_P :]], axis=1)
    in_parts = in_order(spread_x(in_both), x)
    table = lax.all_to_all(table, CTX, 0, 0, tiled=True)
    g_norm_gain = jnp.sum(table[:, 8:], axis=0).reshape(2, 4 * XD)
    table = jnp.sum(table[:, :8].reshape(NC // 2, 2, 2, 4 * XD), axis=1).reshape(NC, 4 * XD)
    table = jnp.concatenate([table, jnp.pad(g_norm_gain, ((0, 14), (0, 0)))])
    last = in_order(gather_x(owned), x)
    tables = in_order(spread_x(table.astype(BF16)), x)
    by_rows = jnp.concatenate([v[:24, :CH] for v in tables], axis=1).astype(F32)
    gains = sum(v[24:32, :CHP].astype(F32) for v in tables).reshape(4, 2 * CHP)[:, :D]
    g_norm_gain = sum(v[32:34].astype(F32) for v in tables).reshape(8 * XD)[:D]

    def side_by_side(parts, width):
        halves = []
        size = parts[0].shape[1] // 2
        for first_column in range(0, 2 * size, size):
            halves += [p[:ROWS, first_column : first_column + width] for p in parts]
        return jnp.concatenate(halves, axis=1).astype(F32)

    branch = branch.astype(F32)
    attn_w = branch[:ROWS, :D]
    qkv_w = branch[:ROWS, AO_P : AO_P + QKV]
    down_w = jnp.concatenate([v[:FSUB, :D] for v in last]).astype(F32)
    mamba_w = jnp.concatenate([v[48 : 48 + CSUB, :D] for v in last]).astype(F32)
    small_rows = jnp.concatenate([v[48 + CSUB : 52 + CSUB, :D].reshape(CSUB, XD) for v in last]).astype(F32)
    in_w = jnp.concatenate(
        [v[:ROWS, :CH] for v in in_parts] + [v[:ROWS, CHP : CHP + CH] for v in in_parts], axis=1
    ).astype(F32)
    g_xproj_w = small_rows[:, : DT_RANK + 2 * N_STATE]
    g_dt_w = small_rows[:, DT_RANK + 2 * N_STATE : 2 * DT_RANK + 2 * N_STATE]

    return (
        output,
        tokens_grad,
        g_norm_gain,
        qkv_w,
        attn_w,
        in_w,
        by_rows[:4],
        by_rows[4],
        g_xproj_w,
        g_dt_w,
        by_rows[5],
        by_rows[7:23].T,
        by_rows[6],
        mamba_w,
        gains[1],
        gains[2],
        gains[3],
        side_by_side(in_order(gate_up, x), FFX),
        down_w,
    )


def solution(mesh):
    mesh = jax.sharding.Mesh(mesh.devices.reshape(NX, NC // 2, 2), SEQ_CTX)
    whole = P()
    ctx = P(CTX, None)
    both = P(SEQ_CTX, None)
    return jax.shard_map(
        body,
        mesh=mesh,
        in_specs=(
            both, whole, ctx, ctx, ctx, whole, whole, ctx, ctx, whole, whole, whole,
            ctx, whole, whole, whole, ctx, ctx, both,
        ),
        out_specs=(
            both, both, whole, ctx, ctx, ctx, whole, whole, ctx, ctx, whole, whole,
            whole, ctx, whole, whole, whole, ctx, ctx,
        ),
        check_vma=False,
    )
```
